32 devices in a mesh: seq: 8 (over z, x), head: 4 (over y, core).
Axes of the slice: x: 2, y: 2, z: 4, core: 2. Of those that a mesh axis runs over, the one named last changes fastest.
Arguments:
- query: bfloat16 [2048, 256], P('seq', 'head'), may hold values from -5 to 5
- key: bfloat16 [2048, 256], P('seq', 'head'), may hold values from -5 to 5
- value: bfloat16 [2048, 2048], P('seq', 'head'), may hold values from -76 to 76
- window_query: bfloat16 [2048, 2048], P('seq', 'head'), may hold values from -4.5 to 4.5
- window_key: bfloat16 [2048, 2048], P('seq', 'head'), may hold values from -4.5 to 4.5
- gain: float32 [2048], P('head'), may hold values from 0.5 to 1.5
- cotangent: bfloat16 [2048, 2048], P('seq', 'head'), may hold values from -11 to 11
Outputs:
- normed: bfloat16 [2048, 2048], P('seq', 'head')
- grad_query: bfloat16 [2048, 256], P('seq', 'head')
- grad_key: bfloat16 [2048, 256], P('seq', 'head')
- grad_value: bfloat16 [2048, 2048], P('seq', 'head')
- grad_window_query: bfloat16 [2048, 2048], P('seq', 'head')
- grad_window_key: bfloat16 [2048, 2048], P('seq', 'head')
The draws below stay inside these ranges and needn't reach their ends.
All inputs are finite; a program needn't handle non-finite values.
Results may differ from the reference program's by a relative error of at most 0.0065.
Values may be sent and summed in bfloat16 or wider, within the bound.
No kernel may reach another device: no remote copies, remote signals or barrier semaphores. Data moves between devices by JAX's collectives and lax.ppermute only.
A program may use at most 128 MiB of HBM per device.

```python
import math
import jax
import jax.numpy as jnp
from jax import lax

HEADS = 16
HEAD_DIM = 128
FEAT = 16
WINDOW = 64
TOK_DEV = 256
TOKENS = 2048
MODEL = 2048
N_SEQ = 8


def block_offsets(seed_key):
    half_block = TOK_DEV // 2
    offsets = jnp.clip(jax.random.normal(seed_key, (TOKENS // half_block, MODEL), jnp.float32), -3.0, 3.0)
    return jnp.repeat(offsets, half_block, axis=0)


def draw_value(key, part):
    base_key = jax.random.fold_in(key, 101)
    noise_key, offset_key, column_key = jax.random.split(base_key, 3)
    head_index = (jnp.arange(MODEL) // HEAD_DIM).astype(jnp.float32)
    columns = jnp.exp(jax.random.uniform(column_key, (MODEL,), jnp.float32, -0.8, 0.8))
    noise = jnp.clip(jax.random.normal(noise_key, (TOKENS, MODEL), jnp.float32), -4.0, 4.0)
    level = noise + 2.0 * block_offsets(offset_key)
    rising = 5.0 ** (0.5 * head_index / (HEADS - 1))
    return (level * (rising * columns)[None, :]).astype(jnp.bfloat16)


def draw_cotangent(key, part):
    base_key = jax.random.fold_in(key, 202)
    noise_key, offset_key = jax.random.split(base_key, 2)
    noise = jnp.clip(jax.random.normal(noise_key, (TOKENS, MODEL), jnp.float32), -4.0, 4.0)
    level = noise + 2.0 * block_offsets(offset_key)
    return level.astype(jnp.bfloat16)


def window_pair(key):
    base_key = jax.random.fold_in(key, 303)
    query_seed, key_seed = jax.random.split(base_key, 2)
    shape = (TOKENS, MODEL)
    query_out = jnp.clip(jax.random.normal(query_seed, shape, jnp.float32), -4.4, 4.4)
    key_out = jnp.clip(jax.random.normal(key_seed, shape, jnp.float32), -4.4, 4.4)
    return (query_out, key_out)


def draw_window_query(key, part):
    return window_pair(key)[0].astype(jnp.bfloat16)


def draw_window_key(key, part):
    return window_pair(key)[1].astype(jnp.bfloat16)


def level_of(stream_key, extent, shards, smallest, largest):
    def one(dim, parts):
        steps = jax.random.uniform(jax.random.fold_in(jax.random.fold_in(stream_key, 6), dim), (parts,), jnp.float32, smallest / len(shards), largest / len(shards))
        return jnp.repeat(jnp.exp(steps), extent[dim] // parts).reshape((-1,) + (1,) * (len(extent) - dim - 1))

    level = one(*shards[0])
    for cut in shards[1:]:
        level = level * one(*cut)
    return level


def scatter_about(stream_key, shape, spread, bound, shards=(), kind=jnp.bfloat16):
    factor_of = level_of(stream_key, shape, shards, -0.22, 0.18) if shards else 1.0
    result = jax.random.normal(stream_key, shape, jnp.float32) * spread * factor_of
    return jnp.minimum(jnp.maximum(result, -bound), bound).astype(kind)


def setup_inputs(seed: int = 0) -> dict:
    splits = jax.random.split(jax.random.key(seed), 8)
    return {
        "query": scatter_about(splits[0], (TOKENS, HEADS * FEAT), 1.0, 5.0, ((0, 8), (1, 4))),
        "key": scatter_about(splits[1], (TOKENS, HEADS * FEAT), 1.0, 5.0, ((0, 8), (1, 4))),
        "value": draw_value(jax.random.fold_in(splits[7], 71), 0),
        "window_query": draw_window_query(jax.random.fold_in(splits[7], 71), 0),
        "window_key": draw_window_key(jax.random.fold_in(splits[7], 71), 0),
        "gain": jnp.clip(1.0 + 0.1 * jax.random.normal(splits[5], (MODEL,), jnp.float32), 0.5, 1.5),
        "cotangent": draw_cotangent(jax.random.fold_in(splits[7], 71), 0),
    }


HIGHEST = lax.Precision.HIGHEST

def narrow(tensor):
    return lax.optimization_barrier(tensor.astype(jnp.bfloat16))

def taylor(inputs, head_count, features):
    length = inputs.shape[0]
    scaled = inputs.astype(jnp.float32).reshape(length, head_count, features) * features ** (-0.25)
    square = (scaled[:, :, :, None] * scaled[:, :, None, :]).reshape(length, head_count, features * features) * math.sqrt(0.5)
    return jnp.concatenate([jnp.ones((length, head_count, 1), jnp.float32), scaled, square], axis=2)

def taylor_back(inputs, head_count, features, upstream):
    length = inputs.shape[0]
    scaled = inputs.astype(jnp.float32).reshape(length, head_count, features) * features ** (-0.25)
    linear_part = upstream[:, :, 1:1 + features]
    square = upstream[:, :, 1 + features:].reshape(length, head_count, features, features) * math.sqrt(0.5)
    summed = linear_part + lax.optimization_barrier(jnp.sum(square * scaled[:, :, None, :], axis=3)) + lax.optimization_barrier(jnp.sum(square * scaled[:, :, :, None], axis=2))
    return (summed * features ** (-0.25)).reshape(length, head_count * features)

def kernel_parts(query, key, head_count, features):
    length = query.shape[0]
    query_heads = query.astype(jnp.float32).reshape(length, head_count, features)
    key_heads = key.astype(jnp.float32).reshape(length, head_count, features)
    scores = jnp.einsum('thf,shf->hts', query_heads, key_heads) / math.sqrt(features)
    causal = lax.broadcasted_iota(jnp.int32, (1, length, length), 1) >= lax.broadcasted_iota(jnp.int32, (1, length, length), 2)
    kernel = jnp.where(causal, 1.0 + scores + 0.5 * scores * scores, 0.0)
    return (scores, kernel, narrow(kernel), causal)

def window_blocks(rows_in, window):
    groups = rows_in.shape[0] // window
    grouped = rows_in.reshape(groups, window, rows_in.shape[1], rows_in.shape[2])
    return jnp.concatenate([grouped[:-1], grouped[1:]], axis=1)

def unblock(blocked, window):
    zero_block = jnp.zeros_like(blocked[:1, :window])
    lower = jnp.concatenate([blocked[:, :window], zero_block], axis=0)
    upper = jnp.concatenate([zero_block, blocked[:, window:]], axis=0)
    joined = lower + upper
    return joined.reshape(joined.shape[0] * window, joined.shape[2] * joined.shape[3])

def window_mask(groups, window, rim_live):
    shape = (groups, 1, window, 2 * window)
    block_index = lax.broadcasted_iota(jnp.int32, shape, 0)
    row_index = lax.broadcasted_iota(jnp.int32, shape, 2)
    col_index = lax.broadcasted_iota(jnp.int32, shape, 3)
    inside = (col_index > row_index) & (col_index <= row_index + window)
    return inside & ((block_index > 0) | (col_index >= window) | rim_live)

def window_parts(window_query, window_key, value, rim_key, rim_value, rim_live, head_count, head_width, window):
    length = window_query.shape[0]
    groups = length // window
    pad_row = jnp.zeros((1, window_key.shape[1]), jnp.bfloat16)
    key_rows = jnp.concatenate([pad_row, rim_key, window_key], axis=0).reshape(length + window, head_count, head_width)
    value_rows = jnp.concatenate([pad_row, rim_value, value], axis=0).reshape(length + window, head_count, head_width)
    key_blocks = window_blocks(key_rows, window)
    value_blocks = window_blocks(value_rows, window)
    query_blocks = window_query.reshape(groups, window, head_count, head_width)
    logits = jnp.einsum('bihd,bjhd->bhij', query_blocks.astype(jnp.float32), key_blocks.astype(jnp.float32)) / math.sqrt(head_width)
    allowed = window_mask(groups, window, rim_live)
    masked = jnp.where(allowed, logits, -1e+30)
    row_max = lax.optimization_barrier(jnp.max(masked, axis=3, keepdims=True))
    exponent = jnp.where(allowed, jnp.exp(masked - row_max), 0.0)
    weights = exponent / lax.optimization_barrier(jnp.sum(exponent, axis=3, keepdims=True))
    weights_narrow = narrow(weights)
    window_out = jnp.einsum('bhij,bjhd->bihd', weights_narrow.astype(jnp.float32), value_blocks.astype(jnp.float32)).reshape(length, head_count, head_width)
    return (weights, weights_narrow, query_blocks, key_blocks, value_blocks, window_out)

def before_sum(stack):
    totals = jnp.cumsum(stack, axis=0)
    return jnp.concatenate([jnp.zeros_like(stack[:1]), totals[:-1]], axis=0)

def after_sum(stack):
    totals = jnp.cumsum(stack[::-1], axis=0)[::-1]
    return jnp.concatenate([totals[1:], jnp.zeros_like(stack[:1])], axis=0)

def reference(query, key, value, window_query, window_key, gain, cotangent):
    block_count = N_SEQ
    length = TOK_DEV
    head_count = HEADS
    features = FEAT
    head_width = HEAD_DIM
    window = WINDOW
    rim_rows = window - 1
    full_width = HEADS * HEAD_DIM
    cut = length - rim_rows

    def split(array):
        return array.reshape(block_count, length, array.shape[1])
    query_split = split(query)
    key_split = split(key)
    value_split = split(value)
    wquery_split = split(window_query)
    wkey_split = split(window_key)
    cot_split = split(cotangent)
    rim_key = jnp.concatenate([jnp.zeros((1, rim_rows, full_width), jnp.bfloat16), wkey_split[:-1, cut:]], axis=0)
    rim_value = jnp.concatenate([jnp.zeros((1, rim_rows, full_width), jnp.bfloat16), value_split[:-1, cut:]], axis=0)
    rim_live = jnp.arange(block_count) > 0
    gain_heads = gain.astype(jnp.float32).reshape(head_count, head_width)

    def state_terms(items):
        feat_key = narrow(taylor(items[0], head_count, features)).astype(jnp.float32)
        value_heads = items[1].astype(jnp.float32).reshape(length, head_count, head_width)
        return (jnp.einsum('the,thd->hed', feat_key, value_heads), lax.optimization_barrier(jnp.sum(feat_key, axis=0)))
    block_state, block_norm = lax.map(state_terms, (key_split, value_split))
    prefix_state = before_sum(block_state)
    prefix_norm = before_sum(block_norm)

    def forward(items):
        query_part, key_part, value_part, wquery_part, wkey_part, cot_part, state_part, norm_part, rim_key_part, rim_value_part, live_part = items
        feat_query = narrow(taylor(query_part, head_count, features)).astype(jnp.float32)
        scores, kernel, kernel_narrow, causal = kernel_parts(query_part, key_part, head_count, features)
        value_heads = value_part.astype(jnp.float32).reshape(length, head_count, head_width)
        numer = jnp.einsum('hts,shd->thd', kernel_narrow.astype(jnp.float32), value_heads) + jnp.einsum('the,hed->thd', feat_query, state_part, precision=HIGHEST)
        denom = lax.optimization_barrier(jnp.sum(kernel, axis=2)).T + jnp.einsum('the,he->th', feat_query, norm_part, precision=HIGHEST)
        linear = numer / denom[:, :, None]
        window_out = window_parts(wquery_part, wkey_part, value_part, rim_key_part, rim_value_part, live_part, head_count, head_width, window)[5]
        merged = linear + window_out
        scaled_cot = cot_part.astype(jnp.float32).reshape(length, head_count, head_width) * gain_heads
        square_sum = lax.optimization_barrier(jnp.sum(merged * merged, axis=(1, 2)))
        cross_sum = lax.optimization_barrier(jnp.sum(scaled_cot * merged, axis=(1, 2)))
        rms = jnp.sqrt(square_sum / full_width + 1e-06)
        normed = (merged / rms[:, None, None] * gain_heads).astype(jnp.bfloat16).reshape(length, full_width)
        grad_out = (scaled_cot - merged * (cross_sum / (full_width * rms * rms))[:, None, None]) / rms[:, None, None]
        scaled_grad = grad_out / denom[:, :, None]
        scaled_narrow = narrow(scaled_grad).astype(jnp.float32)
        ratio_grad = lax.optimization_barrier(jnp.sum(grad_out * linear, axis=2)) / denom
        suffix_term = jnp.einsum('the,thd->hed', feat_query, scaled_narrow)
        suffix_norm_term = jnp.einsum('the,th->he', feat_query, ratio_grad, precision=HIGHEST)
        return (normed, grad_out, denom, ratio_grad, suffix_term, suffix_norm_term)
    normed, grad_out, denom, ratio_grad, suffix_term, suffix_norm_term = lax.map(forward, (query_split, key_split, value_split, wquery_split, wkey_split, cot_split, prefix_state, prefix_norm, rim_key, rim_value, rim_live))
    suffix_state = after_sum(suffix_term)
    suffix_norm = after_sum(suffix_norm_term)

    def backward(items):
        query_part, key_part, value_part, wquery_part, wkey_part, grad_part, denom_part, ratio_part, state_part, norm_part, suffix_part, suffix_norm_part, rim_key_part, rim_value_part, live_part = items
        feat_key = narrow(taylor(key_part, head_count, features)).astype(jnp.float32)
        scores, kernel, kernel_narrow, causal = kernel_parts(query_part, key_part, head_count, features)
        weights, weights_narrow, query_blocks, key_blocks, value_blocks, window_out = window_parts(wquery_part, wkey_part, value_part, rim_key_part, rim_value_part, live_part, head_count, head_width, window)
        groups = length // window
        grad_narrow = narrow(grad_part).astype(jnp.float32)
        grad_blocks = grad_narrow.reshape(groups, window, head_count, head_width)
        dprob = jnp.einsum('bihd,bjhd->bhij', grad_blocks, value_blocks.astype(jnp.float32))
        delta = lax.optimization_barrier(jnp.sum(weights * dprob, axis=3, keepdims=True))
        dlogits = narrow(weights * (dprob - delta)).astype(jnp.float32)
        grad_wquery = (jnp.einsum('bhij,bjhd->bihd', dlogits, key_blocks.astype(jnp.float32)) / math.sqrt(head_width)).reshape(length, full_width).astype(jnp.bfloat16)
        key_grads = unblock(jnp.einsum('bhij,bihd->bjhd', dlogits, query_blocks.astype(jnp.float32)) / math.sqrt(head_width), window)
        value_grads = unblock(jnp.einsum('bhij,bihd->bjhd', weights_narrow.astype(jnp.float32), grad_blocks), window)
        value_heads = value_part.astype(jnp.float32).reshape(length, head_count, head_width)
        scaled_grad = grad_part / denom_part[:, :, None]
        scaled_narrow = narrow(scaled_grad).astype(jnp.float32)
        dscores = (jnp.einsum('thd,shd->hts', scaled_narrow, value_heads) - ratio_part.T[:, :, None]) * (1.0 + scores)
        dscores_narrow = narrow(jnp.where(causal, dscores, 0.0)).astype(jnp.float32)
        query_heads = query_part.astype(jnp.float32).reshape(length, head_count, features)
        key_heads = key_part.astype(jnp.float32).reshape(length, head_count, features)
        local_query = jnp.einsum('hts,shf->thf', dscores_narrow, key_heads) / math.sqrt(features)
        local_key = jnp.einsum('hts,thf->shf', dscores_narrow, query_heads) / math.sqrt(features)
        dfeat_query = jnp.einsum('hed,thd->the', state_part, scaled_grad, precision=HIGHEST) - ratio_part[:, :, None] * norm_part[None]
        dfeat_key = jnp.einsum('hed,thd->the', suffix_part, value_heads, precision=HIGHEST) - suffix_norm_part[None]
        grad_query = (local_query.reshape(length, head_count * features) + taylor_back(query_part, head_count, features, dfeat_query)).astype(jnp.bfloat16)
        grad_key = (local_key.reshape(length, head_count * features) + taylor_back(key_part, head_count, features, dfeat_key)).astype(jnp.bfloat16)
        value_linear = (jnp.einsum('hts,thd->shd', kernel_narrow.astype(jnp.float32), scaled_narrow) + jnp.einsum('the,hed->thd', feat_key, suffix_part, precision=HIGHEST)).reshape(length, full_width)
        value_sum = value_linear + value_grads[window:]
        key_sum = key_grads[window:]
        return (grad_query, grad_key, grad_wquery, value_sum[:cut].astype(jnp.bfloat16), value_sum[cut:], key_sum[:cut].astype(jnp.bfloat16), key_sum[cut:], key_grads[1:window], value_grads[1:window])
    grad_query, grad_key, grad_wquery, value_front, value_tail, key_front, key_tail, rim_key_grads, rim_value_grads = lax.map(backward, (query_split, key_split, value_split, wquery_split, wkey_split, grad_out, denom, ratio_grad, prefix_state, prefix_norm, suffix_state, suffix_norm, rim_key, rim_value, rim_live))
    back_key = jnp.concatenate([rim_key_grads[1:], jnp.zeros_like(rim_key_grads[:1])], axis=0)
    back_value = jnp.concatenate([rim_value_grads[1:], jnp.zeros_like(rim_value_grads[:1])], axis=0)
    grad_value = jnp.concatenate([value_front, (value_tail + back_value).astype(jnp.bfloat16)], axis=1).reshape(TOKENS, full_width)
    grad_wkey = jnp.concatenate([key_front, (key_tail + back_key).astype(jnp.bfloat16)], axis=1).reshape(TOKENS, full_width)
    return (normed.reshape(TOKENS, full_width), grad_query.reshape(TOKENS, head_count * features), grad_key.reshape(TOKENS, head_count * features), grad_value, grad_wquery.reshape(TOKENS, full_width), grad_wkey)
```

```python
import math

import jax
import jax.numpy as jnp
import numpy as np
from jax import lax
from jax.experimental import pallas as pl
from jax.experimental.pallas import tpu as pltpu
from jax.sharding import PartitionSpec as P

HEADS = 16
HEAD_DIM = 128
FEAT = 16
WINDOW = 64
CHUNKS = 2

QUAD = FEAT * (FEAT + 1) // 2
LINEAR = QUAD
CONST = QUAD + FEAT
ROWS = 160
ROOT_HALF = float(np.float32(math.sqrt(0.5)))
SCORE = 1.0 / math.sqrt(FEAT)

F32 = jnp.float32
BF16 = jnp.bfloat16
VMEM_LIMIT = 24 * 1024 * 1024


def feature_tables():
    first = np.zeros((ROWS, FEAT), np.float32)
    second = np.zeros((ROWS, FEAT), np.float32)
    rows = np.zeros((8, ROWS), np.float32)
    scale = FEAT ** (-0.25)
    place = 0
    for distance in range(FEAT // 2 + 1):
        for i in range(FEAT if distance < FEAT // 2 else FEAT // 2):
            first[place, i] = scale
            second[place, (i + distance) % FEAT] = scale
            rows[2, place] = ROOT_HALF * (1.0 if distance == 0 else 2.0)
            place += 1
    for i in range(FEAT):
        first[LINEAR + i, i] = scale
    rows[1, LINEAR:CONST] = 1.0
    rows[0:2, CONST] = 1.0
    rows[2, LINEAR : CONST + 1] = 1.0
    sel = np.concatenate([first, second], axis=0)
    sel_t = np.concatenate([first.T, second.T], axis=0)
    return jnp.asarray(sel, BF16), jnp.asarray(sel_t, BF16), jnp.asarray(rows)


def mm(a, b):
    return lax.dot_general(a, b, (((1,), (0,)), ((), ())), preferred_element_type=F32)


def mm_nt(a, b):
    return lax.dot_general(a, b, (((1,), (1,)), ((), ())), preferred_element_type=F32)


def mm_tn(a, b):
    return lax.dot_general(a, b, (((0,), (0,)), ((), ())), preferred_element_type=F32)


def halves(x):
    high = x.astype(BF16)
    return high, (x - high.astype(F32)).astype(BF16)


def lane_sum(x):
    return jnp.sum(x, axis=1, keepdims=True)


def span(h, size):
    return slice(h * size, (h + 1) * size)


def iota(shape, axis):
    return lax.broadcasted_iota(jnp.int32, shape, axis)


def stack8(lines):
    count = -(-len(lines) // 8) * 8
    place = iota((count, lines[0].shape[1]), 0)
    out = jnp.zeros(place.shape, F32)
    for i, line in enumerate(lines):
        out = jnp.where(place == i, line, out)
    return out.astype(BF16)


def split(x):
    high = x.astype(BF16).astype(F32)
    return high, (x - high).astype(BF16).astype(F32)


def feature_rows(inputs_t, sel):
    a = mm(sel[:ROWS], inputs_t)
    b = mm(sel[ROWS : ROWS + QUAD], inputs_t)
    tail = (iota((ROWS - CONST, inputs_t.shape[1]), 0) == 0).astype(F32)
    return jnp.concatenate([a[:QUAD] * b * ROOT_HALF, a[LINEAR:CONST], tail], axis=0).astype(BF16)


def weighted_features(inputs_t, sel_t, rows):
    a = mm_tn(inputs_t, sel_t[:FEAT]) + rows[0:1]
    b = mm_tn(inputs_t, sel_t[FEAT:]) + rows[1:2]
    return (a * b * rows[2:3]).astype(BF16)


def pull_back(upstream, inputs_t, sel, sel_t):
    a = mm(sel[:QUAD], inputs_t)
    b = mm(sel[ROWS : ROWS + QUAD], inputs_t)
    squares = upstream[:FEAT] * ROOT_HALF
    others = upstream[FEAT:QUAD] * (2.0 * ROOT_HALF)
    on_first = jnp.concatenate([squares * b[:FEAT], others * b[FEAT:], upstream[LINEAR:CONST]], axis=0)
    on_second = jnp.concatenate([squares * a[:FEAT], others * a[FEAT:]], axis=0)
    first_high, first_low = halves(on_first)
    second_high, second_low = halves(on_second)
    first_t = sel_t[:FEAT, :CONST]
    second_t = sel_t[FEAT:, :QUAD]
    return (mm(first_t, first_high) + mm(second_t, second_high)) + (mm(first_t, first_low) + mm(second_t, second_low))


def norm_tile(norm):
    high, low = split(norm)
    pad = jnp.zeros((1, 256 - ROWS), F32)
    row = iota((8, 128), 0)
    out = jnp.where(row == 1, high[:, :128], 0.0)
    out = jnp.where(row == 2, jnp.concatenate([high[:, 128:], pad], axis=1), out)
    out = jnp.where(row == 3, low[:, :128], out)
    return jnp.where(row == 4, jnp.concatenate([low[:, 128:], pad], axis=1), out)


def tile_norm(tile):
    return jnp.concatenate([tile[1:2] + tile[3:4], (tile[2:3] + tile[4:5])[:, : ROWS - 128]], axis=1)


def outer(pairs):
    left, right = [], []
    for a, b in pairs:
        a_high, a_low = split(a)
        b_high, b_low = split(b)
        left += [a_high, a_low, a_high]
        right += [b_high, b_high, b_low]
    return mm_tn(stack8(left), stack8(right))


def store_state(out_ref, head, state, tile):
    row = iota((8, 128), 0)
    last = jnp.where(row == 0, state[CONST:], tile)
    out_ref[span(head, ROWS), :] = jnp.concatenate([state[:CONST], last], axis=0).astype(BF16)


def causal_mask(length):
    return iota((length, length), 0) >= iota((length, length), 1)


def state_body(key_hbm, value_hbm, wkey_hbm, sel_hbm, sel_t_hbm, rows_hbm, *refs):
    states = refs[:CHUNKS]
    rim_ref, key_ref, value_ref, sel_ref, sel_t_ref, rows_ref, sems = refs[CHUNKS:]
    length, width = value_ref.shape
    heads = width // HEAD_DIM
    cut = length - WINDOW
    pairs = [
        (key_hbm, key_ref),
        (sel_hbm, sel_ref),
        (value_hbm, value_ref),
        (wkey_hbm.at[cut:length, :], rim_ref.at[0:WINDOW, :]),
        (value_hbm.at[cut:length, :], rim_ref.at[WINDOW : 2 * WINDOW, :]),
        (sel_t_hbm, sel_t_ref),
        (rows_hbm, rows_ref),
    ]
    copies = [pltpu.make_async_copy(a, b, sems.at[i]) for i, (a, b) in enumerate(pairs)]
    for copy in copies:
        copy.start()
    for copy in copies[:3]:
        copy.wait()
    sel = sel_ref[...]
    ones = jnp.ones((8, length), BF16)
    place = iota((8, 128), 0)
    for h in range(heads):
        feat = feature_rows(key_ref[span(h, FEAT), :], sel)
        state = mm(feat, value_ref[:, span(h, HEAD_DIM)])
        norm = mm_nt(ones, feat)[0:1]
        middle = (state[CONST : CONST + 1] * (1.0 / length)).astype(BF16).astype(F32)
        high, low = split(norm)
        state = state - mm_tn(stack8([high, low]), stack8([middle, middle]))
        tile = jnp.where(place == 5, middle, norm_tile(norm))
        per = heads // CHUNKS
        store_state(states[h // per], h % per, state, tile)
    for copy in copies[3:]:
        copy.wait()


def add_about_body(mine_ref, theirs_ref, out_ref):
    place = iota((8, 128), 0)
    for h in range(mine_ref.shape[0] // ROWS):
        mine = mine_ref[span(h, ROWS), :].astype(F32)
        theirs = theirs_ref[span(h, ROWS), :].astype(F32)
        mine_tile, their_tile = mine[CONST:], theirs[CONST:]
        mine_norm, their_norm = tile_norm(mine_tile), tile_norm(their_tile)
        mine_middle, their_middle = mine_tile[5:6], their_tile[5:6]
        middle = (0.5 * (mine_middle + their_middle)).astype(BF16).astype(F32)
        moved = outer([(mine_norm, mine_middle - middle), (their_norm, their_middle - middle)])
        tile = jnp.where(place == 5, middle, norm_tile(mine_norm + their_norm))
        store_state(out_ref, h, mine + theirs + moved, tile)


def add_body(mine_ref, theirs_ref, out_ref):
    for h in range(mine_ref.shape[0] // ROWS):
        total = mine_ref[span(h, ROWS), :].astype(F32) + theirs_ref[span(h, ROWS), :].astype(F32)
        store_state(out_ref, h, total, norm_tile(tile_norm(total[CONST:])))


def local_body(query_hbm, wquery_hbm, wkey_hbm, cot_hbm, gain_hbm, key_ref, value_ref, sel_ref, sel_t_ref, rows_ref,
               numer_ref, denom_ref, featq_ref, featq_t_ref, featk_ref, query_ref, wquery_ref, wkey_ref, cot_ref, gain_ref, sems):
    pairs = [(query_hbm, query_ref), (wquery_hbm, wquery_ref), (wkey_hbm, wkey_ref), (cot_hbm, cot_ref), (gain_hbm, gain_ref)]
    copies = [pltpu.make_async_copy(a, b, sems.at[i]) for i, (a, b) in enumerate(pairs)]
    for copy in copies:
        copy.start()
    length = value_ref.shape[0]
    heads = value_ref.shape[1] // HEAD_DIM
    sel = sel_ref[...]
    sel_t = sel_t_ref[...]
    rows = rows_ref[...]
    for h in range(heads):
        featk_ref[h] = weighted_features(key_ref[span(h, FEAT), :], sel_t, rows)
    copies[0].wait()
    causal = causal_mask(length)
    lane = iota((length, 128), 1)
    denoms = jnp.zeros((length, 128), F32)
    for h in range(heads):
        query = query_ref[span(h, FEAT), :]
        featq_t_ref[span(h, ROWS), :] = feature_rows(query, sel)
        featq_ref[h] = weighted_features(query, sel_t, rows)
        scores = mm_tn(query, key_ref[span(h, FEAT), :]) * SCORE
        kernel = jnp.where(causal, 1.0 + scores + 0.5 * scores * scores, 0.0)
        denoms = jnp.where(lane == h, lane_sum(kernel), denoms)
        numer_ref[:, span(h, HEAD_DIM)] = mm(kernel.astype(BF16), value_ref[:, span(h, HEAD_DIM)])
    denom_ref[...] = denoms
    for copy in copies[1:]:
        copy.wait()


def window_body(place_ref, wquery_ref, wkey_ref, value_ref, rim_ref, out_ref, weights_ref):
    length = wquery_ref.shape[0]
    heads = value_ref.shape[1] // HEAD_DIM
    live = place_ref[0] > 0
    row = iota((WINDOW, 2 * WINDOW), 0)
    col = iota((WINDOW, 2 * WINDOW), 1)
    inside = (col > row) & (col <= row + WINDOW)
    edge = inside & ((col >= WINDOW) | live)
    starts = range(0, length, WINDOW)
    allowed = jnp.concatenate([edge] + [inside] * (len(starts) - 1), axis=0)
    for h in range(heads):
        columns = span(h, HEAD_DIM)
        keys = jnp.concatenate([rim_ref[:WINDOW, columns], wkey_ref[:, columns]], axis=0)
        values = jnp.concatenate([rim_ref[WINDOW:, columns], value_ref[:, columns]], axis=0)
        query = wquery_ref[:, columns]
        logits = jnp.concatenate([mm_nt(query[s : s + WINDOW], keys[s : s + 2 * WINDOW]) for s in starts], axis=0)
        masked = jnp.where(allowed, logits * (1.0 / math.sqrt(HEAD_DIM)), -1e30)
        exponent = jnp.where(allowed, jnp.exp(masked - jnp.max(masked, axis=1, keepdims=True)), 0.0)
        weights = exponent * (1.0 / lane_sum(exponent))
        weights_ref[h] = weights
        narrow = weights.astype(BF16)
        out_ref[:, columns] = jnp.concatenate([mm(narrow[s : s + WINDOW], values[s : s + 2 * WINDOW]) for s in starts], axis=0)


def taken(place_ref, step, later):
    bit = (place_ref[0] >> step) & 1
    return (1 - bit if later else bit).astype(F32)


def merge_body(steps, chunk, place_ref, *refs):
    parts = refs[:steps]
    feat_ref, numer_ref, denom_ref, window_ref, gain_ref, cot_ref = refs[steps : steps + 6]
    before = refs[steps + 6 : steps + 6 + (2 if chunk else 0)]
    outs = refs[steps + 6 + len(before) :]
    merged_ref, linear_ref, inverse_ref, prefix_ref, norm_ref = outs[:5]
    length = numer_ref.shape[0]
    per = merged_ref.shape[1] // HEAD_DIM
    lane = iota((length, 128), 1)
    inverses = jnp.zeros((length, 128), F32)
    squares = before[0][...] if chunk else jnp.zeros((length, HEAD_DIM), F32)
    crosses = before[1][...] if chunk else jnp.zeros((length, HEAD_DIM), F32)
    for h in range(per):
        whole = chunk * per + h
        state = norm = None
        left, right = [], []
        for step, part in enumerate(parts):
            take = taken(place_ref, step, False)
            block = part[span(h, ROWS), :].astype(F32) * take
            block_norm = tile_norm(block[CONST:])
            middle = part[span(h, ROWS), :].astype(F32)[CONST + 5 : CONST + 6]
            left += list(split(block_norm))
            right += [middle, middle]
            state = block if state is None else state + block
            norm = block_norm if norm is None else norm + block_norm
        state = state + mm_tn(stack8(left), stack8(right))
        prefix_ref[span(h, ROWS), :] = state
        norm_ref[span(h, 8), :] = jnp.broadcast_to(norm, (8, ROWS))
        high, low = halves(state)
        feat = feat_ref[whole]
        numer = numer_ref[:, span(whole, HEAD_DIM)] + mm(feat, high) + mm(feat, low)
        extra = mm_nt(feat, stack8(list(split(norm))))
        inverse = 1.0 / (denom_ref[:, whole : whole + 1] + (extra[:, 0:1] + extra[:, 1:2]))
        inverses = jnp.where(lane == h, inverse, inverses)
        linear = numer * inverse
        linear_ref[:, span(h, HEAD_DIM)] = linear
        merged = linear + window_ref[:, span(whole, HEAD_DIM)]
        merged_ref[:, span(h, HEAD_DIM)] = merged
        squares = squares + merged * merged
        scaled_cot = cot_ref[:, span(whole, HEAD_DIM)].astype(F32) * gain_ref[0:1, span(whole, HEAD_DIM)]
        crosses = crosses + scaled_cot * merged
    inverse_ref[...] = inverses
    if chunk + 1 < CHUNKS:
        outs[5][...] = squares
        outs[6][...] = crosses
    else:
        stats = jnp.where(lane == 0, lane_sum(squares), jnp.where(lane == 1, lane_sum(crosses), 0.0))
        outs[5][...] = jnp.transpose(stats)[:8]


def grad_body(width, stats_ref, *refs):
    merged_refs, linear_refs, inverse_refs = refs[:CHUNKS], refs[CHUNKS : 2 * CHUNKS], refs[2 * CHUNKS : 3 * CHUNKS]
    gain_ref, cot_ref, feat_t_ref = refs[3 * CHUNKS : 3 * CHUNKS + 3]
    terms = refs[3 * CHUNKS + 3 : 4 * CHUNKS + 3]
    grad_ref, cols_ref, ratios_ref = refs[4 * CHUNKS + 3 :]
    length = grad_ref.shape[0]
    heads = grad_ref.shape[1] // HEAD_DIM
    per = heads // CHUNKS
    sums = jnp.transpose(jnp.concatenate([stats_ref[...], jnp.zeros((120, length), F32)], axis=0))
    mean = sums[:, 0:1] / width + 1e-6
    inv_rms = 1.0 / jnp.sqrt(mean)
    pull = sums[:, 1:2] / (width * mean)
    lane = iota((length, 128), 1)
    cols = jnp.where(lane == heads, inv_rms, 0.0)
    narrows = []
    for h in range(heads):
        chunk, local = h // per, span(h % per, HEAD_DIM)
        inverse = inverse_refs[chunk][:, h % per : h % per + 1]
        scaled_cot = cot_ref[:, span(h, HEAD_DIM)].astype(F32) * gain_ref[0:1, span(h, HEAD_DIM)]
        grad = (scaled_cot - merged_refs[chunk][:, local] * pull) * inv_rms
        grad_ref[:, span(h, HEAD_DIM)] = grad
        narrows.append((grad * inverse).astype(BF16))
        cols = jnp.where(lane == h, lane_sum(grad * linear_refs[chunk][:, local]) * inverse, cols)
    cols_ref[...] = cols
    ratios = jnp.transpose(cols)[:8]
    ratios_ref[...] = ratios
    for h in range(heads):
        feat = feat_t_ref[span(h, ROWS), :]
        norm = mm_nt(stack8(list(split(ratios[h : h + 1]))), feat)
        store_state(terms[h // per], h % per, mm(feat, narrows[h]), norm_tile(norm[0:1] + norm[1:2]))


def window_back_body(wquery_ref, wkey_ref, value_ref, rim_ref, weights_ref, grad_ref, gwq_ref, gwk_ref, gv_ref, back_ref):
    length = wquery_ref.shape[0]
    heads = value_ref.shape[1] // HEAD_DIM
    root = 1.0 / math.sqrt(HEAD_DIM)
    starts = range(0, length, WINDOW)
    pad = jnp.zeros((WINDOW, HEAD_DIM), F32)
    for h in range(heads):
        columns = span(h, HEAD_DIM)
        keys = jnp.concatenate([rim_ref[:WINDOW, columns], wkey_ref[:, columns]], axis=0)
        values = jnp.concatenate([rim_ref[WINDOW:, columns], value_ref[:, columns]], axis=0)
        grad = grad_ref[:, columns].astype(BF16)
        query = wquery_ref[:, columns]
        weights = weights_ref[h]
        narrow = weights.astype(BF16)
        dprob = jnp.concatenate([mm_nt(grad[s : s + WINDOW], values[s : s + 2 * WINDOW]) for s in starts], axis=0)
        dlogits = (weights * (dprob - lane_sum(weights * dprob))).astype(BF16)
        grads = [mm(dlogits[s : s + WINDOW], keys[s : s + 2 * WINDOW]) for s in starts]
        gwq_ref[:, columns] = (jnp.concatenate(grads, axis=0) * root).astype(BF16)
        key_parts = [mm_tn(dlogits[s : s + WINDOW], query[s : s + WINDOW]) for s in starts]
        value_parts = [mm_tn(narrow[s : s + WINDOW], grad[s : s + WINDOW]) for s in starts]
        back_ref[:WINDOW, columns] = (key_parts[0][:WINDOW] * root).astype(BF16)
        back_ref[WINDOW:, columns] = value_parts[0][:WINDOW].astype(BF16)
        key_sum = [a[WINDOW:] + b[:WINDOW] for a, b in zip(key_parts, key_parts[1:] + [pad])]
        value_sum = [a[WINDOW:] + b[:WINDOW] for a, b in zip(value_parts, value_parts[1:] + [pad])]
        gwk_ref[:, columns] = jnp.concatenate(key_sum, axis=0) * root
        gv_ref[:, columns] = jnp.concatenate(value_sum, axis=0)


def local_back_body(query_ref, key_ref, value_ref, sel_ref, sel_t_ref, grad_ref, cols_ref, ratios_ref, gv_in_ref, gain_ref, *refs):
    merged_refs, inverse_refs = refs[:CHUNKS], refs[CHUNKS : 2 * CHUNKS]
    prefix_refs, norm_refs = refs[2 * CHUNKS : 3 * CHUNKS], refs[3 * CHUNKS : 4 * CHUNKS]
    gq_ref, gk_ref, gv_ref, normed_ref = refs[4 * CHUNKS :]
    length = value_ref.shape[0]
    heads = value_ref.shape[1] // HEAD_DIM
    per = heads // CHUNKS
    sel = sel_ref[...]
    sel_t = sel_t_ref[...]
    causal = causal_mask(length)
    inv_rms = cols_ref[:, heads : heads + 1]
    for h in range(heads):
        chunk, columns = h // per, span(h, HEAD_DIM)
        merged = merged_refs[chunk][:, span(h % per, HEAD_DIM)]
        normed_ref[:, columns] = (merged * inv_rms * gain_ref[0:1, columns]).astype(BF16)
        scaled = grad_ref[:, columns] * inverse_refs[chunk][:, h % per : h % per + 1]
        narrow, rest = halves(scaled)
        query = query_ref[span(h, FEAT), :]
        key = key_ref[span(h, FEAT), :]
        scores = mm_tn(query, key) * SCORE
        kernel = jnp.where(causal, 1.0 + scores + 0.5 * scores * scores, 0.0).astype(BF16)
        dscores = (mm_nt(narrow, value_ref[:, columns]) - cols_ref[:, h : h + 1]) * (1.0 + scores)
        dscores = jnp.where(causal, dscores, 0.0).astype(BF16)
        gk_ref[span(h, FEAT), :] = mm(query, dscores) * SCORE
        gv_ref[:, columns] = gv_in_ref[:, columns] + mm_tn(kernel, narrow)
        high, low = halves(prefix_refs[chunk][span(h % per, ROWS), :])
        upstream = mm_nt(high, narrow) + (mm_nt(low, narrow) + mm_nt(high, rest))
        upstream = upstream - outer([(norm_refs[chunk][h % per * 8 : h % per * 8 + 1, :], ratios_ref[h : h + 1, :])])
        through = pull_back(upstream, query, sel, sel_t)
        gq_ref[span(h, FEAT), :] = (mm_nt(key, dscores) * SCORE + through).astype(BF16)


def final_body(steps, chunk, place_ref, *refs):
    parts = refs[:steps]
    key_ref, value_ref, sel_ref, sel_t_ref, feat_ref, gk_in_ref, gv_in_ref, back_ref = refs[steps : steps + 8]
    rest = refs[steps + 8 :]
    length = value_ref.shape[0]
    per = parts[0].shape[0] // ROWS
    cut = length - WINDOW
    sel = sel_ref[...]
    sel_t = sel_t_ref[...]
    ones = jnp.where(iota((8, length), 0) < 2, 1.0, 0.0).astype(BF16)
    if chunk + 1 < CHUNKS:
        gwk_in_ref, gk_ref, gv_ref, gwk_ref = rest
        gwk_ref[:cut, :] = gwk_in_ref[:cut, :].astype(BF16)
        gwk_ref[cut:, :] = (gwk_in_ref[cut:, :] + back_ref[:WINDOW, :].astype(F32)).astype(BF16)
        base = 0
    else:
        gk_before, gv_before, gk_ref, gv_ref = rest
        base = chunk * per
        gk_ref[: base * FEAT, :] = gk_before[...]
        gv_ref[:, : base * HEAD_DIM] = gv_before[...]
    for h in range(per):
        whole = chunk * per + h
        columns = span(whole, HEAD_DIM)
        state = None
        for step, part in enumerate(parts):
            block = part[span(h, ROWS), :].astype(F32) * taken(place_ref, step, True)
            state = block if state is None else state + block
        high, low = halves(state)
        value = value_ref[:, columns]
        grad_value = gv_in_ref[:, columns] + (mm(feat_ref[whole], high) + mm(feat_ref[whole], low))
        out_columns = span(base + h, HEAD_DIM)
        gv_ref[:cut, out_columns] = grad_value[:cut].astype(BF16)
        gv_ref[cut:, out_columns] = (grad_value[cut:] + back_ref[WINDOW:, columns].astype(F32)).astype(BF16)
        norm = mm_tn(stack8(list(split(tile_norm(state[CONST:])))), ones)
        upstream = mm_nt(high, value) + mm_nt(low, value) - norm
        through = pull_back(upstream, key_ref[span(whole, FEAT), :], sel, sel_t)
        gk_ref[span(base + h, FEAT), :] = (gk_in_ref[span(whole, FEAT), :] + through).astype(BF16)


def call(body, outs, *args, place=None, hbm=0, copies=0):
    vmem = pl.BlockSpec(memory_space=pltpu.VMEM)
    specs = [pl.BlockSpec(memory_space=pltpu.HBM)] * hbm + [vmem] * (len(args) - hbm)
    args = tuple(pltpu.with_memory_space_constraint(a, pltpu.HBM) if i < hbm else a for i, a in enumerate(args))
    if place is not None:
        specs = [pl.BlockSpec(memory_space=pltpu.SMEM)] + specs
        args = (place,) + args
    return pl.pallas_call(
        body,
        out_shape=[jax.ShapeDtypeStruct(shape, dtype) for shape, dtype in outs],
        in_specs=specs,
        out_specs=[vmem] * len(outs),
        scratch_shapes=[pltpu.SemaphoreType.DMA((copies,))] if copies else [],
        compiler_params=pltpu.CompilerParams(vmem_limit_bytes=VMEM_LIMIT),
    )(*args)


def exchanged(states, add, after_first):
    count = lax.axis_size("seq")
    states = list(states)
    parts = [[] for _ in states]
    extra = None
    step = 1
    while step < count:
        pairs = [(i, i ^ step) for i in range(count)]
        for c, state in enumerate(states):
            parts[c].append(lax.ppermute(state, "seq", pairs))
        if extra is None:
            extra = after_first()
        step *= 2
        if step < count:
            for c, state in enumerate(states):
                (states[c],) = call(add, [(state.shape, BF16)], state, parts[c][-1])
    return parts, states, extra


def shards(query, key, value, window_query, window_key, gain, cotangent):
    length, width = value.shape
    heads = width // HEAD_DIM
    per = heads // CHUNKS
    count = lax.axis_size("seq")
    full_width = HEADS * HEAD_DIM
    place = lax.axis_index("seq").astype(jnp.int32).reshape(1)
    gain_row = gain.reshape(1, width)
    query_t, key_t = query.T, key.T
    state_shape = ((per * ROWS, HEAD_DIM), BF16)
    wide = ((length, width), F32)
    wide_narrow = ((length, width), BF16)
    tables = feature_tables()

    *states, rim, key_v, value_v, sel, sel_t, rows = call(
        state_body,
        [state_shape] * CHUNKS
        + [((2 * WINDOW, width), BF16), (key_t.shape, BF16), wide_narrow]
        + [(t.shape, t.dtype) for t in tables],
        key_t, value, window_key, *tables, hbm=6, copies=7,
    )

    def early():
        rim_in = lax.ppermute(rim, "seq", [(i, i + 1) for i in range(count - 1)])
        local = call(
            local_body,
            [wide, ((length, 128), F32), ((heads, length, ROWS), BF16), ((heads * ROWS, length), BF16), ((heads, length, ROWS), BF16),
             (query_t.shape, BF16), wide_narrow, wide_narrow, wide_narrow, (gain_row.shape, F32)],
            query_t, window_query, window_key, cotangent, gain_row, key_v, value_v, sel, sel_t, rows, hbm=5, copies=5,
        )
        return rim_in, local

    parts, _, (rim_in, local) = exchanged(states, add_about_body, early)
    numer, denom, featq, featq_t, featk, query_v, wquery, wkey, cot, gain_v = local
    window_out, weights = call(
        window_body, [wide, ((heads, length, 2 * WINDOW), F32)], wquery, wkey, value_v, rim_in, place=place
    )
    steps = len(parts[0])
    half = ((length, per * HEAD_DIM), F32)
    square = ((length, 128), F32)
    merged, linear, inverse, prefix, norm, before = [], [], [], [], [], []
    for c in range(CHUNKS):
        tail = [((8, length), F32)] if c + 1 == CHUNKS else [square, square]
        out = call(
            lambda *refs, c=c: merge_body(steps, c, *refs),
            [half, half, square, ((per * ROWS, HEAD_DIM), F32), ((per * 8, ROWS), F32)] + tail,
            *parts[c], featq, numer, denom, window_out, gain_v, cot, *before, place=place,
        )
        for held, item in zip((merged, linear, inverse, prefix, norm), out):
            held.append(item)
        before = out[5:]
    (stats,) = before
    ring = lax.axis_size("head")
    step = 1
    while step < ring:
        stats = stats + lax.ppermute(stats, "head", [(i, i ^ step) for i in range(ring)])
        step *= 2
    *terms, grad, cols, ratios = call(
        lambda *refs: grad_body(float(full_width), *refs),
        [state_shape] * CHUNKS + [wide, square, ((8, length), F32)],
        stats, *merged, *linear, *inverse, gain_v, cot, featq_t,
    )

    def middle():
        grad_wquery, wkey_part, value_part, back = call(
            window_back_body,
            [wide_narrow, wide, wide, ((2 * WINDOW, width), BF16)],
            wquery, wkey, value_v, rim_in, weights, grad,
        )
        back = lax.ppermute(back, "seq", [(i + 1, i) for i in range(count - 1)])
        return grad_wquery, wkey_part, value_part, back

    parts, _, (grad_wquery, wkey_part, value_part, back) = exchanged(terms, add_body, middle)
    grad_query, key_part, value_part, normed = call(
        local_back_body,
        [(query_t.shape, BF16), (key_t.shape, F32), wide, wide_narrow],
        query_v, key_v, value_v, sel, sel_t, grad, cols, ratios, value_part, gain_v, *merged, *inverse, *prefix, *norm,
    )
    common = (key_v, value_v, sel, sel_t, featk, key_part, value_part, back)
    grad_key, grad_value, grad_wkey = call(
        lambda *refs: final_body(steps, 0, *refs),
        [((per * FEAT, length), BF16), ((length, per * HEAD_DIM), BF16), wide_narrow],
        *parts[0], *common, wkey_part, place=place,
    )
    grad_key, grad_value = call(
        lambda *refs: final_body(steps, 1, *refs),
        [(key_t.shape, BF16), wide_narrow],
        *parts[1], *common, grad_key, grad_value, place=place,
    )
    return (normed, grad_query.T, grad_key.T, grad_value, grad_wquery, grad_wkey)


def solution(mesh):
    placed = P("seq", "head")
    return jax.shard_map(
        shards,
        mesh=mesh,
        in_specs=(placed, placed, placed, placed, placed, P("head"), placed),
        out_specs=(placed,) * 6,
        check_vma=False,
    )
```

```python
import math

import jax
import jax.numpy as jnp
import numpy as np
from jax import lax
from jax.experimental import pallas as pl
from jax.experimental.pallas import tpu as pltpu
from jax.sharding import PartitionSpec as P

HEADS = 16
HEAD_DIM = 128
FEAT = 16
WINDOW = 64
CHUNKS = 2

QUAD = FEAT * (FEAT + 1) // 2
LINEAR = QUAD
CONST = QUAD + FEAT
ROWS = 160
ROOT_HALF = float(np.float32(math.sqrt(0.5)))
SCORE = 1.0 / math.sqrt(FEAT)

F32 = jnp.float32
BF16 = jnp.bfloat16
VMEM_LIMIT = 24 * 1024 * 1024


def feature_tables():
    first = np.zeros((ROWS, FEAT), np.float32)
    second = np.zeros((ROWS, FEAT), np.float32)
    rows = np.zeros((8, ROWS), np.float32)
    scale = FEAT ** (-0.25)
    place = 0
    for distance in range(FEAT // 2 + 1):
        for i in range(FEAT if distance < FEAT // 2 else FEAT // 2):
            first[place, i] = scale
            second[place, (i + distance) % FEAT] = scale
            rows[2, place] = ROOT_HALF * (1.0 if distance == 0 else 2.0)
            place += 1
    for i in range(FEAT):
        first[LINEAR + i, i] = scale
    rows[1, LINEAR:CONST] = 1.0
    rows[0:2, CONST] = 1.0
    rows[2, LINEAR : CONST + 1] = 1.0
    sel = np.concatenate([first, second], axis=0)
    sel_t = np.concatenate([first.T, second.T], axis=0)
    return jnp.asarray(sel, BF16), jnp.asarray(sel_t, BF16), jnp.asarray(rows)


def mm(a, b):
    return lax.dot_general(a, b, (((1,), (0,)), ((), ())), preferred_element_type=F32)


def mm_nt(a, b):
    return lax.dot_general(a, b, (((1,), (1,)), ((), ())), preferred_element_type=F32)


def mm_tn(a, b):
    return lax.dot_general(a, b, (((0,), (0,)), ((), ())), preferred_element_type=F32)


def halves(x):
    high = x.astype(BF16)
    return high, (x - high.astype(F32)).astype(BF16)


def lane_sum(x):
    return jnp.sum(x, axis=1, keepdims=True)


def span(h, size):
    return slice(h * size, (h + 1) * size)


def iota(shape, axis):
    return lax.broadcasted_iota(jnp.int32, shape, axis)


def stack8(lines):
    count = -(-len(lines) // 8) * 8
    place = iota((count, lines[0].shape[1]), 0)
    out = jnp.zeros(place.shape, F32)
    for i, line in enumerate(lines):
        out = jnp.where(place == i, line, out)
    return out.astype(BF16)


def split(x):
    high = x.astype(BF16).astype(F32)
    return high, (x - high).astype(BF16).astype(F32)


def feature_rows(inputs_t, sel):
    a = mm(sel[:ROWS], inputs_t)
    b = mm(sel[ROWS : ROWS + QUAD], inputs_t)
    tail = (iota((ROWS - CONST, inputs_t.shape[1]), 0) == 0).astype(F32)
    return jnp.concatenate([a[:QUAD] * b * ROOT_HALF, a[LINEAR:CONST], tail], axis=0).astype(BF16)


def weighted_features(inputs_t, sel_t, rows):
    a = mm_tn(inputs_t, sel_t[:FEAT]) + rows[0:1]
    b = mm_tn(inputs_t, sel_t[FEAT:]) + rows[1:2]
    return (a * b * rows[2:3]).astype(BF16)


def pull_back(upstreams, inputs_t, sel, sel_t):
    firsts = [mm(sel[:QUAD], x) for x in inputs_t]
    seconds = [mm(sel[ROWS : ROWS + QUAD], x) for x in inputs_t]
    first_t = sel_t[:FEAT, :CONST]
    second_t = sel_t[FEAT:, :QUAD]
    sides = []
    for upstream, a, b in zip(upstreams, firsts, seconds):
        squares = upstream[:FEAT] * ROOT_HALF
        others = upstream[FEAT:QUAD] * (2.0 * ROOT_HALF)
        on_first = jnp.concatenate([squares * b[:FEAT], others * b[FEAT:], upstream[LINEAR:CONST]], axis=0)
        on_second = jnp.concatenate([squares * a[:FEAT], others * a[FEAT:]], axis=0)
        sides.append(halves(on_first) + halves(on_second))
    return [
        (mm(first_t, p_high) + mm(second_t, q_high)) + (mm(first_t, p_low) + mm(second_t, q_low))
        for p_high, p_low, q_high, q_low in sides
    ]


def norm_tile(norm):
    high, low = split(norm)
    pad = jnp.zeros((1, 256 - ROWS), F32)
    row = iota((8, 128), 0)
    out = jnp.where(row == 1, high[:, :128], 0.0)
    out = jnp.where(row == 2, jnp.concatenate([high[:, 128:], pad], axis=1), out)
    out = jnp.where(row == 3, low[:, :128], out)
    return jnp.where(row == 4, jnp.concatenate([low[:, 128:], pad], axis=1), out)


def tile_norm(tile):
    return jnp.concatenate([tile[1:2] + tile[3:4], (tile[2:3] + tile[4:5])[:, : ROWS - 128]], axis=1)


def outer(pairs):
    left, right = [], []
    for a, b in pairs:
        a_high, a_low = split(a)
        b_high, b_low = split(b)
        left += [a_high, a_low, a_high]
        right += [b_high, b_high, b_low]
    return mm_tn(stack8(left), stack8(right))


def store_state(out_ref, head, state, tile):
    row = iota((8, 128), 0)
    last = jnp.where(row == 0, state[CONST:], tile)
    out_ref[span(head, ROWS), :] = jnp.concatenate([state[:CONST], last], axis=0).astype(BF16)


def causal_mask(length):
    return iota((length, length), 0) >= iota((length, length), 1)


def state_body(key_hbm, value_hbm, wkey_hbm, sel_hbm, sel_t_hbm, rows_hbm, *refs):
    states = refs[:CHUNKS]
    rim_ref, key_ref, value_ref, sel_ref, sel_t_ref, rows_ref, sems = refs[CHUNKS:]
    length, width = value_ref.shape
    heads = width // HEAD_DIM
    cut = length - WINDOW
    pairs = [
        (key_hbm, key_ref),
        (sel_hbm, sel_ref),
        (value_hbm, value_ref),
        (wkey_hbm.at[cut:length, :], rim_ref.at[0:WINDOW, :]),
        (value_hbm.at[cut:length, :], rim_ref.at[WINDOW : 2 * WINDOW, :]),
        (sel_t_hbm, sel_t_ref),
        (rows_hbm, rows_ref),
    ]
    copies = [pltpu.make_async_copy(a, b, sems.at[i]) for i, (a, b) in enumerate(pairs)]
    for copy in copies:
        copy.start()
    for copy in copies[:3]:
        copy.wait()
    sel = sel_ref[...]
    ones = jnp.ones((8, length), BF16)
    place = iota((8, 128), 0)
    feats = [feature_rows(key_ref[span(h, FEAT), :], sel) for h in range(heads)]
    norms = [mm_nt(ones, feat)[0:1] for feat in feats]
    sums = [mm(feat, value_ref[:, span(h, HEAD_DIM)]) for h, feat in enumerate(feats)]
    middles = [(state[CONST : CONST + 1] * (1.0 / length)).astype(BF16).astype(F32) for state in sums]
    moved = [mm_tn(stack8(list(split(norm))), stack8([middle, middle])) for norm, middle in zip(norms, middles)]
    tiles = [jnp.where(place == 5, middle, norm_tile(norm)) for norm, middle in zip(norms, middles)]
    per = heads // CHUNKS
    for h in range(heads):
        store_state(states[h // per], h % per, sums[h] - moved[h], tiles[h])
    for copy in copies[3:]:
        copy.wait()


def add_about_body(mine_ref, theirs_ref, out_ref):
    place = iota((8, 128), 0)
    totals, tiles, moves = [], [], []
    for h in range(mine_ref.shape[0] // ROWS):
        mine = mine_ref[span(h, ROWS), :].astype(F32)
        theirs = theirs_ref[span(h, ROWS), :].astype(F32)
        mine_tile, their_tile = mine[CONST:], theirs[CONST:]
        mine_norm, their_norm = tile_norm(mine_tile), tile_norm(their_tile)
        mine_middle, their_middle = mine_tile[5:6], their_tile[5:6]
        middle = (0.5 * (mine_middle + their_middle)).astype(BF16).astype(F32)
        moves.append(outer([(mine_norm, mine_middle - middle), (their_norm, their_middle - middle)]))
        tiles.append(jnp.where(place == 5, middle, norm_tile(mine_norm + their_norm)))
        totals.append(mine + theirs)
    for h, total in enumerate(totals):
        store_state(out_ref, h, total + moves[h], tiles[h])


def add_body(mine_ref, theirs_ref, out_ref):
    for h in range(mine_ref.shape[0] // ROWS):
        total = mine_ref[span(h, ROWS), :].astype(F32) + theirs_ref[span(h, ROWS), :].astype(F32)
        store_state(out_ref, h, total, norm_tile(tile_norm(total[CONST:])))


def gather_about_body(bits, ahead, place_ref, *refs):
    parts, mine_ref, out_ref = refs[: len(bits)], refs[-2], refs[-1]
    place = iota((8, 128), 0)
    weights = [taken(place_ref, bit, False) for bit in bits] + [taken(place_ref, ahead, True)]
    totals, tiles, moves = [], [], []
    for h in range(mine_ref.shape[0] // ROWS):
        blocks = [ref[span(h, ROWS), :].astype(F32) for ref in parts + (mine_ref,)]
        middles = [block[CONST + 5 : CONST + 6] for block in blocks]
        norms = [tile_norm(block[CONST:]) * weight for block, weight in zip(blocks, weights)]
        norm = sum(norms)
        sizes = [n[:, CONST : CONST + 1] for n in norms]
        middle = sum(size * m for size, m in zip(sizes, middles)) * (1.0 / jnp.maximum(sum(sizes), 1.0))
        middle = middle.astype(BF16).astype(F32)
        moves.append(outer([(n, m - middle) for n, m in zip(norms, middles)]))
        tiles.append(jnp.where(place == 5, middle, norm_tile(norm)))
        totals.append(sum(block * weight for block, weight in zip(blocks, weights)))
    for h, total in enumerate(totals):
        store_state(out_ref, h, total + moves[h], tiles[h])


def gather_body(bits, ahead, place_ref, *refs):
    parts, mine_ref, out_ref = refs[: len(bits)], refs[-2], refs[-1]
    weights = [taken(place_ref, bit, True) for bit in bits] + [taken(place_ref, ahead, False)]
    for h in range(mine_ref.shape[0] // ROWS):
        total = sum(ref[span(h, ROWS), :].astype(F32) * weight for ref, weight in zip(parts + (mine_ref,), weights))
        store_state(out_ref, h, total, norm_tile(tile_norm(total[CONST:])))


def local_body(query_hbm, key_ref, value_ref, sel_ref, sel_t_ref, rows_ref,
               numer_ref, denom_ref, featq_ref, featq_t_ref, query_ref, sems):
    copy = pltpu.make_async_copy(query_hbm, query_ref, sems.at[0])
    copy.start()
    length = value_ref.shape[0]
    heads = value_ref.shape[1] // HEAD_DIM
    sel = sel_ref[...]
    sel_t = sel_t_ref[...]
    rows = rows_ref[...]
    keys = [key_ref[span(h, FEAT), :] for h in range(heads)]
    copy.wait()
    causal = causal_mask(length)
    lane = iota((length, 128), 1)
    queries = [query_ref[span(h, FEAT), :] for h in range(heads)]
    scores = [mm_tn(query, key) * SCORE for query, key in zip(queries, keys)]
    columns = [feature_rows(query, sel) for query in queries]
    features = [weighted_features(query, sel_t, rows) for query in queries]
    kernels = [jnp.where(causal, 1.0 + score + 0.5 * score * score, 0.0) for score in scores]
    numers = [mm(kernel.astype(BF16), value_ref[:, span(h, HEAD_DIM)]) for h, kernel in enumerate(kernels)]
    denoms = jnp.zeros((length, 128), F32)
    for h in range(heads):
        denoms = jnp.where(lane == h, lane_sum(kernels[h]), denoms)
    for h in range(heads):
        featq_t_ref[span(h, ROWS), :] = columns[h]
        featq_ref[h] = features[h]
        numer_ref[:, span(h, HEAD_DIM)] = numers[h]
    denom_ref[...] = denoms


def window_body(place_ref, wquery_hbm, wkey_hbm, cot_hbm, gain_hbm, value_ref, rim_ref,
                out_ref, weights_ref, wquery_ref, wkey_ref, cot_ref, gain_ref, sems):
    pairs = [(wquery_hbm, wquery_ref), (wkey_hbm, wkey_ref), (cot_hbm, cot_ref), (gain_hbm, gain_ref)]
    copies = [pltpu.make_async_copy(a, b, sems.at[i]) for i, (a, b) in enumerate(pairs)]
    for copy in copies:
        copy.start()
    length = wquery_ref.shape[0]
    heads = value_ref.shape[1] // HEAD_DIM
    live = place_ref[0] > 0
    row = iota((WINDOW, 2 * WINDOW), 0)
    col = iota((WINDOW, 2 * WINDOW), 1)
    inside = (col > row) & (col <= row + WINDOW)
    edge = inside & ((col >= WINDOW) | live)
    starts = range(0, length, WINDOW)
    allowed = jnp.concatenate([edge] + [inside] * (len(starts) - 1), axis=0)
    copies[0].wait()
    copies[1].wait()
    for h in range(heads):
        columns = span(h, HEAD_DIM)
        keys = jnp.concatenate([rim_ref[:WINDOW, columns], wkey_ref[:, columns]], axis=0)
        values = jnp.concatenate([rim_ref[WINDOW:, columns], value_ref[:, columns]], axis=0)
        query = wquery_ref[:, columns]
        logits = jnp.concatenate([mm_nt(query[s : s + WINDOW], keys[s : s + 2 * WINDOW]) for s in starts], axis=0)
        masked = jnp.where(allowed, logits * (1.0 / math.sqrt(HEAD_DIM)), -1e30)
        exponent = jnp.where(allowed, jnp.exp(masked - jnp.max(masked, axis=1, keepdims=True)), 0.0)
        weights = exponent * (1.0 / lane_sum(exponent))
        weights_ref[h] = weights
        narrow = weights.astype(BF16)
        out_ref[:, columns] = jnp.concatenate([mm(narrow[s : s + WINDOW], values[s : s + 2 * WINDOW]) for s in starts], axis=0)
    copies[2].wait()
    copies[3].wait()


def taken(place_ref, bit, later):
    if bit is None:
        return 1.0
    side = (place_ref[0] >> bit) & 1
    return (1 - side if later else side).astype(F32)


def merge_body(bits, chunk, place_ref, *refs):
    steps = len(bits)
    parts = refs[:steps]
    feat_ref, numer_ref, denom_ref, window_ref, gain_ref, cot_ref = refs[steps : steps + 6]
    before = refs[steps + 6 : steps + 6 + (2 if chunk else 0)]
    outs = refs[steps + 6 + len(before) :]
    merged_ref, linear_ref, inverse_ref, prefix_ref, norm_ref = outs[:5]
    length = numer_ref.shape[0]
    per = merged_ref.shape[1] // HEAD_DIM
    lane = iota((length, 128), 1)
    inverses = jnp.zeros((length, 128), F32)
    squares = before[0][...] if chunk else jnp.zeros((length, HEAD_DIM), F32)
    crosses = before[1][...] if chunk else jnp.zeros((length, HEAD_DIM), F32)
    states, norms, lefts, rights = [], [], [], []
    for h in range(per):
        state = norm = None
        left, right = [], []
        for bit, part in zip(bits, parts):
            block = part[span(h, ROWS), :].astype(F32)
            middle = block[CONST + 5 : CONST + 6]
            block = block * taken(place_ref, bit, False)
            block_norm = tile_norm(block[CONST:])
            left += list(split(block_norm))
            right += [middle, middle]
            state = block if state is None else state + block
            norm = block_norm if norm is None else norm + block_norm
        states.append(state)
        norms.append(norm)
        lefts.append(stack8(left))
        rights.append(stack8(right))
    moved = [mm_tn(left, right) for left, right in zip(lefts, rights)]
    states = [state + move for state, move in zip(states, moved)]
    parted = [halves(state) for state in states]
    wholes = [chunk * per + h for h in range(per)]
    feats = [feat_ref[whole] for whole in wholes]
    extras = [mm_nt(feat, stack8(list(split(norm)))) for feat, norm in zip(feats, norms)]
    reads = [mm(feat, high) + mm(feat, low) for feat, (high, low) in zip(feats, parted)]
    linears, mergeds = [], []
    for h, whole in enumerate(wholes):
        columns = span(whole, HEAD_DIM)
        inverse = 1.0 / (denom_ref[:, whole : whole + 1] + (extras[h][:, 0:1] + extras[h][:, 1:2]))
        inverses = jnp.where(lane == h, inverse, inverses)
        linear = (numer_ref[:, columns] + reads[h]) * inverse
        merged = linear + window_ref[:, columns]
        squares = squares + merged * merged
        scaled_cot = cot_ref[:, columns].astype(F32) * gain_ref[0:1, columns]
        crosses = crosses + scaled_cot * merged
        linears.append(linear)
        mergeds.append(merged)
    for h in range(per):
        linear_ref[:, span(h, HEAD_DIM)] = linears[h]
        merged_ref[:, span(h, HEAD_DIM)] = mergeds[h]
        prefix_ref[span(h, ROWS), :] = states[h]
        norm_ref[span(h, 8), :] = jnp.broadcast_to(norms[h], (8, ROWS))
    inverse_ref[...] = inverses
    if chunk + 1 < CHUNKS:
        outs[5][...] = squares
        outs[6][...] = crosses
    else:
        stats = jnp.where(lane == 0, lane_sum(squares), jnp.where(lane == 1, lane_sum(crosses), 0.0))
        outs[5][...] = jnp.transpose(stats)[:8]


def grad_body(width, sources, *refs):
    stats_refs, refs = refs[:sources], refs[sources:]
    merged_refs, linear_refs, inverse_refs = refs[:CHUNKS], refs[CHUNKS : 2 * CHUNKS], refs[2 * CHUNKS : 3 * CHUNKS]
    gain_ref, cot_ref, feat_t_ref = refs[3 * CHUNKS : 3 * CHUNKS + 3]
    terms = refs[3 * CHUNKS + 3 : 4 * CHUNKS + 3]
    grad_ref, cols_ref, ratios_ref = refs[4 * CHUNKS + 3 :]
    length = grad_ref.shape[0]
    heads = grad_ref.shape[1] // HEAD_DIM
    per = heads // CHUNKS
    stats = stats_refs[0][...]
    for ref in stats_refs[1:]:
        stats = stats + ref[...]
    sums = jnp.transpose(jnp.concatenate([stats, jnp.zeros((120, length), F32)], axis=0))
    mean = sums[:, 0:1] / width + 1e-6
    inv_rms = 1.0 / jnp.sqrt(mean)
    pull = sums[:, 1:2] / (width * mean)
    lane = iota((length, 128), 1)
    cols = jnp.where(lane == heads, inv_rms, 0.0)
    grads, narrows = [], []
    for h in range(heads):
        chunk, local = h // per, span(h % per, HEAD_DIM)
        inverse = inverse_refs[chunk][:, h % per : h % per + 1]
        scaled_cot = cot_ref[:, span(h, HEAD_DIM)].astype(F32) * gain_ref[0:1, span(h, HEAD_DIM)]
        grad = (scaled_cot - merged_refs[chunk][:, local] * pull) * inv_rms
        grads.append(grad)
        narrows.append((grad * inverse).astype(BF16))
        cols = jnp.where(lane == h, lane_sum(grad * linear_refs[chunk][:, local]) * inverse, cols)
    feats = [feat_t_ref[span(h, ROWS), :] for h in range(heads)]
    sums = [mm(feat, narrow) for feat, narrow in zip(feats, narrows)]
    ratios = jnp.transpose(cols)[:8]
    norms = [mm_nt(stack8(list(split(ratios[h : h + 1]))), feats[h]) for h in range(heads)]
    for h in range(heads):
        store_state(terms[h // per], h % per, sums[h], norm_tile(norms[h][0:1] + norms[h][1:2]))
        grad_ref[:, span(h, HEAD_DIM)] = grads[h]
    cols_ref[...] = cols
    ratios_ref[...] = ratios


def window_back_body(wquery_ref, wkey_ref, value_ref, rim_ref, weights_ref, grad_ref, gwq_ref, gwk_ref, gv_ref, back_ref):
    length = wquery_ref.shape[0]
    heads = value_ref.shape[1] // HEAD_DIM
    root = 1.0 / math.sqrt(HEAD_DIM)
    starts = range(0, length, WINDOW)
    pad = jnp.zeros((WINDOW, HEAD_DIM), F32)
    for h in range(heads):
        columns = span(h, HEAD_DIM)
        keys = jnp.concatenate([rim_ref[:WINDOW, columns], wkey_ref[:, columns]], axis=0)
        values = jnp.concatenate([rim_ref[WINDOW:, columns], value_ref[:, columns]], axis=0)
        grad = grad_ref[:, columns].astype(BF16)
        query = wquery_ref[:, columns]
        weights = weights_ref[h]
        narrow = weights.astype(BF16)
        dprob = jnp.concatenate([mm_nt(grad[s : s + WINDOW], values[s : s + 2 * WINDOW]) for s in starts], axis=0)
        dlogits = (weights * (dprob - lane_sum(weights * dprob))).astype(BF16)
        grads = [mm(dlogits[s : s + WINDOW], keys[s : s + 2 * WINDOW]) for s in starts]
        gwq_ref[:, columns] = (jnp.concatenate(grads, axis=0) * root).astype(BF16)
        key_parts = [mm_tn(dlogits[s : s + WINDOW], query[s : s + WINDOW]) for s in starts]
        value_parts = [mm_tn(narrow[s : s + WINDOW], grad[s : s + WINDOW]) for s in starts]
        back_ref[:WINDOW, columns] = (key_parts[0][:WINDOW] * root).astype(BF16)
        back_ref[WINDOW:, columns] = value_parts[0][:WINDOW].astype(BF16)
        key_sum = [a[WINDOW:] + b[:WINDOW] for a, b in zip(key_parts, key_parts[1:] + [pad])]
        value_sum = [a[WINDOW:] + b[:WINDOW] for a, b in zip(value_parts, value_parts[1:] + [pad])]
        gwk_ref[:, columns] = jnp.concatenate(key_sum, axis=0) * root
        gv_ref[:, columns] = jnp.concatenate(value_sum, axis=0)


def local_back_body(query_ref, key_ref, value_ref, sel_ref, sel_t_ref, rows_ref, grad_ref, cols_ref, ratios_ref, gv_in_ref, gain_ref, *refs):
    merged_refs, inverse_refs = refs[:CHUNKS], refs[CHUNKS : 2 * CHUNKS]
    prefix_refs, norm_refs = refs[2 * CHUNKS : 3 * CHUNKS], refs[3 * CHUNKS : 4 * CHUNKS]
    gq_ref, gk_ref, gv_ref, normed_ref, feat_ref = refs[4 * CHUNKS :]
    length = value_ref.shape[0]
    heads = value_ref.shape[1] // HEAD_DIM
    per = heads // CHUNKS
    sel = sel_ref[...]
    sel_t = sel_t_ref[...]
    causal = causal_mask(length)
    inv_rms = cols_ref[:, heads : heads + 1]
    queries = [query_ref[span(h, FEAT), :] for h in range(heads)]
    keys = [key_ref[span(h, FEAT), :] for h in range(heads)]
    scaled = [grad_ref[:, span(h, HEAD_DIM)] * inverse_refs[h // per][:, h % per : h % per + 1] for h in range(heads)]
    parted = [halves(x) for x in scaled]
    scores = [mm_tn(query, key) * SCORE for query, key in zip(queries, keys)]
    probs = [mm_nt(narrow, value_ref[:, span(h, HEAD_DIM)]) for h, (narrow, _) in enumerate(parted)]
    kernels = [jnp.where(causal, 1.0 + score + 0.5 * score * score, 0.0).astype(BF16) for score in scores]
    values = [mm_tn(kernel, narrow) for kernel, (narrow, _) in zip(kernels, parted)]
    dscores = [
        jnp.where(causal, (probs[h] - cols_ref[:, h : h + 1]) * (1.0 + scores[h]), 0.0).astype(BF16) for h in range(heads)
    ]
    by_query = [mm_nt(key, dscore) * SCORE for key, dscore in zip(keys, dscores)]
    by_key = [mm(query, dscore) * SCORE for query, dscore in zip(queries, dscores)]
    states = [halves(prefix_refs[h // per][span(h % per, ROWS), :]) for h in range(heads)]
    upstreams = [
        mm_nt(high, narrow) + (mm_nt(low, narrow) + mm_nt(high, rest))
        for (high, low), (narrow, rest) in zip(states, parted)
    ]
    drops = [
        outer([(norm_refs[h // per][h % per * 8 : h % per * 8 + 1, :], ratios_ref[h : h + 1, :])]) for h in range(heads)
    ]
    through = pull_back([up - drop for up, drop in zip(upstreams, drops)], queries, sel, sel_t)
    rows = rows_ref[...]
    features = [weighted_features(key, sel_t, rows) for key in keys]
    for h in range(heads):
        columns = span(h, HEAD_DIM)
        merged = merged_refs[h // per][:, span(h % per, HEAD_DIM)]
        normed_ref[:, columns] = (merged * inv_rms * gain_ref[0:1, columns]).astype(BF16)
        feat_ref[h] = features[h]
        gk_ref[span(h, FEAT), :] = by_key[h]
        gv_ref[:, columns] = gv_in_ref[:, columns] + values[h]
        gq_ref[span(h, FEAT), :] = (by_query[h] + through[h]).astype(BF16)


def final_body(bits, chunk, place_ref, *refs):
    steps = len(bits)
    parts = refs[:steps]
    key_ref, value_ref, sel_ref, sel_t_ref, feat_ref, gk_in_ref, gv_in_ref, back_ref = refs[steps : steps + 8]
    rest = refs[steps + 8 :]
    length = value_ref.shape[0]
    per = parts[0].shape[0] // ROWS
    cut = length - WINDOW
    sel = sel_ref[...]
    sel_t = sel_t_ref[...]
    ones = jnp.where(iota((8, length), 0) < 2, 1.0, 0.0).astype(BF16)
    if chunk + 1 < CHUNKS:
        gwk_in_ref, gk_ref, gv_ref, gwk_ref = rest
        gwk_ref[:cut, :] = gwk_in_ref[:cut, :].astype(BF16)
        gwk_ref[cut:, :] = (gwk_in_ref[cut:, :] + back_ref[:WINDOW, :].astype(F32)).astype(BF16)
        base = 0
    else:
        gk_before, gv_before, gk_ref, gv_ref = rest
        base = chunk * per
        gk_ref[: base * FEAT, :] = gk_before[...]
        gv_ref[:, : base * HEAD_DIM] = gv_before[...]
    wholes = [chunk * per + h for h in range(per)]
    states = []
    for h in range(per):
        state = None
        for bit, part in zip(bits, parts):
            block = part[span(h, ROWS), :].astype(F32) * taken(place_ref, bit, True)
            state = block if state is None else state + block
        states.append(state)
    parted = [halves(state) for state in states]
    values = [value_ref[:, span(whole, HEAD_DIM)] for whole in wholes]
    upstreams = [mm_nt(high, value) + mm_nt(low, value) for (high, low), value in zip(parted, values)]
    norms = [mm_tn(stack8(list(split(tile_norm(state[CONST:])))), ones) for state in states]
    reads = [mm(feat_ref[whole], high) + mm(feat_ref[whole], low) for whole, (high, low) in zip(wholes, parted)]
    keys = [key_ref[span(whole, FEAT), :] for whole in wholes]
    through = pull_back([up - norm for up, norm in zip(upstreams, norms)], keys, sel, sel_t)
    for h, whole in enumerate(wholes):
        columns = span(whole, HEAD_DIM)
        grad_value = gv_in_ref[:, columns] + reads[h]
        out_columns = span(base + h, HEAD_DIM)
        gv_ref[:cut, out_columns] = grad_value[:cut].astype(BF16)
        gv_ref[cut:, out_columns] = (grad_value[cut:] + back_ref[WINDOW:, columns].astype(F32)).astype(BF16)
        gk_ref[span(base + h, FEAT), :] = (gk_in_ref[span(whole, FEAT), :] + through[h]).astype(BF16)


def call(body, outs, *args, place=None, hbm=0, copies=0, results=(), ties=()):
    vmem = pl.BlockSpec(memory_space=pltpu.VMEM)
    specs = [pl.BlockSpec(memory_space=pltpu.HBM)] * hbm + [vmem] * (len(args) - hbm)
    args = tuple(
        pltpu.with_memory_space_constraint(a, pltpu.HBM if i < hbm else pltpu.VMEM) for i, a in enumerate(args)
    )
    if place is not None:
        specs = [pl.BlockSpec(memory_space=pltpu.SMEM)] + specs
        args = (place,) + args
    given = len(args)
    if ties:
        specs = specs + [pl.BlockSpec(memory_space=pl.ANY)] * len(ties)
        args = args + tuple(ties)
    return pl.pallas_call(
        body if not ties else lambda *refs: body(*refs[:given], *refs[given + len(ties) :]),
        out_shape=[
            jax.ShapeDtypeStruct(shape, dtype) if i in results else pltpu.VMEM(shape, dtype)
            for i, (shape, dtype) in enumerate(outs)
        ],
        in_specs=specs,
        out_specs=[vmem] * len(outs),
        scratch_shapes=[pltpu.SemaphoreType.DMA((copies,))] if copies else [],
        compiler_params=pltpu.CompilerParams(vmem_limit_bytes=VMEM_LIMIT),
    )(*args)


def exchanged(states, add, gather, place, after_first):
    count = lax.axis_size("seq")
    bits = list(range(count.bit_length() - 1))
    orders = [bits if c % 2 == 0 else bits[::-1] for c in range(len(states))]
    held = list(states)
    parts = [[] for _ in states]
    extra, ties = None, []
    for step in range(len(bits)):
        for c, order in enumerate(orders):
            pairs = [(i, i ^ (1 << order[step])) for i in range(count)]
            parts[c].append(lax.ppermute(held[c], "seq", pairs))
        if extra is None:
            extra, ties = after_first()
        if step + 1 == len(bits):
            break
        for c, order in enumerate(orders):
            tie = ties.pop(0) if c == 0 and ties else ()
            shape = [(held[c].shape, BF16)]
            if c % 2:
                counts = order[:1] + [None] * step
                (held[c],) = call(
                    lambda *refs: gather(counts, order[step + 1], *refs), shape, *parts[c], states[c], place=place, ties=tie
                )
            else:
                (held[c],) = call(add, shape, held[c], parts[c][-1], ties=tie)
    takes = [order[:1] + [None] * (len(bits) - 1) if c % 2 else order for c, order in enumerate(orders)]
    return parts, takes, extra


def shards(query, key, value, window_query, window_key, gain, cotangent):
    length, width = value.shape
    heads = width // HEAD_DIM
    per = heads // CHUNKS
    count = lax.axis_size("seq")
    full_width = HEADS * HEAD_DIM
    place = lax.axis_index("seq").astype(jnp.int32).reshape(1)
    gain_row = gain.reshape(1, width)
    query_t, key_t = query.T, key.T
    state_shape = ((per * ROWS, HEAD_DIM), BF16)
    wide = ((length, width), F32)
    wide_narrow = ((length, width), BF16)
    tables = feature_tables()

    *states, rim, key_v, value_v, sel, sel_t, rows = call(
        state_body,
        [state_shape] * CHUNKS
        + [((2 * WINDOW, width), BF16), (key_t.shape, BF16), wide_narrow]
        + [(t.shape, t.dtype) for t in tables],
        key_t, value, window_key, *tables, hbm=6, copies=7,
    )

    def early():
        rim_in = lax.ppermute(rim, "seq", [(i, (i + 1) % count) for i in range(count)])
        local = call(
            local_body,
            [wide, ((length, 128), F32), ((heads, length, ROWS), BF16), ((heads * ROWS, length), BF16), (query_t.shape, BF16)],
            query_t, key_v, value_v, sel, sel_t, rows, hbm=1, copies=1,
        )
        return (rim_in, local), [(local[1],), (rim_in,)]

    parts, takes, (rim_in, local) = exchanged(states, add_about_body, gather_about_body, place, early)
    numer, denom, featq, featq_t, query_v = local
    window_out, weights, wquery, wkey, cot, gain_v = call(
        window_body,
        [wide, ((heads, length, 2 * WINDOW), F32), wide_narrow, wide_narrow, wide_narrow, (gain_row.shape, F32)],
        window_query, window_key, cotangent, gain_row, value_v, rim_in, place=place, hbm=4, copies=4,
    )
    half = ((length, per * HEAD_DIM), F32)
    square = ((length, 128), F32)
    merged, linear, inverse, prefix, norm, before = [], [], [], [], [], []
    for c in range(CHUNKS):
        tail = [((8, length), F32)] if c + 1 == CHUNKS else [square, square]
        out = call(
            lambda *refs, c=c: merge_body(takes[c], c, *refs),
            [half, half, square, ((per * ROWS, HEAD_DIM), F32), ((per * 8, ROWS), F32)] + tail,
            *parts[c], featq, numer, denom, window_out, gain_v, cot, *before, place=place,
        )
        for held, item in zip((merged, linear, inverse, prefix, norm), out):
            held.append(item)
        before = out[5:]
    (stats,) = before
    ring = lax.axis_size("head")
    stats = [stats] + [lax.ppermute(stats, "head", [(i, i ^ s) for i in range(ring)]) for s in range(1, ring)]
    *terms, grad, cols, ratios = call(
        lambda *refs: grad_body(float(full_width), ring, *refs),
        [state_shape] * CHUNKS + [wide, square, ((8, length), F32)],
        *stats, *merged, *linear, *inverse, gain_v, cot, featq_t,
    )

    def middle():
        grad_wquery, wkey_part, value_part, back = call(
            window_back_body,
            [wide_narrow, wide, wide, ((2 * WINDOW, width), BF16)],
            wquery, wkey, value_v, rim_in, weights, grad, results=(0,),
        )
        back = lax.ppermute(back, "seq", [((i + 1) % count, i) for i in range(count)])
        return (grad_wquery, wkey_part, value_part, back), [(wkey_part,)]

    parts, takes, (grad_wquery, wkey_part, value_part, back) = exchanged(terms, add_body, gather_body, place, middle)
    grad_query, key_part, value_part, normed, featk = call(
        local_back_body,
        [(query_t.shape, BF16), (key_t.shape, F32), wide, wide_narrow, ((heads, length, ROWS), BF16)],
        query_v, key_v, value_v, sel, sel_t, rows, grad, cols, ratios, value_part, gain_v, *merged, *inverse, *prefix, *norm, results=(0, 3),
    )
    common = (key_v, value_v, sel, sel_t, featk, key_part, value_part, back)
    grad_key, grad_value, grad_wkey = call(
        lambda *refs: final_body(takes[0], 0, *refs),
        [((per * FEAT, length), BF16), ((length, per * HEAD_DIM), BF16), wide_narrow],
        *parts[0], *common, wkey_part, place=place, results=(2,),
    )
    grad_key, grad_value = call(
        lambda *refs: final_body(takes[1], 1, *refs),
        [(key_t.shape, BF16), wide_narrow],
        *parts[1], *common, grad_key, grad_value, place=place, results=(0, 1),
    )
    return (normed, grad_query.T, grad_key.T, grad_value, grad_wquery, grad_wkey)


def solution(mesh):
    placed = P("seq", "head")
    return jax.shard_map(
        shards,
        mesh=mesh,
        in_specs=(placed, placed, placed, placed, placed, P("head"), placed),
        out_specs=(placed,) * 6,
        check_vma=False,
    )
```

```python
import math

import jax
import jax.numpy as jnp
import numpy as np
from jax import lax
from jax.experimental import pallas as pl
from jax.experimental.pallas import tpu as pltpu
from jax.sharding import PartitionSpec as P

HEADS = 16
HEAD_DIM = 128
FEAT = 16
WINDOW = 64
CHUNKS = 2

QUAD = FEAT * (FEAT + 1) // 2
LINEAR = QUAD
CONST = QUAD + FEAT
ROWS = 160
ROOT_HALF = float(np.float32(math.sqrt(0.5)))
SCORE = 1.0 / math.sqrt(FEAT)

F32 = jnp.float32
BF16 = jnp.bfloat16
VMEM_LIMIT = 24 * 1024 * 1024


def feature_tables():
    first = np.zeros((ROWS, FEAT), np.float32)
    second = np.zeros((ROWS, FEAT), np.float32)
    rows = np.zeros((8, ROWS), np.float32)
    scale = FEAT ** (-0.25)
    place = 0
    for distance in range(FEAT // 2 + 1):
        for i in range(FEAT if distance < FEAT // 2 else FEAT // 2):
            first[place, i] = scale
            second[place, (i + distance) % FEAT] = scale
            rows[2, place] = ROOT_HALF * (1.0 if distance == 0 else 2.0)
            place += 1
    for i in range(FEAT):
        first[LINEAR + i, i] = scale
    rows[1, LINEAR:CONST] = 1.0
    rows[0:2, CONST] = 1.0
    rows[2, LINEAR : CONST + 1] = 1.0
    sel = np.concatenate([first, second], axis=0)
    sel_t = np.concatenate([first.T, second.T], axis=0)
    return jnp.asarray(sel, BF16), jnp.asarray(sel_t, BF16), jnp.asarray(rows)


def mm(a, b):
    return lax.dot_general(a, b, (((1,), (0,)), ((), ())), preferred_element_type=F32)


def mm_nt(a, b):
    return lax.dot_general(a, b, (((1,), (1,)), ((), ())), preferred_element_type=F32)


def mm_tn(a, b):
    return lax.dot_general(a, b, (((0,), (0,)), ((), ())), preferred_element_type=F32)


def halves(x):
    high = x.astype(BF16)
    return high, (x - high.astype(F32)).astype(BF16)


def lane_sum(x):
    return jnp.sum(x, axis=1, keepdims=True)


def span(h, size):
    return slice(h * size, (h + 1) * size)


def iota(shape, axis):
    return lax.broadcasted_iota(jnp.int32, shape, axis)


def stack8(lines):
    count = -(-len(lines) // 8) * 8
    place = iota((count, lines[0].shape[1]), 0)
    out = jnp.zeros(place.shape, F32)
    for i, line in enumerate(lines):
        out = jnp.where(place == i, line, out)
    return out.astype(BF16)


def split(x):
    high = x.astype(BF16).astype(F32)
    return high, (x - high).astype(BF16).astype(F32)


def feature_rows(inputs_t, sel):
    a = mm(sel[:ROWS], inputs_t)
    b = mm(sel[ROWS : ROWS + QUAD], inputs_t)
    tail = (iota((ROWS - CONST, inputs_t.shape[1]), 0) == 0).astype(F32)
    return jnp.concatenate([a[:QUAD] * b * ROOT_HALF, a[LINEAR:CONST], tail], axis=0).astype(BF16)


def weighted_features(inputs_t, sel_t, rows):
    a = mm_tn(inputs_t, sel_t[:FEAT]) + rows[0:1]
    b = mm_tn(inputs_t, sel_t[FEAT:]) + rows[1:2]
    return (a * b * rows[2:3]).astype(BF16)


def pull_back(upstreams, inputs_t, sel, sel_t):
    firsts = [mm(sel[:QUAD], x) for x in inputs_t]
    seconds = [mm(sel[ROWS : ROWS + QUAD], x) for x in inputs_t]
    first_t = sel_t[:FEAT, :CONST]
    second_t = sel_t[FEAT:, :QUAD]
    sides = []
    for upstream, a, b in zip(upstreams, firsts, seconds):
        squares = upstream[:FEAT] * ROOT_HALF
        others = upstream[FEAT:QUAD] * (2.0 * ROOT_HALF)
        on_first = jnp.concatenate([squares * b[:FEAT], others * b[FEAT:], upstream[LINEAR:CONST]], axis=0)
        on_second = jnp.concatenate([squares * a[:FEAT], others * a[FEAT:]], axis=0)
        sides.append(halves(on_first) + halves(on_second))
    return [
        (mm(first_t, p_high) + mm(second_t, q_high)) + (mm(first_t, p_low) + mm(second_t, q_low))
        for p_high, p_low, q_high, q_low in sides
    ]


def norm_tile(norm):
    high, low = split(norm)
    pad = jnp.zeros((1, 256 - ROWS), F32)
    row = iota((8, 128), 0)
    out = jnp.where(row == 1, high[:, :128], 0.0)
    out = jnp.where(row == 2, jnp.concatenate([high[:, 128:], pad], axis=1), out)
    out = jnp.where(row == 3, low[:, :128], out)
    return jnp.where(row == 4, jnp.concatenate([low[:, 128:], pad], axis=1), out)


def tile_norm(tile):
    return jnp.concatenate([tile[1:2] + tile[3:4], (tile[2:3] + tile[4:5])[:, : ROWS - 128]], axis=1)


def outer(pairs):
    left, right = [], []
    for a, b in pairs:
        a_high, a_low = split(a)
        b_high, b_low = split(b)
        left += [a_high, a_low, a_high]
        right += [b_high, b_high, b_low]
    return mm_tn(stack8(left), stack8(right))


def store_state(out_ref, head, state, tile):
    row = iota((8, 128), 0)
    last = jnp.where(row == 0, state[CONST:], tile)
    out_ref[span(head, ROWS), :] = jnp.concatenate([state[:CONST], last], axis=0).astype(BF16)


def causal_mask(length):
    return iota((length, length), 0) >= iota((length, length), 1)


def state_body(key_hbm, value_hbm, wkey_hbm, sel_hbm, sel_t_hbm, rows_hbm, *refs):
    states = refs[:CHUNKS]
    rim_ref, key_ref, value_ref, sel_ref, sel_t_ref, rows_ref, sems = refs[CHUNKS:]
    length, width = value_ref.shape
    heads = width // HEAD_DIM
    cut = length - WINDOW
    pairs = [
        (key_hbm, key_ref),
        (sel_hbm, sel_ref),
        (value_hbm, value_ref),
        (wkey_hbm.at[cut:length, :], rim_ref.at[0:WINDOW, :]),
        (value_hbm.at[cut:length, :], rim_ref.at[WINDOW : 2 * WINDOW, :]),
        (sel_t_hbm, sel_t_ref),
        (rows_hbm, rows_ref),
    ]
    copies = [pltpu.make_async_copy(a, b, sems.at[i]) for i, (a, b) in enumerate(pairs)]
    for copy in copies:
        copy.start()
    copies[0].wait()
    copies[1].wait()
    sel = sel_ref[...]
    ones = jnp.ones((8, length), BF16)
    place = iota((8, 128), 0)
    feats = [feature_rows(key_ref[span(h, FEAT), :], sel) for h in range(heads)]
    norms = [mm_nt(ones, feat)[0:1] for feat in feats]
    copies[2].wait()
    sums = [mm(feat, value_ref[:, span(h, HEAD_DIM)]) for h, feat in enumerate(feats)]
    middles = [(state[CONST : CONST + 1] * (1.0 / length)).astype(BF16).astype(F32) for state in sums]
    moved = [mm_tn(stack8(list(split(norm))), stack8([middle, middle])) for norm, middle in zip(norms, middles)]
    tiles = [jnp.where(place == 5, middle, norm_tile(norm)) for norm, middle in zip(norms, middles)]
    per = heads // CHUNKS
    for h in range(heads):
        store_state(states[h // per], h % per, sums[h] - moved[h], tiles[h])
    for copy in copies[3:]:
        copy.wait()


def add_about_body(mine_ref, theirs_ref, out_ref):
    place = iota((8, 128), 0)
    totals, tiles, moves = [], [], []
    for h in range(mine_ref.shape[0] // ROWS):
        mine = mine_ref[span(h, ROWS), :].astype(F32)
        theirs = theirs_ref[span(h, ROWS), :].astype(F32)
        mine_tile, their_tile = mine[CONST:], theirs[CONST:]
        mine_norm, their_norm = tile_norm(mine_tile), tile_norm(their_tile)
        mine_middle, their_middle = mine_tile[5:6], their_tile[5:6]
        middle = (0.5 * (mine_middle + their_middle)).astype(BF16).astype(F32)
        moves.append(outer([(mine_norm, mine_middle - middle), (their_norm, their_middle - middle)]))
        tiles.append(jnp.where(place == 5, middle, norm_tile(mine_norm + their_norm)))
        totals.append(mine + theirs)
    for h, total in enumerate(totals):
        store_state(out_ref, h, total + moves[h], tiles[h])


def add_body(mine_ref, theirs_ref, out_ref):
    for h in range(mine_ref.shape[0] // ROWS):
        total = mine_ref[span(h, ROWS), :].astype(F32) + theirs_ref[span(h, ROWS), :].astype(F32)
        store_state(out_ref, h, total, norm_tile(tile_norm(total[CONST:])))


def gather_about_body(bits, ahead, place_ref, *refs):
    parts, mine_ref, out_ref = refs[: len(bits)], refs[-2], refs[-1]
    place = iota((8, 128), 0)
    weights = [taken(place_ref, bit, False) for bit in bits] + [taken(place_ref, ahead, True)]
    totals, tiles, moves = [], [], []
    for h in range(mine_ref.shape[0] // ROWS):
        blocks = [ref[span(h, ROWS), :].astype(F32) for ref in parts + (mine_ref,)]
        middles = [block[CONST + 5 : CONST + 6] for block in blocks]
        norms = [tile_norm(block[CONST:]) * weight for block, weight in zip(blocks, weights)]
        norm = sum(norms)
        sizes = [n[:, CONST : CONST + 1] for n in norms]
        middle = sum(size * m for size, m in zip(sizes, middles)) * (1.0 / jnp.maximum(sum(sizes), 1.0))
        middle = middle.astype(BF16).astype(F32)
        moves.append(outer([(n, m - middle) for n, m in zip(norms, middles)]))
        tiles.append(jnp.where(place == 5, middle, norm_tile(norm)))
        totals.append(sum(block * weight for block, weight in zip(blocks, weights)))
    for h, total in enumerate(totals):
        store_state(out_ref, h, total + moves[h], tiles[h])


def gather_body(bits, ahead, place_ref, *refs):
    parts, mine_ref, out_ref = refs[: len(bits)], refs[-2], refs[-1]
    weights = [taken(place_ref, bit, True) for bit in bits] + [taken(place_ref, ahead, False)]
    for h in range(mine_ref.shape[0] // ROWS):
        total = sum(ref[span(h, ROWS), :].astype(F32) * weight for ref, weight in zip(parts + (mine_ref,), weights))
        store_state(out_ref, h, total, norm_tile(tile_norm(total[CONST:])))


def local_body(query_hbm, wquery_hbm, wkey_hbm, key_ref, value_ref, sel_ref, sel_t_ref, rows_ref,
               numer_ref, denom_ref, featq_ref, featq_t_ref, query_ref, wquery_ref, wkey_ref, sems):
    pairs = [(query_hbm, query_ref), (wquery_hbm, wquery_ref), (wkey_hbm, wkey_ref)]
    copies = [pltpu.make_async_copy(a, b, sems.at[i]) for i, (a, b) in enumerate(pairs)]
    for copy in copies:
        copy.start()
    length = value_ref.shape[0]
    heads = value_ref.shape[1] // HEAD_DIM
    sel = sel_ref[...]
    sel_t = sel_t_ref[...]
    rows = rows_ref[...]
    keys = [key_ref[span(h, FEAT), :] for h in range(heads)]
    copies[0].wait()
    causal = causal_mask(length)
    lane = iota((length, 128), 1)
    queries = [query_ref[span(h, FEAT), :] for h in range(heads)]
    scores = [mm_tn(query, key) * SCORE for query, key in zip(queries, keys)]
    columns = [feature_rows(query, sel) for query in queries]
    features = [weighted_features(query, sel_t, rows) for query in queries]
    kernels = [jnp.where(causal, 1.0 + score + 0.5 * score * score, 0.0) for score in scores]
    numers = [mm(kernel.astype(BF16), value_ref[:, span(h, HEAD_DIM)]) for h, kernel in enumerate(kernels)]
    denoms = jnp.zeros((length, 128), F32)
    for h in range(heads):
        denoms = jnp.where(lane == h, lane_sum(kernels[h]), denoms)
    for h in range(heads):
        featq_t_ref[span(h, ROWS), :] = columns[h]
        featq_ref[h] = features[h]
        numer_ref[:, span(h, HEAD_DIM)] = numers[h]
    denom_ref[...] = denoms
    copies[1].wait()
    copies[2].wait()


def window_body(place_ref, cot_hbm, gain_hbm, wquery_ref, wkey_ref, value_ref, rim_ref,
                out_ref, weights_ref, cot_ref, gain_ref, sems):
    pairs = [(cot_hbm, cot_ref), (gain_hbm, gain_ref)]
    copies = [pltpu.make_async_copy(a, b, sems.at[i]) for i, (a, b) in enumerate(pairs)]
    for copy in copies:
        copy.start()
    length = wquery_ref.shape[0]
    heads = value_ref.shape[1] // HEAD_DIM
    live = place_ref[0] > 0
    row = iota((WINDOW, 2 * WINDOW), 0)
    col = iota((WINDOW, 2 * WINDOW), 1)
    inside = (col > row) & (col <= row + WINDOW)
    edge = inside & ((col >= WINDOW) | live)
    starts = range(0, length, WINDOW)
    allowed = jnp.concatenate([edge] + [inside] * (len(starts) - 1), axis=0)
    for h in range(heads):
        columns = span(h, HEAD_DIM)
        keys = jnp.concatenate([rim_ref[:WINDOW, columns], wkey_ref[:, columns]], axis=0)
        values = jnp.concatenate([rim_ref[WINDOW:, columns], value_ref[:, columns]], axis=0)
        query = wquery_ref[:, columns]
        logits = jnp.concatenate([mm_nt(query[s : s + WINDOW], keys[s : s + 2 * WINDOW]) for s in starts], axis=0)
        masked = jnp.where(allowed, logits * (1.0 / math.sqrt(HEAD_DIM)), -1e30)
        exponent = jnp.where(allowed, jnp.exp(masked - jnp.max(masked, axis=1, keepdims=True)), 0.0)
        weights = exponent * (1.0 / lane_sum(exponent))
        weights_ref[h] = weights
        narrow = weights.astype(BF16)
        out_ref[:, columns] = jnp.concatenate([mm(narrow[s : s + WINDOW], values[s : s + 2 * WINDOW]) for s in starts], axis=0)
    copies[0].wait()
    copies[1].wait()


def taken(place_ref, bit, later):
    if bit is None:
        return 1.0
    side = (place_ref[0] >> bit) & 1
    return (1 - side if later else side).astype(F32)


def merge_body(bits, chunk, place_ref, *refs):
    steps = len(bits)
    parts = refs[:steps]
    feat_ref, numer_ref, denom_ref, window_ref, gain_ref, cot_ref = refs[steps : steps + 6]
    before = refs[steps + 6 : steps + 6 + (2 if chunk else 0)]
    outs = refs[steps + 6 + len(before) :]
    merged_ref, linear_ref, inverse_ref, prefix_ref, norm_ref = outs[:5]
    length = numer_ref.shape[0]
    per = merged_ref.shape[1] // HEAD_DIM
    lane = iota((length, 128), 1)
    inverses = jnp.zeros((length, 128), F32)
    squares = before[0][...] if chunk else jnp.zeros((length, HEAD_DIM), F32)
    crosses = before[1][...] if chunk else jnp.zeros((length, HEAD_DIM), F32)
    states, norms, lefts, rights = [], [], [], []
    for h in range(per):
        state = norm = None
        left, right = [], []
        for bit, part in zip(bits, parts):
            block = part[span(h, ROWS), :].astype(F32)
            middle = block[CONST + 5 : CONST + 6]
            block = block * taken(place_ref, bit, False)
            block_norm = tile_norm(block[CONST:])
            left += list(split(block_norm))
            right += [middle, middle]
            state = block if state is None else state + block
            norm = block_norm if norm is None else norm + block_norm
        states.append(state)
        norms.append(norm)
        lefts.append(stack8(left))
        rights.append(stack8(right))
    moved = [mm_tn(left, right) for left, right in zip(lefts, rights)]
    states = [state + move for state, move in zip(states, moved)]
    parted = [halves(state) for state in states]
    wholes = [chunk * per + h for h in range(per)]
    feats = [feat_ref[whole] for whole in wholes]
    extras = [mm_nt(feat, stack8(list(split(norm)))) for feat, norm in zip(feats, norms)]
    reads = [mm(feat, high) + mm(feat, low) for feat, (high, low) in zip(feats, parted)]
    linears, mergeds = [], []
    for h, whole in enumerate(wholes):
        columns = span(whole, HEAD_DIM)
        inverse = 1.0 / (denom_ref[:, whole : whole + 1] + (extras[h][:, 0:1] + extras[h][:, 1:2]))
        inverses = jnp.where(lane == h, inverse, inverses)
        linear = (numer_ref[:, columns] + reads[h]) * inverse
        merged = linear + window_ref[:, columns]
        squares = squares + merged * merged
        scaled_cot = cot_ref[:, columns].astype(F32) * gain_ref[0:1, columns]
        crosses = crosses + scaled_cot * merged
        linears.append(linear)
        mergeds.append(merged)
    for h in range(per):
        linear_ref[:, span(h, HEAD_DIM)] = linears[h]
        merged_ref[:, span(h, HEAD_DIM)] = mergeds[h]
        prefix_ref[span(h, ROWS), :] = states[h]
        norm_ref[span(h, 8), :] = jnp.broadcast_to(norms[h], (8, ROWS))
    inverse_ref[...] = inverses
    if chunk + 1 < CHUNKS:
        outs[5][...] = squares
        outs[6][...] = crosses
    else:
        stats = jnp.where(lane == 0, lane_sum(squares), jnp.where(lane == 1, lane_sum(crosses), 0.0))
        outs[5][...] = jnp.transpose(stats)[:8]


def grad_body(width, sources, *refs):
    stats_refs, refs = refs[:sources], refs[sources:]
    merged_refs, linear_refs, inverse_refs = refs[:CHUNKS], refs[CHUNKS : 2 * CHUNKS], refs[2 * CHUNKS : 3 * CHUNKS]
    gain_ref, cot_ref, feat_t_ref = refs[3 * CHUNKS : 3 * CHUNKS + 3]
    terms = refs[3 * CHUNKS + 3 : 4 * CHUNKS + 3]
    grad_ref, cols_ref, ratios_ref = refs[4 * CHUNKS + 3 :]
    length = grad_ref.shape[0]
    heads = grad_ref.shape[1] // HEAD_DIM
    per = heads // CHUNKS
    stats = stats_refs[0][...]
    for ref in stats_refs[1:]:
        stats = stats + ref[...]
    sums = jnp.transpose(jnp.concatenate([stats, jnp.zeros((120, length), F32)], axis=0))
    mean = sums[:, 0:1] / width + 1e-6
    inv_rms = 1.0 / jnp.sqrt(mean)
    pull = sums[:, 1:2] / (width * mean)
    lane = iota((length, 128), 1)
    cols = jnp.where(lane == heads, inv_rms, 0.0)
    grads, narrows = [], []
    for h in range(heads):
        chunk, local = h // per, span(h % per, HEAD_DIM)
        inverse = inverse_refs[chunk][:, h % per : h % per + 1]
        scaled_cot = cot_ref[:, span(h, HEAD_DIM)].astype(F32) * gain_ref[0:1, span(h, HEAD_DIM)]
        grad = (scaled_cot - merged_refs[chunk][:, local] * pull) * inv_rms
        grads.append(grad)
        narrows.append((grad * inverse).astype(BF16))
        cols = jnp.where(lane == h, lane_sum(grad * linear_refs[chunk][:, local]) * inverse, cols)
    feats = [feat_t_ref[span(h, ROWS), :] for h in range(heads)]
    sums = [mm(feat, narrow) for feat, narrow in zip(feats, narrows)]
    ratios = jnp.transpose(cols)[:8]
    norms = [mm_nt(stack8(list(split(ratios[h : h + 1]))), feats[h]) for h in range(heads)]
    for h in range(heads):
        store_state(terms[h // per], h % per, sums[h], norm_tile(norms[h][0:1] + norms[h][1:2]))
        grad_ref[:, span(h, HEAD_DIM)] = grads[h]
    cols_ref[...] = cols
    ratios_ref[...] = ratios


def window_back_body(wquery_ref, wkey_ref, value_ref, rim_ref, weights_ref, grad_ref, cols_ref, gain_ref, *refs):
    merged_refs, (gwq_ref, gwk_ref, gv_ref, back_ref, normed_ref) = refs[:CHUNKS], refs[CHUNKS:]
    length = wquery_ref.shape[0]
    heads = value_ref.shape[1] // HEAD_DIM
    root = 1.0 / math.sqrt(HEAD_DIM)
    starts = range(0, length, WINDOW)
    pad = jnp.zeros((WINDOW, HEAD_DIM), F32)
    inv_rms = cols_ref[:, heads : heads + 1]
    per = heads // CHUNKS
    for h in range(heads):
        columns = span(h, HEAD_DIM)
        merged = merged_refs[h // per][:, span(h % per, HEAD_DIM)]
        normed_ref[:, columns] = (merged * inv_rms * gain_ref[0:1, columns]).astype(BF16)
        keys = jnp.concatenate([rim_ref[:WINDOW, columns], wkey_ref[:, columns]], axis=0)
        values = jnp.concatenate([rim_ref[WINDOW:, columns], value_ref[:, columns]], axis=0)
        grad = grad_ref[:, columns].astype(BF16)
        query = wquery_ref[:, columns]
        weights = weights_ref[h]
        narrow = weights.astype(BF16)
        dprob = jnp.concatenate([mm_nt(grad[s : s + WINDOW], values[s : s + 2 * WINDOW]) for s in starts], axis=0)
        dlogits = (weights * (dprob - lane_sum(weights * dprob))).astype(BF16)
        grads = [mm(dlogits[s : s + WINDOW], keys[s : s + 2 * WINDOW]) for s in starts]
        gwq_ref[:, columns] = (jnp.concatenate(grads, axis=0) * root).astype(BF16)
        key_parts = [mm_tn(dlogits[s : s + WINDOW], query[s : s + WINDOW]) for s in starts]
        value_parts = [mm_tn(narrow[s : s + WINDOW], grad[s : s + WINDOW]) for s in starts]
        back_ref[:WINDOW, columns] = (key_parts[0][:WINDOW] * root).astype(BF16)
        back_ref[WINDOW:, columns] = value_parts[0][:WINDOW].astype(BF16)
        key_sum = [a[WINDOW:] + b[:WINDOW] for a, b in zip(key_parts, key_parts[1:] + [pad])]
        value_sum = [a[WINDOW:] + b[:WINDOW] for a, b in zip(value_parts, value_parts[1:] + [pad])]
        gwk_ref[:, columns] = jnp.concatenate(key_sum, axis=0) * root
        gv_ref[:, columns] = jnp.concatenate(value_sum, axis=0)


def local_back_body(query_ref, key_ref, value_ref, sel_ref, sel_t_ref, rows_ref, grad_ref, cols_ref, ratios_ref, gv_in_ref, *refs):
    inverse_refs, prefix_refs, norm_refs = refs[:CHUNKS], refs[CHUNKS : 2 * CHUNKS], refs[2 * CHUNKS : 3 * CHUNKS]
    gq_ref, gk_ref, gv_ref, feat_ref = refs[3 * CHUNKS :]
    length = value_ref.shape[0]
    heads = value_ref.shape[1] // HEAD_DIM
    per = heads // CHUNKS
    sel = sel_ref[...]
    sel_t = sel_t_ref[...]
    causal = causal_mask(length)
    queries = [query_ref[span(h, FEAT), :] for h in range(heads)]
    keys = [key_ref[span(h, FEAT), :] for h in range(heads)]
    scaled = [grad_ref[:, span(h, HEAD_DIM)] * inverse_refs[h // per][:, h % per : h % per + 1] for h in range(heads)]
    parted = [halves(x) for x in scaled]
    scores = [mm_tn(query, key) * SCORE for query, key in zip(queries, keys)]
    probs = [mm_nt(narrow, value_ref[:, span(h, HEAD_DIM)]) for h, (narrow, _) in enumerate(parted)]
    kernels = [jnp.where(causal, 1.0 + score + 0.5 * score * score, 0.0).astype(BF16) for score in scores]
    values = [mm_tn(kernel, narrow) for kernel, (narrow, _) in zip(kernels, parted)]
    dscores = [
        jnp.where(causal, (probs[h] - cols_ref[:, h : h + 1]) * (1.0 + scores[h]), 0.0).astype(BF16) for h in range(heads)
    ]
    by_query = [mm_nt(key, dscore) * SCORE for key, dscore in zip(keys, dscores)]
    by_key = [mm(query, dscore) * SCORE for query, dscore in zip(queries, dscores)]
    states = [halves(prefix_refs[h // per][span(h % per, ROWS), :]) for h in range(heads)]
    upstreams = [
        mm_nt(high, narrow) + (mm_nt(low, narrow) + mm_nt(high, rest))
        for (high, low), (narrow, rest) in zip(states, parted)
    ]
    drops = [
        outer([(norm_refs[h // per][h % per * 8 : h % per * 8 + 1, :], ratios_ref[h : h + 1, :])]) for h in range(heads)
    ]
    through = pull_back([up - drop for up, drop in zip(upstreams, drops)], queries, sel, sel_t)
    rows = rows_ref[...]
    features = [weighted_features(key, sel_t, rows) for key in keys]
    for h in range(heads):
        columns = span(h, HEAD_DIM)
        feat_ref[h] = features[h]
        gk_ref[span(h, FEAT), :] = by_key[h]
        gv_ref[:, columns] = gv_in_ref[:, columns] + values[h]
        gq_ref[span(h, FEAT), :] = (by_query[h] + through[h]).astype(BF16)


def final_body(bits, chunk, place_ref, *refs):
    steps = len(bits)
    parts = refs[:steps]
    key_ref, value_ref, sel_ref, sel_t_ref, feat_ref, gk_in_ref, gv_in_ref, back_ref = refs[steps : steps + 8]
    rest = refs[steps + 8 :]
    length = value_ref.shape[0]
    per = parts[0].shape[0] // ROWS
    cut = length - WINDOW
    sel = sel_ref[...]
    sel_t = sel_t_ref[...]
    ones = jnp.where(iota((8, length), 0) < 2, 1.0, 0.0).astype(BF16)
    if chunk + 1 < CHUNKS:
        gwk_in_ref, gk_ref, gv_ref, gwk_ref = rest
        gwk_ref[:cut, :] = gwk_in_ref[:cut, :].astype(BF16)
        gwk_ref[cut:, :] = (gwk_in_ref[cut:, :] + back_ref[:WINDOW, :].astype(F32)).astype(BF16)
    else:
        gwk_in, gq_in, gk_before, gv_before, gwk_out, gq_out, gk_out, gv_out, gk_ref, gv_ref, sems = rest
        own, other = chunk * per, (1 - chunk) * per
        early = [
            (gwk_in, gwk_out),
            (gv_before, gv_out.at[:, other * HEAD_DIM : (other + per) * HEAD_DIM]),
            (gk_before, gk_out.at[other * FEAT : (other + per) * FEAT, :]),
            (gq_in, gq_out),
        ]
        late = [
            (gv_ref, gv_out.at[:, own * HEAD_DIM : (own + per) * HEAD_DIM]),
            (gk_ref, gk_out.at[own * FEAT : (own + per) * FEAT, :]),
        ]
        copies = [pltpu.make_async_copy(a, b, sems.at[i]) for i, (a, b) in enumerate(early + late)]
        for copy in copies[: len(early)]:
            copy.start()
    wholes = [chunk * per + h for h in range(per)]
    states = []
    for h in range(per):
        state = None
        for bit, part in zip(bits, parts):
            block = part[span(h, ROWS), :].astype(F32) * taken(place_ref, bit, True)
            state = block if state is None else state + block
        states.append(state)
    parted = [halves(state) for state in states]
    values = [value_ref[:, span(whole, HEAD_DIM)] for whole in wholes]
    upstreams = [mm_nt(high, value) + mm_nt(low, value) for (high, low), value in zip(parted, values)]
    norms = [mm_tn(stack8(list(split(tile_norm(state[CONST:])))), ones) for state in states]
    reads = [mm(feat_ref[whole], high) + mm(feat_ref[whole], low) for whole, (high, low) in zip(wholes, parted)]
    keys = [key_ref[span(whole, FEAT), :] for whole in wholes]
    through = pull_back([up - norm for up, norm in zip(upstreams, norms)], keys, sel, sel_t)
    for h, whole in enumerate(wholes):
        columns = span(whole, HEAD_DIM)
        grad_value = gv_in_ref[:, columns] + reads[h]
        gv_ref[:cut, span(h, HEAD_DIM)] = grad_value[:cut].astype(BF16)
        gv_ref[cut:, span(h, HEAD_DIM)] = (grad_value[cut:] + back_ref[WINDOW:, columns].astype(F32)).astype(BF16)
    if chunk + 1 == CHUNKS:
        copies[-2].start()
    for h, whole in enumerate(wholes):
        gk_ref[span(h, FEAT), :] = (gk_in_ref[span(whole, FEAT), :] + through[h]).astype(BF16)
    if chunk + 1 == CHUNKS:
        copies[-1].start()
        for copy in copies:
            copy.wait()


def call(body, outs, *args, place=None, hbm=0, copies=0, results=(), ties=(), held=None):
    vmem = pl.BlockSpec(memory_space=pltpu.VMEM)
    specs = [pl.BlockSpec(memory_space=pltpu.HBM)] * hbm + [vmem] * (len(args) - hbm)
    args = tuple(
        pltpu.with_memory_space_constraint(a, pltpu.HBM if i < hbm else pltpu.VMEM) for i, a in enumerate(args)
    )
    if place is not None:
        specs = [pl.BlockSpec(memory_space=pltpu.SMEM)] + specs
        args = (place,) + args
    given = len(args)
    if ties:
        specs = specs + [pl.BlockSpec(memory_space=pl.ANY)] * len(ties)
        args = args + tuple(ties)
    return pl.pallas_call(
        body if not ties else lambda *refs: body(*refs[:given], *refs[given + len(ties) :]),
        out_shape=[
            pltpu.HBM(shape, dtype) if i in results else pltpu.VMEM(shape, dtype)
            for i, (shape, dtype) in enumerate(outs)
        ],
        in_specs=specs,
        out_specs=[
            pl.BlockSpec(memory_space=pltpu.HBM) if held and i in results else vmem for i in range(len(outs))
        ],
        scratch_shapes=[pltpu.VMEM(shape, dtype) for shape, dtype in held or ()]
        + ([pltpu.SemaphoreType.DMA((copies,))] if copies else []),
        compiler_params=pltpu.CompilerParams(vmem_limit_bytes=VMEM_LIMIT),
    )(*args)


def exchanged(states, add, gather, place, after_first):
    count = lax.axis_size("seq")
    bits = list(range(count.bit_length() - 1))
    orders = [bits if c % 2 == 0 else bits[::-1] for c in range(len(states))]
    held = list(states)
    parts = [[] for _ in states]
    extra, ties = None, {}
    for step in range(len(bits)):
        for c, order in enumerate(orders):
            pairs = [(i, i ^ (1 << order[step])) for i in range(count)]
            parts[c].append(lax.ppermute(held[c], "seq", pairs))
        if extra is None:
            extra, ties = after_first()
        if step + 1 == len(bits):
            break
        for c, order in enumerate(orders):
            tie = ties.get((step, c), ())
            shape = [(held[c].shape, BF16)]
            if c % 2:
                counts = order[:1] + [None] * step
                (held[c],) = call(
                    lambda *refs: gather(counts, order[step + 1], *refs), shape, *parts[c], states[c], place=place, ties=tie
                )
            else:
                (held[c],) = call(add, shape, held[c], parts[c][-1], ties=tie)
    takes = [order[:1] + [None] * (len(bits) - 1) if c % 2 else order for c, order in enumerate(orders)]
    return parts, takes, extra


def shards(query, key, value, window_query, window_key, gain, cotangent):
    length, width = value.shape
    heads = width // HEAD_DIM
    per = heads // CHUNKS
    count = lax.axis_size("seq")
    full_width = HEADS * HEAD_DIM
    place = lax.axis_index("seq").astype(jnp.int32).reshape(1)
    gain_row = gain.reshape(1, width)
    query_t, key_t = query.T, key.T
    state_shape = ((per * ROWS, HEAD_DIM), BF16)
    wide = ((length, width), F32)
    wide_narrow = ((length, width), BF16)
    tables = feature_tables()

    *states, rim, key_v, value_v, sel, sel_t, rows = call(
        state_body,
        [state_shape] * CHUNKS
        + [((2 * WINDOW, width), BF16), (key_t.shape, BF16), wide_narrow]
        + [(t.shape, t.dtype) for t in tables],
        key_t, value, window_key, *tables, hbm=6, copies=7,
    )

    def early():
        rim_in = lax.ppermute(rim, "seq", [(i, (i + 1) % count) for i in range(count)])
        local = call(
            local_body,
            [wide, ((length, 128), F32), ((heads, length, ROWS), BF16), ((heads * ROWS, length), BF16), (query_t.shape, BF16),
             wide_narrow, wide_narrow],
            query_t, window_query, window_key, key_v, value_v, sel, sel_t, rows, hbm=3, copies=3,
        )
        return (rim_in, local), {(0, 1): (local[1],), (1, 1): (rim_in,)}

    parts, takes, (rim_in, local) = exchanged(states, add_about_body, gather_about_body, place, early)
    numer, denom, featq, featq_t, query_v, wquery, wkey = local
    window_out, weights, cot, gain_v = call(
        window_body,
        [wide, ((heads, length, 2 * WINDOW), F32), wide_narrow, (gain_row.shape, F32)],
        cotangent, gain_row, wquery, wkey, value_v, rim_in, place=place, hbm=2, copies=2,
    )
    half = ((length, per * HEAD_DIM), F32)
    square = ((length, 128), F32)
    merged, linear, inverse, prefix, norm, before = [], [], [], [], [], []
    for c in range(CHUNKS):
        tail = [((8, length), F32)] if c + 1 == CHUNKS else [square, square]
        out = call(
            lambda *refs, c=c: merge_body(takes[c], c, *refs),
            [half, half, square, ((per * ROWS, HEAD_DIM), F32), ((per * 8, ROWS), F32)] + tail,
            *parts[c], featq, numer, denom, window_out, gain_v, cot, *before, place=place,
        )
        for held, item in zip((merged, linear, inverse, prefix, norm), out):
            held.append(item)
        before = out[5:]
    (stats,) = before
    ring = lax.axis_size("head")
    stats = [stats] + [lax.ppermute(stats, "head", [(i, i ^ s) for i in range(ring)]) for s in range(1, ring)]
    *terms, grad, cols, ratios = call(
        lambda *refs: grad_body(float(full_width), ring, *refs),
        [state_shape] * CHUNKS + [wide, square, ((8, length), F32)],
        *stats, *merged, *linear, *inverse, gain_v, cot, featq_t,
    )

    def middle():
        grad_wquery, wkey_part, value_part, back, normed = call(
            window_back_body,
            [wide_narrow, wide, wide, ((2 * WINDOW, width), BF16), wide_narrow],
            wquery, wkey, value_v, rim_in, weights, grad, cols, gain_v, *merged, results=(0, 4),
        )
        back = lax.ppermute(back, "seq", [((i + 1) % count, i) for i in range(count)])
        return (grad_wquery, wkey_part, value_part, back, normed), {(0, 0): (wkey_part,)}

    parts, takes, (grad_wquery, wkey_part, value_part, back, normed) = exchanged(terms, add_body, gather_body, place, middle)
    grad_query, key_part, value_part, featk = call(
        local_back_body,
        [(query_t.shape, BF16), (key_t.shape, F32), wide, ((heads, length, ROWS), BF16)],
        query_v, key_v, value_v, sel, sel_t, rows, grad, cols, ratios, value_part, *inverse, *prefix, *norm,
    )
    common = (key_v, value_v, sel, sel_t, featk, key_part, value_part, back)
    grad_key, grad_value, grad_wkey = call(
        lambda *refs: final_body(takes[0], 0, *refs),
        [((per * FEAT, length), BF16), ((length, per * HEAD_DIM), BF16), wide_narrow],
        *parts[0], *common, wkey_part, place=place,
    )
    grad_wkey, grad_query, grad_key, grad_value = call(
        lambda *refs: final_body(takes[1], 1, *refs),
        [wide_narrow, (query_t.shape, BF16), (key_t.shape, BF16), wide_narrow],
        *parts[1], *common, grad_wkey, grad_query, grad_key, grad_value, place=place, results=(0, 1, 2, 3), copies=6,
        held=[((per * FEAT, length), BF16), ((length, per * HEAD_DIM), BF16)],
    )
    return (normed, grad_query.T, grad_key.T, grad_value, grad_wquery, grad_wkey)


def solution(mesh):
    placed = P("seq", "head")
    return jax.shard_map(
        shards,
        mesh=mesh,
        in_specs=(placed, placed, placed, placed, placed, P("head"), placed),
        out_specs=(placed,) * 6,
        check_vma=False,
    )
```

```python
import math

import jax
import jax.numpy as jnp
import numpy as np
from jax import lax
from jax.experimental import pallas as pl
from jax.experimental.pallas import tpu as pltpu
from jax.sharding import PartitionSpec as P

HEADS = 16
HEAD_DIM = 128
FEAT = 16
WINDOW = 64
CHUNKS = 2

QUAD = FEAT * (FEAT + 1) // 2
LINEAR = QUAD
CONST = QUAD + FEAT
ROWS = 160
ROOT_HALF = float(np.float32(math.sqrt(0.5)))
SCORE = 1.0 / math.sqrt(FEAT)

F32 = jnp.float32
BF16 = jnp.bfloat16
VMEM_LIMIT = 24 * 1024 * 1024


def feature_tables():
    first = np.zeros((ROWS, FEAT), np.float32)
    second = np.zeros((ROWS, FEAT), np.float32)
    rows = np.zeros((8, ROWS), np.float32)
    scale = FEAT ** (-0.25)
    place = 0
    for distance in range(FEAT // 2 + 1):
        for i in range(FEAT if distance < FEAT // 2 else FEAT // 2):
            first[place, i] = scale
            second[place, (i + distance) % FEAT] = scale
            rows[2, place] = ROOT_HALF * (1.0 if distance == 0 else 2.0)
            place += 1
    for i in range(FEAT):
        first[LINEAR + i, i] = scale
    rows[1, LINEAR:CONST] = 1.0
    rows[0:2, CONST] = 1.0
    rows[2, LINEAR : CONST + 1] = 1.0
    sel = np.concatenate([first, second], axis=0)
    sel_t = np.concatenate([first.T, second.T], axis=0)
    return jnp.asarray(sel, BF16), jnp.asarray(sel_t, BF16), jnp.asarray(rows)


def mm(a, b):
    return lax.dot_general(a, b, (((1,), (0,)), ((), ())), preferred_element_type=F32)


def mm_nt(a, b):
    return lax.dot_general(a, b, (((1,), (1,)), ((), ())), preferred_element_type=F32)


def mm_tn(a, b):
    return lax.dot_general(a, b, (((0,), (0,)), ((), ())), preferred_element_type=F32)


def halves(x):
    high = x.astype(BF16)
    return high, (x - high.astype(F32)).astype(BF16)


def lane_sum(x):
    return jnp.sum(x, axis=1, keepdims=True)


def row_sum(x):
    ones = jnp.ones((8, x.shape[1]), BF16)
    high, low = halves(x)
    return mm_nt(ones, high) + mm_nt(ones, low)


def span(h, size):
    return slice(h * size, (h + 1) * size)


def iota(shape, axis):
    return lax.broadcasted_iota(jnp.int32, shape, axis)


def stack8(lines):
    count = -(-len(lines) // 8) * 8
    place = iota((count, lines[0].shape[1]), 0)
    out = jnp.zeros(place.shape, F32)
    for i, line in enumerate(lines):
        out = jnp.where(place == i, line, out)
    return out.astype(BF16)


def split(x):
    high = x.astype(BF16).astype(F32)
    return high, (x - high).astype(BF16).astype(F32)


def feature_rows(inputs_t, sel):
    a = mm(sel[:ROWS], inputs_t)
    b = mm(sel[ROWS : ROWS + QUAD], inputs_t)
    tail = (iota((ROWS - CONST, inputs_t.shape[1]), 0) == 0).astype(F32)
    return jnp.concatenate([a[:QUAD] * b * ROOT_HALF, a[LINEAR:CONST], tail], axis=0).astype(BF16)


def weighted_features(inputs_t, sel_t, rows):
    a = mm_tn(inputs_t, sel_t[:FEAT]) + rows[0:1]
    b = mm_tn(inputs_t, sel_t[FEAT:]) + rows[1:2]
    return (a * b * rows[2:3]).astype(BF16)


def pull_back(upstreams, inputs_t, sel, sel_t):
    firsts = [mm(sel[:QUAD], x) for x in inputs_t]
    seconds = [mm(sel[ROWS : ROWS + QUAD], x) for x in inputs_t]
    first_t = sel_t[:FEAT, :CONST]
    second_t = sel_t[FEAT:, :QUAD]
    sides = []
    for upstream, a, b in zip(upstreams, firsts, seconds):
        squares = upstream[:FEAT] * ROOT_HALF
        others = upstream[FEAT:QUAD] * (2.0 * ROOT_HALF)
        on_first = jnp.concatenate([squares * b[:FEAT], others * b[FEAT:], upstream[LINEAR:CONST]], axis=0)
        on_second = jnp.concatenate([squares * a[:FEAT], others * a[FEAT:]], axis=0)
        sides.append(halves(on_first) + halves(on_second))
    return [
        (mm(first_t, p_high) + mm(second_t, q_high)) + (mm(first_t, p_low) + mm(second_t, q_low))
        for p_high, p_low, q_high, q_low in sides
    ]


def norm_tile(norm):
    high, low = split(norm)
    pad = jnp.zeros((1, 256 - ROWS), F32)
    row = iota((8, 128), 0)
    out = jnp.where(row == 1, high[:, :128], 0.0)
    out = jnp.where(row == 2, jnp.concatenate([high[:, 128:], pad], axis=1), out)
    out = jnp.where(row == 3, low[:, :128], out)
    return jnp.where(row == 4, jnp.concatenate([low[:, 128:], pad], axis=1), out)


def tile_norm(tile):
    return jnp.concatenate([tile[1:2] + tile[3:4], (tile[2:3] + tile[4:5])[:, : ROWS - 128]], axis=1)


def outer(pairs):
    left, right = [], []
    for a, b in pairs:
        a_high, a_low = split(a)
        b_high, b_low = split(b)
        left += [a_high, a_low, a_high]
        right += [b_high, b_high, b_low]
    return mm_tn(stack8(left), stack8(right))


def store_state(out_ref, head, state, tile):
    row = iota((8, 128), 0)
    last = jnp.where(row == 0, state[CONST:], tile)
    out_ref[span(head, ROWS), :] = jnp.concatenate([state[:CONST], last], axis=0).astype(BF16)


def causal_mask(length):
    return iota((length, length), 0) >= iota((length, length), 1)


def state_body(key_hbm, value_hbm, wkey_hbm, sel_hbm, sel_t_hbm, rows_hbm, *refs):
    states = refs[:CHUNKS]
    rim_ref, key_ref, value_ref, sel_ref, sel_t_ref, rows_ref, sems = refs[CHUNKS:]
    length, width = value_ref.shape
    heads = width // HEAD_DIM
    cut = length - WINDOW
    pairs = [
        (key_hbm, key_ref),
        (sel_hbm, sel_ref),
        (value_hbm, value_ref),
        (wkey_hbm.at[cut:length, :], rim_ref.at[0:WINDOW, :]),
        (value_hbm.at[cut:length, :], rim_ref.at[WINDOW : 2 * WINDOW, :]),
        (sel_t_hbm, sel_t_ref),
        (rows_hbm, rows_ref),
    ]
    copies = [pltpu.make_async_copy(a, b, sems.at[i]) for i, (a, b) in enumerate(pairs)]
    for copy in copies:
        copy.start()
    copies[0].wait()
    copies[1].wait()
    sel = sel_ref[...]
    ones = jnp.ones((8, length), BF16)
    place = iota((8, 128), 0)
    feats = [feature_rows(key_ref[span(h, FEAT), :], sel) for h in range(heads)]
    norms = [mm_nt(ones, feat)[0:1] for feat in feats]
    copies[2].wait()
    values = [value_ref[:, span(h, HEAD_DIM)] for h in range(heads)]
    middles = [(jnp.sum(value.astype(F32), axis=0, keepdims=True) * (1.0 / length)).astype(BF16) for value in values]
    sums = [mm(feat, value) for feat, value in zip(feats, values)]
    moved = [mm(feat, jnp.broadcast_to(middle, value.shape)) for feat, middle, value in zip(feats, middles, values)]
    tiles = [jnp.where(place == 5, middle.astype(F32), norm_tile(norm)) for norm, middle in zip(norms, middles)]
    per = heads // CHUNKS
    for h in range(heads):
        store_state(states[h // per], h % per, sums[h] - moved[h], tiles[h])
    for copy in copies[3:]:
        copy.wait()


def add_about_body(mine_ref, theirs_ref, out_ref):
    place = iota((8, 128), 0)
    totals, tiles, moves = [], [], []
    for h in range(mine_ref.shape[0] // ROWS):
        mine = mine_ref[span(h, ROWS), :].astype(F32)
        theirs = theirs_ref[span(h, ROWS), :].astype(F32)
        mine_tile, their_tile = mine[CONST:], theirs[CONST:]
        mine_norm, their_norm = tile_norm(mine_tile), tile_norm(their_tile)
        mine_middle, their_middle = mine_tile[5:6], their_tile[5:6]
        middle = (0.5 * (mine_middle + their_middle)).astype(BF16).astype(F32)
        moves.append(outer([(mine_norm, mine_middle - middle), (their_norm, their_middle - middle)]))
        tiles.append(jnp.where(place == 5, middle, norm_tile(mine_norm + their_norm)))
        totals.append(mine + theirs)
    for h, total in enumerate(totals):
        store_state(out_ref, h, total + moves[h], tiles[h])


def add_body(mine_ref, theirs_ref, out_ref):
    for h in range(mine_ref.shape[0] // ROWS):
        total = mine_ref[span(h, ROWS), :].astype(F32) + theirs_ref[span(h, ROWS), :].astype(F32)
        store_state(out_ref, h, total, norm_tile(tile_norm(total[CONST:])))


def gather_about_body(bits, ahead, place_ref, *refs):
    parts, mine_ref, out_ref = refs[: len(bits)], refs[-2], refs[-1]
    place = iota((8, 128), 0)
    weights = [taken(place_ref, bit, False) for bit in bits] + [taken(place_ref, ahead, True)]
    totals, tiles, moves = [], [], []
    for h in range(mine_ref.shape[0] // ROWS):
        blocks = [ref[span(h, ROWS), :].astype(F32) for ref in parts + (mine_ref,)]
        middles = [block[CONST + 5 : CONST + 6] for block in blocks]
        norms = [tile_norm(block[CONST:]) * weight for block, weight in zip(blocks, weights)]
        norm = sum(norms)
        sizes = [n[:, CONST : CONST + 1] for n in norms]
        middle = sum(size * m for size, m in zip(sizes, middles)) * (1.0 / jnp.maximum(sum(sizes), 1.0))
        middle = middle.astype(BF16).astype(F32)
        moves.append(outer([(n, m - middle) for n, m in zip(norms, middles)]))
        tiles.append(jnp.where(place == 5, middle, norm_tile(norm)))
        totals.append(sum(block * weight for block, weight in zip(blocks, weights)))
    for h, total in enumerate(totals):
        store_state(out_ref, h, total + moves[h], tiles[h])


def gather_body(bits, ahead, place_ref, *refs):
    parts, mine_ref, out_ref = refs[: len(bits)], refs[-2], refs[-1]
    weights = [taken(place_ref, bit, True) for bit in bits] + [taken(place_ref, ahead, False)]
    for h in range(mine_ref.shape[0] // ROWS):
        total = sum(ref[span(h, ROWS), :].astype(F32) * weight for ref, weight in zip(parts + (mine_ref,), weights))
        store_state(out_ref, h, total, norm_tile(tile_norm(total[CONST:])))


def local_body(query_hbm, wquery_hbm, wkey_hbm, key_ref, value_ref, sel_ref, sel_t_ref, rows_ref,
               numer_ref, denom_ref, featq_ref, featq_t_ref, query_ref, wquery_ref, wkey_ref, sems):
    pairs = [(query_hbm, query_ref), (wquery_hbm, wquery_ref), (wkey_hbm, wkey_ref)]
    copies = [pltpu.make_async_copy(a, b, sems.at[i]) for i, (a, b) in enumerate(pairs)]
    for copy in copies:
        copy.start()
    length = value_ref.shape[0]
    heads = value_ref.shape[1] // HEAD_DIM
    sel = sel_ref[...]
    sel_t = sel_t_ref[...]
    rows = rows_ref[...]
    keys = [key_ref[span(h, FEAT), :] for h in range(heads)]
    copies[0].wait()
    causal = causal_mask(length)
    lane = iota((length, 128), 1)
    queries = [query_ref[span(h, FEAT), :] for h in range(heads)]
    scores = [mm_tn(query, key) * SCORE for query, key in zip(queries, keys)]
    columns = [feature_rows(query, sel) for query in queries]
    features = [weighted_features(query, sel_t, rows) for query in queries]
    kernels = [jnp.where(causal, 1.0 + score + 0.5 * score * score, 0.0) for score in scores]
    numers = [mm(kernel.astype(BF16), value_ref[:, span(h, HEAD_DIM)]) for h, kernel in enumerate(kernels)]
    denoms = jnp.zeros((length, 128), F32)
    for h in range(heads):
        denoms = jnp.where(lane == h, lane_sum(kernels[h]), denoms)
    for h in range(heads):
        featq_t_ref[span(h, ROWS), :] = columns[h]
        featq_ref[h] = features[h]
        numer_ref[:, span(h, HEAD_DIM)] = numers[h]
    denom_ref[...] = denoms
    copies[1].wait()
    copies[2].wait()


def window_body(place_ref, cot_hbm, gain_hbm, wquery_ref, wkey_ref, value_ref, rim_ref,
                out_ref, weights_ref, cot_ref, gain_ref, sems):
    pairs = [(cot_hbm, cot_ref), (gain_hbm, gain_ref)]
    copies = [pltpu.make_async_copy(a, b, sems.at[i]) for i, (a, b) in enumerate(pairs)]
    for copy in copies:
        copy.start()
    length = wquery_ref.shape[0]
    heads = value_ref.shape[1] // HEAD_DIM
    live = place_ref[0] > 0
    row = iota((WINDOW, 2 * WINDOW), 0)
    col = iota((WINDOW, 2 * WINDOW), 1)
    inside = (col > row) & (col <= row + WINDOW)
    edge = inside & ((col >= WINDOW) | live)
    starts = range(0, length, WINDOW)
    allowed = jnp.concatenate([edge] + [inside] * (len(starts) - 1), axis=0)
    for h in range(heads):
        columns = span(h, HEAD_DIM)
        keys = jnp.concatenate([rim_ref[:WINDOW, columns], wkey_ref[:, columns]], axis=0)
        values = jnp.concatenate([rim_ref[WINDOW:, columns], value_ref[:, columns]], axis=0)
        query = wquery_ref[:, columns]
        logits = jnp.concatenate([mm_nt(query[s : s + WINDOW], keys[s : s + 2 * WINDOW]) for s in starts], axis=0)
        masked = jnp.where(allowed, logits * (1.0 / math.sqrt(HEAD_DIM)), -1e30)
        exponent = jnp.where(allowed, jnp.exp(masked - jnp.max(masked, axis=1, keepdims=True)), 0.0)
        weights = exponent * (1.0 / lane_sum(exponent))
        weights_ref[h] = weights
        narrow = weights.astype(BF16)
        out_ref[:, columns] = jnp.concatenate([mm(narrow[s : s + WINDOW], values[s : s + 2 * WINDOW]) for s in starts], axis=0)
    copies[0].wait()
    copies[1].wait()


def taken(place_ref, bit, later):
    if bit is None:
        return 1.0
    side = (place_ref[0] >> bit) & 1
    return (1 - side if later else side).astype(F32)


def merge_body(bits, chunk, place_ref, *refs):
    steps = len(bits)
    parts = refs[:steps]
    feat_ref, numer_ref, denom_ref, window_ref, gain_ref, cot_ref = refs[steps : steps + 6]
    before = refs[steps + 6 : steps + 6 + (2 if chunk else 0)]
    outs = refs[steps + 6 + len(before) :]
    merged_ref, linear_ref, inverse_ref, prefix_ref, norm_ref = outs[:5]
    length = numer_ref.shape[0]
    per = merged_ref.shape[1] // HEAD_DIM
    lane = iota((length, 128), 1)
    inverses = jnp.zeros((length, 128), F32)
    squares = before[0][...] if chunk else jnp.zeros((length, HEAD_DIM), F32)
    crosses = before[1][...] if chunk else jnp.zeros((length, HEAD_DIM), F32)
    states, norms, lefts, rights = [], [], [], []
    for h in range(per):
        state = norm = None
        left, right = [], []
        for bit, part in zip(bits, parts):
            block = part[span(h, ROWS), :].astype(F32)
            middle = block[CONST + 5 : CONST + 6]
            block = block * taken(place_ref, bit, False)
            block_norm = tile_norm(block[CONST:])
            left += list(split(block_norm))
            right += [middle, middle]
            state = block if state is None else state + block
            norm = block_norm if norm is None else norm + block_norm
        states.append(state)
        norms.append(norm)
        lefts.append(stack8(left))
        rights.append(stack8(right))
    moved = [mm_tn(left, right) for left, right in zip(lefts, rights)]
    states = [state + move for state, move in zip(states, moved)]
    parted = [halves(state) for state in states]
    wholes = [chunk * per + h for h in range(per)]
    feats = [feat_ref[whole] for whole in wholes]
    extras = [mm_nt(feat, stack8(list(split(norm)))) for feat, norm in zip(feats, norms)]
    reads = [mm(feat, high) + mm(feat, low) for feat, (high, low) in zip(feats, parted)]
    linears, mergeds = [], []
    for h, whole in enumerate(wholes):
        columns = span(whole, HEAD_DIM)
        inverse = 1.0 / (denom_ref[:, whole : whole + 1] + (extras[h][:, 0:1] + extras[h][:, 1:2]))
        inverses = jnp.where(lane == h, inverse, inverses)
        linear = (numer_ref[:, columns] + reads[h]) * inverse
        merged = linear + window_ref[:, columns]
        squares = squares + merged * merged
        scaled_cot = cot_ref[:, columns].astype(F32) * gain_ref[0:1, columns]
        crosses = crosses + scaled_cot * merged
        linears.append(linear)
        mergeds.append(merged)
    for h in range(per):
        linear_ref[:, span(h, HEAD_DIM)] = linears[h]
        merged_ref[:, span(h, HEAD_DIM)] = mergeds[h]
        prefix_ref[span(h, ROWS), :] = states[h]
        norm_ref[span(h, 8), :] = jnp.broadcast_to(norms[h], (8, ROWS))
    inverse_ref[...] = inverses
    if chunk + 1 < CHUNKS:
        outs[5][...] = squares
        outs[6][...] = crosses
    else:
        place = iota((8, length), 0)
        outs[5][...] = jnp.where(place == 0, row_sum(squares), jnp.where(place == 1, row_sum(crosses), 0.0))


def grad_body(width, sources, *refs):
    stats_refs, refs = refs[:sources], refs[sources:]
    merged_refs, linear_refs, inverse_refs = refs[:CHUNKS], refs[CHUNKS : 2 * CHUNKS], refs[2 * CHUNKS : 3 * CHUNKS]
    gain_ref, cot_ref, feat_t_ref = refs[3 * CHUNKS : 3 * CHUNKS + 3]
    terms = refs[3 * CHUNKS + 3 : 4 * CHUNKS + 3]
    grad_ref, cols_ref, ratios_ref = refs[4 * CHUNKS + 3 :]
    length = grad_ref.shape[0]
    heads = grad_ref.shape[1] // HEAD_DIM
    per = heads // CHUNKS
    stats = stats_refs[0][...]
    for ref in stats_refs[1:]:
        stats = stats + ref[...]
    sums = jnp.transpose(jnp.concatenate([stats, jnp.zeros((120, length), F32)], axis=0))
    mean = sums[:, 0:1] / width + 1e-6
    inv_rms = 1.0 / jnp.sqrt(mean)
    pull = sums[:, 1:2] / (width * mean)
    lane = iota((length, 128), 1)
    cols_ref[...] = jnp.where(lane == heads, inv_rms, 0.0)
    grads, narrows, ratios = [], [], []
    for h in range(heads):
        chunk, local = h // per, span(h % per, HEAD_DIM)
        inverse = inverse_refs[chunk][:, h % per : h % per + 1]
        scaled_cot = cot_ref[:, span(h, HEAD_DIM)].astype(F32) * gain_ref[0:1, span(h, HEAD_DIM)]
        grad = (scaled_cot - merged_refs[chunk][:, local] * pull) * inv_rms
        grads.append(grad)
        narrows.append((grad * inverse).astype(BF16))
        ratios.append(row_sum(grad * linear_refs[chunk][:, local] * inverse)[0:1])
    feats = [feat_t_ref[span(h, ROWS), :] for h in range(heads)]
    sums = [mm(feat, narrow) for feat, narrow in zip(feats, narrows)]
    norms = [mm_nt(stack8(list(split(ratio))), feat) for ratio, feat in zip(ratios, feats)]
    for h in range(heads):
        store_state(terms[h // per], h % per, sums[h], norm_tile(norms[h][0:1] + norms[h][1:2]))
        grad_ref[:, span(h, HEAD_DIM)] = grads[h]
    ratios_ref[...] = jnp.zeros(ratios_ref.shape, F32)
    for h in range(heads):
        ratios_ref[h : h + 1, :] = ratios[h]


def window_back_body(wquery_ref, wkey_ref, value_ref, rim_ref, weights_ref, grad_ref, cols_ref, gain_ref, *refs):
    merged_refs, (gwq_ref, gwk_ref, gv_ref, back_ref, normed_ref) = refs[:CHUNKS], refs[CHUNKS:]
    length = wquery_ref.shape[0]
    heads = value_ref.shape[1] // HEAD_DIM
    root = 1.0 / math.sqrt(HEAD_DIM)
    starts = range(0, length, WINDOW)
    pad = jnp.zeros((WINDOW, HEAD_DIM), F32)
    inv_rms = cols_ref[:, heads : heads + 1]
    per = heads // CHUNKS
    for h in range(heads):
        columns = span(h, HEAD_DIM)
        merged = merged_refs[h // per][:, span(h % per, HEAD_DIM)]
        normed_ref[:, columns] = (merged * inv_rms * gain_ref[0:1, columns]).astype(BF16)
        keys = jnp.concatenate([rim_ref[:WINDOW, columns], wkey_ref[:, columns]], axis=0)
        values = jnp.concatenate([rim_ref[WINDOW:, columns], value_ref[:, columns]], axis=0)
        grad = grad_ref[:, columns].astype(BF16)
        query = wquery_ref[:, columns]
        weights = weights_ref[h]
        narrow = weights.astype(BF16)
        dprob = jnp.concatenate([mm_nt(grad[s : s + WINDOW], values[s : s + 2 * WINDOW]) for s in starts], axis=0)
        dlogits = (weights * (dprob - lane_sum(weights * dprob))).astype(BF16)
        grads = [mm(dlogits[s : s + WINDOW], keys[s : s + 2 * WINDOW]) for s in starts]
        gwq_ref[:, columns] = (jnp.concatenate(grads, axis=0) * root).astype(BF16)
        key_parts = [mm_tn(dlogits[s : s + WINDOW], query[s : s + WINDOW]) for s in starts]
        value_parts = [mm_tn(narrow[s : s + WINDOW], grad[s : s + WINDOW]) for s in starts]
        back_ref[:WINDOW, columns] = (key_parts[0][:WINDOW] * root).astype(BF16)
        back_ref[WINDOW:, columns] = value_parts[0][:WINDOW].astype(BF16)
        key_sum = [a[WINDOW:] + b[:WINDOW] for a, b in zip(key_parts, key_parts[1:] + [pad])]
        value_sum = [a[WINDOW:] + b[:WINDOW] for a, b in zip(value_parts, value_parts[1:] + [pad])]
        gwk_ref[:, columns] = jnp.concatenate(key_sum, axis=0) * root
        gv_ref[:, columns] = jnp.concatenate(value_sum, axis=0)


def local_back_body(query_ref, key_ref, value_ref, sel_ref, sel_t_ref, rows_ref, grad_ref, ratios_ref, gv_in_ref, *refs):
    inverse_refs, prefix_refs, norm_refs = refs[:CHUNKS], refs[CHUNKS : 2 * CHUNKS], refs[2 * CHUNKS : 3 * CHUNKS]
    gq_ref, gk_ref, gv_ref, feat_ref = refs[3 * CHUNKS :]
    length = value_ref.shape[0]
    heads = value_ref.shape[1] // HEAD_DIM
    per = heads // CHUNKS
    sel = sel_ref[...]
    sel_t = sel_t_ref[...]
    causal = causal_mask(length)
    queries = [query_ref[span(h, FEAT), :] for h in range(heads)]
    keys = [key_ref[span(h, FEAT), :] for h in range(heads)]
    scaled = [grad_ref[:, span(h, HEAD_DIM)] * inverse_refs[h // per][:, h % per : h % per + 1] for h in range(heads)]
    parted = [halves(x) for x in scaled]
    cols = jnp.transpose(jnp.concatenate([ratios_ref[...], jnp.zeros((120, length), F32)], axis=0))
    scores = [mm_tn(query, key) * SCORE for query, key in zip(queries, keys)]
    probs = [mm_nt(narrow, value_ref[:, span(h, HEAD_DIM)]) for h, (narrow, _) in enumerate(parted)]
    kernels = [jnp.where(causal, 1.0 + score + 0.5 * score * score, 0.0).astype(BF16) for score in scores]
    values = [mm_tn(kernel, narrow) for kernel, (narrow, _) in zip(kernels, parted)]
    dscores = [
        jnp.where(causal, (probs[h] - cols[:, h : h + 1]) * (1.0 + scores[h]), 0.0).astype(BF16) for h in range(heads)
    ]
    by_query = [mm_nt(key, dscore) * SCORE for key, dscore in zip(keys, dscores)]
    by_key = [mm(query, dscore) * SCORE for query, dscore in zip(queries, dscores)]
    states = [halves(prefix_refs[h // per][span(h % per, ROWS), :]) for h in range(heads)]
    upstreams = [
        mm_nt(high, narrow) + (mm_nt(low, narrow) + mm_nt(high, rest))
        for (high, low), (narrow, rest) in zip(states, parted)
    ]
    drops = [
        outer([(norm_refs[h // per][h % per * 8 : h % per * 8 + 1, :], ratios_ref[h : h + 1, :])]) for h in range(heads)
    ]
    through = pull_back([up - drop for up, drop in zip(upstreams, drops)], queries, sel, sel_t)
    rows = rows_ref[...]
    features = [weighted_features(key, sel_t, rows) for key in keys]
    for h in range(heads):
        columns = span(h, HEAD_DIM)
        feat_ref[h] = features[h]
        gk_ref[span(h, FEAT), :] = by_key[h]
        gv_ref[:, columns] = gv_in_ref[:, columns] + values[h]
        gq_ref[span(h, FEAT), :] = (by_query[h] + through[h]).astype(BF16)


def final_body(bits, chunk, place_ref, *refs):
    steps = len(bits)
    parts = refs[:steps]
    key_ref, value_ref, sel_ref, sel_t_ref, feat_ref, gk_in_ref, gv_in_ref, back_ref = refs[steps : steps + 8]
    rest = refs[steps + 8 :]
    length = value_ref.shape[0]
    per = parts[0].shape[0] // ROWS
    cut = length - WINDOW
    sel = sel_ref[...]
    sel_t = sel_t_ref[...]
    ones = jnp.where(iota((8, length), 0) < 2, 1.0, 0.0).astype(BF16)
    if chunk + 1 < CHUNKS:
        gwk_in_ref, gk_ref, gv_ref, gwk_ref = rest
        gwk_ref[:cut, :] = gwk_in_ref[:cut, :].astype(BF16)
        gwk_ref[cut:, :] = (gwk_in_ref[cut:, :] + back_ref[:WINDOW, :].astype(F32)).astype(BF16)
    else:
        gwk_in, gq_in, gk_before, gv_before, gwk_out, gq_out, gk_out, gv_out, gk_ref, gv_ref, sems = rest
        own, other = chunk * per, (1 - chunk) * per
        early = [
            (gwk_in, gwk_out),
            (gv_before, gv_out.at[:, other * HEAD_DIM : (other + per) * HEAD_DIM]),
            (gk_before, gk_out.at[other * FEAT : (other + per) * FEAT, :]),
            (gq_in, gq_out),
        ]
        late = [
            (gv_ref, gv_out.at[:, own * HEAD_DIM : (own + per) * HEAD_DIM]),
            (gk_ref, gk_out.at[own * FEAT : (own + per) * FEAT, :]),
        ]
        copies = [pltpu.make_async_copy(a, b, sems.at[i]) for i, (a, b) in enumerate(early + late)]
        for copy in copies[: len(early)]:
            copy.start()
    wholes = [chunk * per + h for h in range(per)]
    states = []
    for h in range(per):
        state = None
        for bit, part in zip(bits, parts):
            block = part[span(h, ROWS), :].astype(F32) * taken(place_ref, bit, True)
            state = block if state is None else state + block
        states.append(state)
    parted = [halves(state) for state in states]
    values = [value_ref[:, span(whole, HEAD_DIM)] for whole in wholes]
    upstreams = [mm_nt(high, value) + mm_nt(low, value) for (high, low), value in zip(parted, values)]
    norms = [mm_tn(stack8(list(split(tile_norm(state[CONST:])))), ones) for state in states]
    reads = [mm(feat_ref[whole], high) + mm(feat_ref[whole], low) for whole, (high, low) in zip(wholes, parted)]
    keys = [key_ref[span(whole, FEAT), :] for whole in wholes]
    through = pull_back([up - norm for up, norm in zip(upstreams, norms)], keys, sel, sel_t)
    for h, whole in enumerate(wholes):
        columns = span(whole, HEAD_DIM)
        grad_value = gv_in_ref[:, columns] + reads[h]
        gv_ref[:cut, span(h, HEAD_DIM)] = grad_value[:cut].astype(BF16)
        gv_ref[cut:, span(h, HEAD_DIM)] = (grad_value[cut:] + back_ref[WINDOW:, columns].astype(F32)).astype(BF16)
    if chunk + 1 == CHUNKS:
        copies[-2].start()
    for h, whole in enumerate(wholes):
        gk_ref[span(h, FEAT), :] = (gk_in_ref[span(whole, FEAT), :] + through[h]).astype(BF16)
    if chunk + 1 == CHUNKS:
        copies[-1].start()
        for copy in copies:
            copy.wait()


def call(body, outs, *args, place=None, hbm=0, copies=0, results=(), ties=(), held=None):
    vmem = pl.BlockSpec(memory_space=pltpu.VMEM)
    specs = [pl.BlockSpec(memory_space=pltpu.HBM)] * hbm + [vmem] * (len(args) - hbm)
    args = tuple(
        pltpu.with_memory_space_constraint(a, pltpu.HBM if i < hbm else pltpu.VMEM) for i, a in enumerate(args)
    )
    if place is not None:
        specs = [pl.BlockSpec(memory_space=pltpu.SMEM)] + specs
        args = (place,) + args
    given = len(args)
    if ties:
        specs = specs + [pl.BlockSpec(memory_space=pl.ANY)] * len(ties)
        args = args + tuple(ties)
    return pl.pallas_call(
        body if not ties else lambda *refs: body(*refs[:given], *refs[given + len(ties) :]),
        out_shape=[
            pltpu.HBM(shape, dtype) if i in results else pltpu.VMEM(shape, dtype)
            for i, (shape, dtype) in enumerate(outs)
        ],
        in_specs=specs,
        out_specs=[
            pl.BlockSpec(memory_space=pltpu.HBM) if held and i in results else vmem for i in range(len(outs))
        ],
        scratch_shapes=[pltpu.VMEM(shape, dtype) for shape, dtype in held or ()]
        + ([pltpu.SemaphoreType.DMA((copies,))] if copies else []),
        compiler_params=pltpu.CompilerParams(vmem_limit_bytes=VMEM_LIMIT),
    )(*args)


def exchanged(states, add, gather, place, after_first):
    count = lax.axis_size("seq")
    bits = list(range(count.bit_length() - 1))
    orders = [bits if c % 2 == 0 else bits[::-1] for c in range(len(states))]
    held = list(states)
    parts = [[] for _ in states]
    extra, ties = None, {}
    for step in range(len(bits)):
        for c, order in enumerate(orders):
            pairs = [(i, i ^ (1 << order[step])) for i in range(count)]
            parts[c].append(lax.ppermute(held[c], "seq", pairs))
        if extra is None:
            extra, ties = after_first()
        if step + 1 == len(bits):
            break
        for c, order in enumerate(orders):
            tie = ties.get((step, c), ())
            shape = [(held[c].shape, BF16)]
            if c % 2:
                counts = order[:1] + [None] * step
                (held[c],) = call(
                    lambda *refs: gather(counts, order[step + 1], *refs), shape, *parts[c], states[c], place=place, ties=tie
                )
            else:
                (held[c],) = call(add, shape, held[c], parts[c][-1], ties=tie)
    takes = [order[:1] + [None] * (len(bits) - 1) if c % 2 else order for c, order in enumerate(orders)]
    return parts, takes, extra


def shards(query, key, value, window_query, window_key, gain, cotangent):
    length, width = value.shape
    heads = width // HEAD_DIM
    per = heads // CHUNKS
    count = lax.axis_size("seq")
    full_width = HEADS * HEAD_DIM
    place = lax.axis_index("seq").astype(jnp.int32).reshape(1)
    gain_row = gain.reshape(1, width)
    query_t, key_t = query.T, key.T
    state_shape = ((per * ROWS, HEAD_DIM), BF16)
    wide = ((length, width), F32)
    wide_narrow = ((length, width), BF16)
    tables = feature_tables()

    *states, rim, key_v, value_v, sel, sel_t, rows = call(
        state_body,
        [state_shape] * CHUNKS
        + [((2 * WINDOW, width), BF16), (key_t.shape, BF16), wide_narrow]
        + [(t.shape, t.dtype) for t in tables],
        key_t, value, window_key, *tables, hbm=6, copies=7,
    )

    def early():
        rim_in = lax.ppermute(rim, "seq", [(i, (i + 1) % count) for i in range(count)])
        local = call(
            local_body,
            [wide, ((length, 128), F32), ((heads, length, ROWS), BF16), ((heads * ROWS, length), BF16), (query_t.shape, BF16),
             wide_narrow, wide_narrow],
            query_t, window_query, window_key, key_v, value_v, sel, sel_t, rows, hbm=3, copies=3,
        )
        return (rim_in, local), {(0, 1): (local[1],), (1, 1): (rim_in,)}

    parts, takes, (rim_in, local) = exchanged(states, add_about_body, gather_about_body, place, early)
    numer, denom, featq, featq_t, query_v, wquery, wkey = local
    window_out, weights, cot, gain_v = call(
        window_body,
        [wide, ((heads, length, 2 * WINDOW), F32), wide_narrow, (gain_row.shape, F32)],
        cotangent, gain_row, wquery, wkey, value_v, rim_in, place=place, hbm=2, copies=2,
    )
    half = ((length, per * HEAD_DIM), F32)
    square = ((length, 128), F32)
    merged, linear, inverse, prefix, norm, before = [], [], [], [], [], []
    for c in range(CHUNKS):
        tail = [((8, length), F32)] if c + 1 == CHUNKS else [square, square]
        out = call(
            lambda *refs, c=c: merge_body(takes[c], c, *refs),
            [half, half, square, ((per * ROWS, HEAD_DIM), F32), ((per * 8, ROWS), F32)] + tail,
            *parts[c], featq, numer, denom, window_out, gain_v, cot, *before, place=place,
        )
        for held, item in zip((merged, linear, inverse, prefix, norm), out):
            held.append(item)
        before = out[5:]
    (stats,) = before
    ring = lax.axis_size("head")
    stats = [stats] + [lax.ppermute(stats, "head", [(i, i ^ s) for i in range(ring)]) for s in range(1, ring)]
    *terms, grad, cols, ratios = call(
        lambda *refs: grad_body(float(full_width), ring, *refs),
        [state_shape] * CHUNKS + [wide, square, ((8, length), F32)],
        *stats, *merged, *linear, *inverse, gain_v, cot, featq_t,
    )

    def middle():
        grad_wquery, wkey_part, value_part, back, normed = call(
            window_back_body,
            [wide_narrow, wide, wide, ((2 * WINDOW, width), BF16), wide_narrow],
            wquery, wkey, value_v, rim_in, weights, grad, cols, gain_v, *merged, results=(0, 4),
        )
        back = lax.ppermute(back, "seq", [((i + 1) % count, i) for i in range(count)])
        return (grad_wquery, wkey_part, value_part, back, normed), {(0, 0): (wkey_part,)}

    parts, takes, (grad_wquery, wkey_part, value_part, back, normed) = exchanged(terms, add_body, gather_body, place, middle)
    grad_query, key_part, value_part, featk = call(
        local_back_body,
        [(query_t.shape, BF16), (key_t.shape, F32), wide, ((heads, length, ROWS), BF16)],
        query_v, key_v, value_v, sel, sel_t, rows, grad, ratios, value_part, *inverse, *prefix, *norm,
    )
    common = (key_v, value_v, sel, sel_t, featk, key_part, value_part, back)
    grad_key, grad_value, grad_wkey = call(
        lambda *refs: final_body(takes[0], 0, *refs),
        [((per * FEAT, length), BF16), ((length, per * HEAD_DIM), BF16), wide_narrow],
        *parts[0], *common, wkey_part, place=place,
    )
    grad_wkey, grad_query, grad_key, grad_value = call(
        lambda *refs: final_body(takes[1], 1, *refs),
        [wide_narrow, (query_t.shape, BF16), (key_t.shape, BF16), wide_narrow],
        *parts[1], *common, grad_wkey, grad_query, grad_key, grad_value, place=place, results=(0, 1, 2, 3), copies=6,
        held=[((per * FEAT, length), BF16), ((length, per * HEAD_DIM), BF16)],
    )
    return (normed, grad_query.T, grad_key.T, grad_value, grad_wquery, grad_wkey)


def solution(mesh):
    placed = P("seq", "head")
    return jax.shard_map(
        shards,
        mesh=mesh,
        in_specs=(placed, placed, placed, placed, placed, P("head"), placed),
        out_specs=(placed,) * 6,
        check_vma=False,
    )
```

```python
import math

import jax
import jax.numpy as jnp
import numpy as np
from jax import lax
from jax.experimental import pallas as pl
from jax.experimental.pallas import tpu as pltpu
from jax.sharding import PartitionSpec as P

HEADS = 16
HEAD_DIM = 128
FEAT = 16
WINDOW = 64
CHUNKS = 2

QUAD = FEAT * (FEAT + 1) // 2
LINEAR = QUAD
CONST = QUAD + FEAT
ROWS = 160
ROOT_HALF = float(np.float32(math.sqrt(0.5)))
SCORE = 1.0 / math.sqrt(FEAT)

F32 = jnp.float32
BF16 = jnp.bfloat16
VMEM_LIMIT = 24 * 1024 * 1024


def feature_tables():
    first = np.zeros((ROWS, FEAT), np.float32)
    second = np.zeros((ROWS, FEAT), np.float32)
    rows = np.zeros((8, ROWS), np.float32)
    scale = FEAT ** (-0.25)
    place = 0
    for distance in range(FEAT // 2 + 1):
        for i in range(FEAT if distance < FEAT // 2 else FEAT // 2):
            first[place, i] = scale
            second[place, (i + distance) % FEAT] = scale
            rows[2, place] = ROOT_HALF * (1.0 if distance == 0 else 2.0)
            place += 1
    for i in range(FEAT):
        first[LINEAR + i, i] = scale
    rows[1, LINEAR:CONST] = 1.0
    rows[0:2, CONST] = 1.0
    rows[2, LINEAR : CONST + 1] = 1.0
    sel = np.concatenate([first, second], axis=0)
    sel_t = np.concatenate([first.T, second.T], axis=0)
    return jnp.asarray(sel, BF16), jnp.asarray(sel_t, BF16), jnp.asarray(rows)


def mm(a, b):
    return lax.dot_general(a, b, (((1,), (0,)), ((), ())), preferred_element_type=F32)


def mm_nt(a, b):
    return lax.dot_general(a, b, (((1,), (1,)), ((), ())), preferred_element_type=F32)


def mm_tn(a, b):
    return lax.dot_general(a, b, (((0,), (0,)), ((), ())), preferred_element_type=F32)


def halves(x):
    high = x.astype(BF16)
    return high, (x - high.astype(F32)).astype(BF16)


def lane_sum(x):
    return jnp.sum(x, axis=1, keepdims=True)


def row_sum(x):
    ones = jnp.ones((8, x.shape[1]), BF16)
    high, low = halves(x)
    return mm_nt(ones, high) + mm_nt(ones, low)


def span(h, size):
    return slice(h * size, (h + 1) * size)


def iota(shape, axis):
    return lax.broadcasted_iota(jnp.int32, shape, axis)


def stack8(lines):
    count = -(-len(lines) // 8) * 8
    place = iota((count, lines[0].shape[1]), 0)
    out = jnp.zeros(place.shape, F32)
    for i, line in enumerate(lines):
        out = jnp.where(place == i, line, out)
    return out.astype(BF16)


def split(x):
    high = x.astype(BF16).astype(F32)
    return high, (x - high).astype(BF16).astype(F32)


def feature_rows(inputs_t, sel):
    a = mm(sel[:ROWS], inputs_t)
    b = mm(sel[ROWS : ROWS + QUAD], inputs_t)
    tail = (iota((ROWS - CONST, inputs_t.shape[1]), 0) == 0).astype(F32)
    return jnp.concatenate([a[:QUAD] * b * ROOT_HALF, a[LINEAR:CONST], tail], axis=0).astype(BF16)


def weighted_features(inputs_t, sel_t, rows):
    a = mm_tn(inputs_t, sel_t[:FEAT]) + rows[0:1]
    b = mm_tn(inputs_t, sel_t[FEAT:]) + rows[1:2]
    return (a * b * rows[2:3]).astype(BF16)


def pull_back(upstreams, inputs_t, sel, sel_t):
    firsts = [mm(sel[:QUAD], x) for x in inputs_t]
    seconds = [mm(sel[ROWS : ROWS + QUAD], x) for x in inputs_t]
    first_t = sel_t[:FEAT, :CONST]
    second_t = sel_t[FEAT:, :QUAD]
    sides = []
    for upstream, a, b in zip(upstreams, firsts, seconds):
        squares = upstream[:FEAT] * ROOT_HALF
        others = upstream[FEAT:QUAD] * (2.0 * ROOT_HALF)
        on_first = jnp.concatenate([squares * b[:FEAT], others * b[FEAT:], upstream[LINEAR:CONST]], axis=0)
        on_second = jnp.concatenate([squares * a[:FEAT], others * a[FEAT:]], axis=0)
        sides.append(halves(on_first) + halves(on_second))
    return [
        (mm(first_t, p_high) + mm(second_t, q_high)) + (mm(first_t, p_low) + mm(second_t, q_low))
        for p_high, p_low, q_high, q_low in sides
    ]


def norm_tile(norm):
    high, low = split(norm)
    pad = jnp.zeros((1, 256 - ROWS), F32)
    row = iota((8, 128), 0)
    out = jnp.where(row == 1, high[:, :128], 0.0)
    out = jnp.where(row == 2, jnp.concatenate([high[:, 128:], pad], axis=1), out)
    out = jnp.where(row == 3, low[:, :128], out)
    return jnp.where(row == 4, jnp.concatenate([low[:, 128:], pad], axis=1), out)


def tile_norm(tile):
    return jnp.concatenate([tile[1:2] + tile[3:4], (tile[2:3] + tile[4:5])[:, : ROWS - 128]], axis=1)


def outer(pairs):
    left, right = [], []
    for a, b in pairs:
        a_high, a_low = split(a)
        b_high, b_low = split(b)
        left += [a_high, a_low, a_high]
        right += [b_high, b_high, b_low]
    return mm_tn(stack8(left), stack8(right))


def store_state(out_ref, head, state, tile):
    row = iota((8, 128), 0)
    last = jnp.where(row == 0, state[CONST:], tile)
    out_ref[span(head, ROWS), :] = jnp.concatenate([state[:CONST], last], axis=0).astype(BF16)


def causal_mask(length):
    return iota((length, length), 0) >= iota((length, length), 1)


def state_body(key_hbm, value_hbm, wkey_hbm, sel_hbm, sel_t_hbm, rows_hbm, *refs):
    states = refs[:CHUNKS]
    rim_ref, key_ref, value_ref, sel_ref, sel_t_ref, rows_ref, sems = refs[CHUNKS:]
    length, width = value_ref.shape
    heads = width // HEAD_DIM
    cut = length - WINDOW
    pairs = [
        (key_hbm, key_ref),
        (sel_hbm, sel_ref),
        (value_hbm, value_ref),
        (wkey_hbm.at[cut:length, :], rim_ref.at[0:WINDOW, :]),
        (value_hbm.at[cut:length, :], rim_ref.at[WINDOW : 2 * WINDOW, :]),
        (sel_t_hbm, sel_t_ref),
        (rows_hbm, rows_ref),
    ]
    copies = [pltpu.make_async_copy(a, b, sems.at[i]) for i, (a, b) in enumerate(pairs)]
    for copy in copies:
        copy.start()
    copies[0].wait()
    copies[1].wait()
    sel = sel_ref[...]
    ones = jnp.ones((8, length), BF16)
    place = iota((8, 128), 0)
    feats = [feature_rows(key_ref[span(h, FEAT), :], sel) for h in range(heads)]
    norms = [mm_nt(ones, feat)[0:1] for feat in feats]
    copies[2].wait()
    values = [value_ref[:, span(h, HEAD_DIM)] for h in range(heads)]
    middles = [(jnp.sum(value.astype(F32), axis=0, keepdims=True) * (1.0 / length)).astype(BF16) for value in values]
    sums = [mm(feat, value) for feat, value in zip(feats, values)]
    moved = [mm(feat, jnp.broadcast_to(middle, value.shape)) for feat, middle, value in zip(feats, middles, values)]
    tiles = [jnp.where(place == 5, middle.astype(F32), norm_tile(norm)) for norm, middle in zip(norms, middles)]
    per = heads // CHUNKS
    for h in range(heads):
        store_state(states[h // per], h % per, sums[h] - moved[h], tiles[h])
    for copy in copies[3:]:
        copy.wait()


def add_about_body(mine_ref, theirs_ref, out_ref):
    place = iota((8, 128), 0)
    totals, tiles, moves = [], [], []
    for h in range(mine_ref.shape[0] // ROWS):
        mine = mine_ref[span(h, ROWS), :].astype(F32)
        theirs = theirs_ref[span(h, ROWS), :].astype(F32)
        mine_tile, their_tile = mine[CONST:], theirs[CONST:]
        mine_norm, their_norm = tile_norm(mine_tile), tile_norm(their_tile)
        mine_middle, their_middle = mine_tile[5:6], their_tile[5:6]
        middle = (0.5 * (mine_middle + their_middle)).astype(BF16).astype(F32)
        moves.append(outer([(mine_norm, mine_middle - middle), (their_norm, their_middle - middle)]))
        tiles.append(jnp.where(place == 5, middle, norm_tile(mine_norm + their_norm)))
        totals.append(mine + theirs)
    for h, total in enumerate(totals):
        store_state(out_ref, h, total + moves[h], tiles[h])


def add_body(mine_ref, theirs_ref, out_ref):
    for h in range(mine_ref.shape[0] // ROWS):
        total = mine_ref[span(h, ROWS), :].astype(F32) + theirs_ref[span(h, ROWS), :].astype(F32)
        store_state(out_ref, h, total, norm_tile(tile_norm(total[CONST:])))


def gather_about_body(bits, ahead, place_ref, *refs):
    parts, mine_ref, out_ref = refs[: len(bits)], refs[-2], refs[-1]
    place = iota((8, 128), 0)
    weights = [taken(place_ref, bit, False) for bit in bits] + [taken(place_ref, ahead, True)]
    totals, tiles, moves = [], [], []
    for h in range(mine_ref.shape[0] // ROWS):
        blocks = [ref[span(h, ROWS), :].astype(F32) for ref in parts + (mine_ref,)]
        middles = [block[CONST + 5 : CONST + 6] for block in blocks]
        norms = [tile_norm(block[CONST:]) * weight for block, weight in zip(blocks, weights)]
        norm = sum(norms)
        sizes = [n[:, CONST : CONST + 1] for n in norms]
        middle = sum(size * m for size, m in zip(sizes, middles)) * (1.0 / jnp.maximum(sum(sizes), 1.0))
        middle = middle.astype(BF16).astype(F32)
        moves.append(outer([(n, m - middle) for n, m in zip(norms, middles)]))
        tiles.append(jnp.where(place == 5, middle, norm_tile(norm)))
        totals.append(sum(block * weight for block, weight in zip(blocks, weights)))
    for h, total in enumerate(totals):
        store_state(out_ref, h, total + moves[h], tiles[h])


def gather_body(bits, ahead, place_ref, *refs):
    parts, mine_ref, out_ref = refs[: len(bits)], refs[-2], refs[-1]
    weights = [taken(place_ref, bit, True) for bit in bits] + [taken(place_ref, ahead, False)]
    for h in range(mine_ref.shape[0] // ROWS):
        total = sum(ref[span(h, ROWS), :].astype(F32) * weight for ref, weight in zip(parts + (mine_ref,), weights))
        store_state(out_ref, h, total, norm_tile(tile_norm(total[CONST:])))


def local_body(query_hbm, wquery_hbm, wkey_hbm, key_ref, value_ref, sel_ref, sel_t_ref, rows_ref,
               numer_ref, denom_ref, featq_ref, featq_t_ref, query_ref, wquery_ref, wkey_ref, sems):
    pairs = [(query_hbm, query_ref), (wquery_hbm, wquery_ref), (wkey_hbm, wkey_ref)]
    copies = [pltpu.make_async_copy(a, b, sems.at[i]) for i, (a, b) in enumerate(pairs)]
    for copy in copies:
        copy.start()
    length = value_ref.shape[0]
    heads = value_ref.shape[1] // HEAD_DIM
    sel = sel_ref[...]
    sel_t = sel_t_ref[...]
    rows = rows_ref[...]
    keys = [key_ref[span(h, FEAT), :] for h in range(heads)]
    copies[0].wait()
    causal = causal_mask(length)
    lane = iota((length, 128), 1)
    queries = [query_ref[span(h, FEAT), :] for h in range(heads)]
    scores = [mm_tn(query, key) * SCORE for query, key in zip(queries, keys)]
    columns = [feature_rows(query, sel) for query in queries]
    features = [weighted_features(query, sel_t, rows) for query in queries]
    kernels = [jnp.where(causal, 1.0 + score + 0.5 * score * score, 0.0) for score in scores]
    numers = [mm(kernel.astype(BF16), value_ref[:, span(h, HEAD_DIM)]) for h, kernel in enumerate(kernels)]
    denoms = jnp.zeros((length, 128), F32)
    for h in range(heads):
        denoms = jnp.where(lane == h, lane_sum(kernels[h]), denoms)
    for h in range(heads):
        featq_t_ref[span(h, ROWS), :] = columns[h]
        featq_ref[h] = features[h]
        numer_ref[:, span(h, HEAD_DIM)] = numers[h]
    denom_ref[...] = denoms
    copies[1].wait()
    copies[2].wait()


def window_body(place_ref, cot_hbm, gain_hbm, wquery_ref, wkey_ref, value_ref, rim_ref,
                out_ref, weights_ref, cot_ref, gain_ref, sems):
    pairs = [(cot_hbm, cot_ref), (gain_hbm, gain_ref)]
    copies = [pltpu.make_async_copy(a, b, sems.at[i]) for i, (a, b) in enumerate(pairs)]
    for copy in copies:
        copy.start()
    length = wquery_ref.shape[0]
    heads = value_ref.shape[1] // HEAD_DIM
    live = place_ref[0] > 0
    row = iota((WINDOW, 2 * WINDOW), 0)
    col = iota((WINDOW, 2 * WINDOW), 1)
    inside = (col > row) & (col <= row + WINDOW)
    edge = inside & ((col >= WINDOW) | live)
    starts = range(0, length, WINDOW)
    allowed = jnp.concatenate([edge] + [inside] * (len(starts) - 1), axis=0)
    for h in range(heads):
        columns = span(h, HEAD_DIM)
        keys = jnp.concatenate([rim_ref[:WINDOW, columns], wkey_ref[:, columns]], axis=0)
        values = jnp.concatenate([rim_ref[WINDOW:, columns], value_ref[:, columns]], axis=0)
        query = wquery_ref[:, columns]
        logits = jnp.concatenate([mm_nt(query[s : s + WINDOW], keys[s : s + 2 * WINDOW]) for s in starts], axis=0)
        masked = jnp.where(allowed, logits * (1.0 / math.sqrt(HEAD_DIM)), -1e30)
        exponent = jnp.where(allowed, jnp.exp(masked - jnp.max(masked, axis=1, keepdims=True)), 0.0)
        weights = exponent * (1.0 / lane_sum(exponent))
        weights_ref[h] = weights
        narrow = weights.astype(BF16)
        out_ref[:, columns] = jnp.concatenate([mm(narrow[s : s + WINDOW], values[s : s + 2 * WINDOW]) for s in starts], axis=0)
    copies[0].wait()
    copies[1].wait()


def taken(place_ref, bit, later):
    if bit is None:
        return 1.0
    side = (place_ref[0] >> bit) & 1
    return (1 - side if later else side).astype(F32)


def merge_body(bits, chunk, place_ref, *refs):
    steps = len(bits)
    parts = refs[:steps]
    feat_ref, numer_ref, denom_ref, window_ref, gain_ref, cot_ref = refs[steps : steps + 6]
    before = refs[steps + 6 : steps + 6 + (2 if chunk else 0)]
    outs = refs[steps + 6 + len(before) :]
    merged_ref, linear_ref, inverse_ref, prefix_ref, norm_ref = outs[:5]
    length = numer_ref.shape[0]
    per = merged_ref.shape[1] // HEAD_DIM
    lane = iota((length, 128), 1)
    inverses = jnp.zeros((length, 128), F32)
    squares = before[0][...] if chunk else jnp.zeros((length, HEAD_DIM), F32)
    crosses = before[1][...] if chunk else jnp.zeros((length, HEAD_DIM), F32)
    states, norms, lefts, rights = [], [], [], []
    for h in range(per):
        state = norm = None
        left, right = [], []
        for bit, part in zip(bits, parts):
            block = part[span(h, ROWS), :].astype(F32)
            middle = block[CONST + 5 : CONST + 6]
            block = block * taken(place_ref, bit, False)
            block_norm = tile_norm(block[CONST:])
            left += list(split(block_norm))
            right += [middle, middle]
            state = block if state is None else state + block
            norm = block_norm if norm is None else norm + block_norm
        states.append(state)
        norms.append(norm)
        lefts.append(stack8(left))
        rights.append(stack8(right))
    moved = [mm_tn(left, right) for left, right in zip(lefts, rights)]
    states = [state + move for state, move in zip(states, moved)]
    parted = [halves(state) for state in states]
    wholes = [chunk * per + h for h in range(per)]
    feats = [feat_ref[whole] for whole in wholes]
    extras = [mm_nt(feat, stack8(list(split(norm)))) for feat, norm in zip(feats, norms)]
    reads = [mm(feat, high) + mm(feat, low) for feat, (high, low) in zip(feats, parted)]
    linears, mergeds = [], []
    for h, whole in enumerate(wholes):
        columns = span(whole, HEAD_DIM)
        inverse = 1.0 / (denom_ref[:, whole : whole + 1] + (extras[h][:, 0:1] + extras[h][:, 1:2]))
        inverses = jnp.where(lane == h, inverse, inverses)
        linear = (numer_ref[:, columns] + reads[h]) * inverse
        merged = linear + window_ref[:, columns]
        squares = squares + merged * merged
        scaled_cot = cot_ref[:, columns].astype(F32) * gain_ref[0:1, columns]
        crosses = crosses + scaled_cot * merged
        linears.append(linear)
        mergeds.append(merged)
    for h in range(per):
        linear_ref[:, span(h, HEAD_DIM)] = linears[h]
        merged_ref[:, span(h, HEAD_DIM)] = mergeds[h]
        prefix_ref[span(h, ROWS), :] = states[h]
        norm_ref[span(h, 8), :] = jnp.broadcast_to(norms[h], (8, ROWS))
    inverse_ref[...] = inverses
    if chunk + 1 < CHUNKS:
        outs[5][...] = squares
        outs[6][...] = crosses
    else:
        place = iota((8, length), 0)
        outs[5][...] = jnp.where(place == 0, row_sum(squares), jnp.where(place == 1, row_sum(crosses), 0.0))


def grad_body(width, sources, *refs):
    stats_refs, refs = refs[:sources], refs[sources:]
    merged_refs, linear_refs, inverse_refs = refs[:CHUNKS], refs[CHUNKS : 2 * CHUNKS], refs[2 * CHUNKS : 3 * CHUNKS]
    gain_ref, cot_ref, feat_t_ref = refs[3 * CHUNKS : 3 * CHUNKS + 3]
    terms = refs[3 * CHUNKS + 3 : 4 * CHUNKS + 3]
    grad_ref, cols_ref, ratios_ref = refs[4 * CHUNKS + 3 :]
    length = grad_ref.shape[0]
    heads = grad_ref.shape[1] // HEAD_DIM
    per = heads // CHUNKS
    stats = stats_refs[0][...]
    for ref in stats_refs[1:]:
        stats = stats + ref[...]
    sums = jnp.transpose(jnp.concatenate([stats, jnp.zeros((120, length), F32)], axis=0))
    mean = sums[:, 0:1] / width + 1e-6
    inv_rms = 1.0 / jnp.sqrt(mean)
    pull = sums[:, 1:2] / (width * mean)
    lane = iota((length, 128), 1)
    cols_ref[...] = jnp.where(lane == heads, inv_rms, 0.0)
    grads, narrows, ratios = [], [], []
    for h in range(heads):
        chunk, local = h // per, span(h % per, HEAD_DIM)
        inverse = inverse_refs[chunk][:, h % per : h % per + 1]
        scaled_cot = cot_ref[:, span(h, HEAD_DIM)].astype(F32) * gain_ref[0:1, span(h, HEAD_DIM)]
        grad = (scaled_cot - merged_refs[chunk][:, local] * pull) * inv_rms
        grads.append(grad)
        narrows.append((grad * inverse).astype(BF16))
        ratios.append(row_sum(grad * linear_refs[chunk][:, local] * inverse)[0:1])
    feats = [feat_t_ref[span(h, ROWS), :] for h in range(heads)]
    sums = [mm(feat, narrow) for feat, narrow in zip(feats, narrows)]
    norms = [mm_nt(stack8(list(split(ratio))), feat) for ratio, feat in zip(ratios, feats)]
    for h in range(heads):
        store_state(terms[h // per], h % per, sums[h], norm_tile(norms[h][0:1] + norms[h][1:2]))
        grad_ref[:, span(h, HEAD_DIM)] = grads[h]
    ratios_ref[...] = jnp.zeros(ratios_ref.shape, F32)
    for h in range(heads):
        ratios_ref[h : h + 1, :] = ratios[h]


def window_back_body(wquery_ref, wkey_ref, value_ref, rim_ref, weights_ref, grad_ref, cols_ref, gain_ref, *refs):
    merged_refs, (gwq_ref, gwk_ref, gv_ref, back_ref, normed_ref) = refs[:CHUNKS], refs[CHUNKS:]
    length = wquery_ref.shape[0]
    heads = value_ref.shape[1] // HEAD_DIM
    root = 1.0 / math.sqrt(HEAD_DIM)
    starts = range(0, length, WINDOW)
    pad = jnp.zeros((WINDOW, HEAD_DIM), F32)
    inv_rms = cols_ref[:, heads : heads + 1]
    per = heads // CHUNKS
    for h in range(heads):
        columns = span(h, HEAD_DIM)
        merged = merged_refs[h // per][:, span(h % per, HEAD_DIM)]
        normed_ref[:, columns] = (merged * inv_rms * gain_ref[0:1, columns]).astype(BF16)
        keys = jnp.concatenate([rim_ref[:WINDOW, columns], wkey_ref[:, columns]], axis=0)
        values = jnp.concatenate([rim_ref[WINDOW:, columns], value_ref[:, columns]], axis=0)
        grad = grad_ref[:, columns].astype(BF16)
        query = wquery_ref[:, columns]
        weights = weights_ref[h]
        narrow = weights.astype(BF16)
        dprob = jnp.concatenate([mm_nt(grad[s : s + WINDOW], values[s : s + 2 * WINDOW]) for s in starts], axis=0)
        dlogits = (weights * (dprob - lane_sum(weights * dprob))).astype(BF16)
        grads = [mm(dlogits[s : s + WINDOW], keys[s : s + 2 * WINDOW]) for s in starts]
        gwq_ref[:, columns] = (jnp.concatenate(grads, axis=0) * root).astype(BF16)
        key_parts = [mm_tn(dlogits[s : s + WINDOW], query[s : s + WINDOW]) for s in starts]
        value_parts = [mm_tn(narrow[s : s + WINDOW], grad[s : s + WINDOW]) for s in starts]
        back_ref[:WINDOW, columns] = (key_parts[0][:WINDOW] * root).astype(BF16)
        back_ref[WINDOW:, columns] = value_parts[0][:WINDOW].astype(BF16)
        key_sum = [a[WINDOW:] + b[:WINDOW] for a, b in zip(key_parts, key_parts[1:] + [pad])]
        value_sum = [a[WINDOW:] + b[:WINDOW] for a, b in zip(value_parts, value_parts[1:] + [pad])]
        gwk_ref[:, columns] = jnp.concatenate(key_sum, axis=0) * root
        gv_ref[:, columns] = jnp.concatenate(value_sum, axis=0)


def local_back_body(query_ref, key_ref, value_ref, sel_ref, sel_t_ref, rows_ref, grad_ref, ratios_ref, gv_in_ref, *refs):
    inverse_refs, prefix_refs, norm_refs = refs[:CHUNKS], refs[CHUNKS : 2 * CHUNKS], refs[2 * CHUNKS : 3 * CHUNKS]
    gq_ref, gk_ref, gv_ref, feat_ref = refs[3 * CHUNKS :]
    length = value_ref.shape[0]
    heads = value_ref.shape[1] // HEAD_DIM
    per = heads // CHUNKS
    sel = sel_ref[...]
    sel_t = sel_t_ref[...]
    causal = causal_mask(length)
    queries = [query_ref[span(h, FEAT), :] for h in range(heads)]
    keys = [key_ref[span(h, FEAT), :] for h in range(heads)]
    scaled = [grad_ref[:, span(h, HEAD_DIM)] * inverse_refs[h // per][:, h % per : h % per + 1] for h in range(heads)]
    parted = [halves(x) for x in scaled]
    cols = jnp.transpose(jnp.concatenate([ratios_ref[...], jnp.zeros((120, length), F32)], axis=0))
    scores = [mm_tn(query, key) * SCORE for query, key in zip(queries, keys)]
    probs = [mm_nt(narrow, value_ref[:, span(h, HEAD_DIM)]) for h, (narrow, _) in enumerate(parted)]
    kernels = [jnp.where(causal, 1.0 + score + 0.5 * score * score, 0.0).astype(BF16) for score in scores]
    values = [mm_tn(kernel, narrow) for kernel, (narrow, _) in zip(kernels, parted)]
    dscores = [
        jnp.where(causal, (probs[h] - cols[:, h : h + 1]) * (1.0 + scores[h]), 0.0).astype(BF16) for h in range(heads)
    ]
    by_query = [mm_nt(key, dscore) * SCORE for key, dscore in zip(keys, dscores)]
    by_key = [mm(query, dscore) * SCORE for query, dscore in zip(queries, dscores)]
    states = [halves(prefix_refs[h // per][span(h % per, ROWS), :]) for h in range(heads)]
    upstreams = [
        mm_nt(high, narrow) + (mm_nt(low, narrow) + mm_nt(high, rest))
        for (high, low), (narrow, rest) in zip(states, parted)
    ]
    drops = [
        outer([(norm_refs[h // per][h % per * 8 : h % per * 8 + 1, :], ratios_ref[h : h + 1, :])]) for h in range(heads)
    ]
    through = pull_back([up - drop for up, drop in zip(upstreams, drops)], queries, sel, sel_t)
    rows = rows_ref[...]
    features = [weighted_features(key, sel_t, rows) for key in keys]
    for h in range(heads):
        columns = span(h, HEAD_DIM)
        feat_ref[h] = features[h]
        gk_ref[span(h, FEAT), :] = by_key[h]
        gv_ref[:, columns] = gv_in_ref[:, columns] + values[h]
        gq_ref[span(h, FEAT), :] = (by_query[h] + through[h]).astype(BF16)


def final_body(bits, chunk, place_ref, *refs):
    steps = len(bits)
    parts = refs[:steps]
    key_ref, value_ref, sel_ref, sel_t_ref, feat_ref, gk_in_ref, gv_in_ref, back_ref = refs[steps : steps + 8]
    rest = refs[steps + 8 :]
    length = value_ref.shape[0]
    per = parts[0].shape[0] // ROWS
    cut = length - WINDOW
    sel = sel_ref[...]
    sel_t = sel_t_ref[...]
    ones = jnp.where(iota((8, length), 0) < 2, 1.0, 0.0).astype(BF16)
    if chunk + 1 < CHUNKS:
        gwk_in_ref, gk_ref, gv_ref, gwk_ref = rest
        gwk_ref[:cut, :] = gwk_in_ref[:cut, :].astype(BF16)
        gwk_ref[cut:, :] = (gwk_in_ref[cut:, :] + back_ref[:WINDOW, :].astype(F32)).astype(BF16)
    else:
        gwk_in, gq_in, gk_before, gv_before, gwk_out, gq_out, gk_out, gv_out, gk_ref, gv_ref, sems = rest
        own, other = chunk * per, (1 - chunk) * per
        early = [
            (gwk_in, gwk_out),
            (gv_before, gv_out.at[:, other * HEAD_DIM : (other + per) * HEAD_DIM]),
            (gk_before, gk_out.at[other * FEAT : (other + per) * FEAT, :]),
            (gq_in, gq_out),
        ]
        late = [
            (gv_ref, gv_out.at[:, own * HEAD_DIM : (own + per) * HEAD_DIM]),
            (gk_ref, gk_out.at[own * FEAT : (own + per) * FEAT, :]),
        ]
        copies = [pltpu.make_async_copy(a, b, sems.at[i]) for i, (a, b) in enumerate(early + late)]
        for copy in copies[: len(early)]:
            copy.start()
    wholes = [chunk * per + h for h in range(per)]
    states = []
    for h in range(per):
        state = None
        for bit, part in zip(bits, parts):
            block = part[span(h, ROWS), :].astype(F32) * taken(place_ref, bit, True)
            state = block if state is None else state + block
        states.append(state)
    parted = [halves(state) for state in states]
    values = [value_ref[:, span(whole, HEAD_DIM)] for whole in wholes]
    upstreams = [mm_nt(high, value) + mm_nt(low, value) for (high, low), value in zip(parted, values)]
    norms = [mm_tn(stack8(list(split(tile_norm(state[CONST:])))), ones) for state in states]
    reads = [mm(feat_ref[whole], high) + mm(feat_ref[whole], low) for whole, (high, low) in zip(wholes, parted)]
    keys = [key_ref[span(whole, FEAT), :] for whole in wholes]
    through = pull_back([up - norm for up, norm in zip(upstreams, norms)], keys, sel, sel_t)
    for h, whole in enumerate(wholes):
        columns = span(whole, HEAD_DIM)
        grad_value = gv_in_ref[:, columns] + reads[h]
        gv_ref[:cut, span(h, HEAD_DIM)] = grad_value[:cut].astype(BF16)
        gv_ref[cut:, span(h, HEAD_DIM)] = (grad_value[cut:] + back_ref[WINDOW:, columns].astype(F32)).astype(BF16)
    if chunk + 1 == CHUNKS:
        copies[-2].start()
    for h, whole in enumerate(wholes):
        gk_ref[span(h, FEAT), :] = (gk_in_ref[span(whole, FEAT), :] + through[h]).astype(BF16)
    if chunk + 1 == CHUNKS:
        copies[-1].start()
        for copy in copies:
            copy.wait()


def call(body, outs, *args, place=None, hbm=0, copies=0, results=(), ties=(), held=None):
    vmem = pl.BlockSpec(memory_space=pltpu.VMEM)
    specs = [pl.BlockSpec(memory_space=pltpu.HBM)] * hbm + [vmem] * (len(args) - hbm)
    args = tuple(
        pltpu.with_memory_space_constraint(a, pltpu.HBM if i < hbm else pltpu.VMEM) for i, a in enumerate(args)
    )
    if place is not None:
        specs = [pl.BlockSpec(memory_space=pltpu.SMEM)] + specs
        args = (place,) + args
    given = len(args)
    if ties:
        specs = specs + [pl.BlockSpec(memory_space=pl.ANY)] * len(ties)
        args = args + tuple(ties)
    return pl.pallas_call(
        body if not ties else lambda *refs: body(*refs[:given], *refs[given + len(ties) :]),
        out_shape=[
            pltpu.HBM(shape, dtype) if i in results else pltpu.VMEM(shape, dtype)
            for i, (shape, dtype) in enumerate(outs)
        ],
        in_specs=specs,
        out_specs=[
            pl.BlockSpec(memory_space=pltpu.HBM) if held and i in results else vmem for i in range(len(outs))
        ],
        scratch_shapes=[pltpu.VMEM(shape, dtype) for shape, dtype in held or ()]
        + ([pltpu.SemaphoreType.DMA((copies,))] if copies else []),
        compiler_params=pltpu.CompilerParams(vmem_limit_bytes=VMEM_LIMIT),
    )(*args)


def exchanged(states, add, gather, place, after_first):
    count = lax.axis_size("seq")
    bits = list(range(count.bit_length() - 1))
    orders = [bits if c % 2 == 0 else bits[::-1] for c in range(len(states))]
    held = list(states)
    parts = [[] for _ in states]
    extra, ties = None, {}
    for step in range(len(bits)):
        for c, order in enumerate(orders):
            pairs = [(i, i ^ (1 << order[step])) for i in range(count)]
            parts[c].append(lax.ppermute(held[c], "seq", pairs))
        if extra is None:
            extra, ties = after_first()
        if step + 1 == len(bits):
            break
        for c, order in enumerate(orders):
            tie = ties.get((step, c), ())
            shape = [(held[c].shape, BF16)]
            if c % 2:
                counts = order[:1] + [None] * step
                (held[c],) = call(
                    lambda *refs: gather(counts, order[step + 1], *refs), shape, *parts[c], states[c], place=place, ties=tie
                )
            else:
                (held[c],) = call(add, shape, held[c], parts[c][-1], ties=tie)
    takes = [order[:1] + [None] * (len(bits) - 1) if c % 2 else order for c, order in enumerate(orders)]
    return parts, takes, extra


def shards(query, key, value, window_query, window_key, gain, cotangent):
    length, width = value.shape
    heads = width // HEAD_DIM
    per = heads // CHUNKS
    count = lax.axis_size("seq")
    full_width = HEADS * HEAD_DIM
    place = lax.axis_index("seq").astype(jnp.int32).reshape(1)
    gain_row = gain.reshape(1, width)
    query_t, key_t = query.T, key.T
    state_shape = ((per * ROWS, HEAD_DIM), BF16)
    wide = ((length, width), F32)
    wide_narrow = ((length, width), BF16)
    tables = feature_tables()

    *states, rim, key_v, value_v, sel, sel_t, rows = call(
        state_body,
        [state_shape] * CHUNKS
        + [((2 * WINDOW, width), BF16), (key_t.shape, BF16), wide_narrow]
        + [(t.shape, t.dtype) for t in tables],
        key_t, value, window_key, *tables, hbm=6, copies=7,
    )

    def early():
        rim_in = lax.ppermute(rim, "seq", [(i, (i + 1) % count) for i in range(count)])
        local = call(
            local_body,
            [wide, ((length, 128), F32), ((heads, length, ROWS), BF16), ((heads * ROWS, length), BF16), (query_t.shape, BF16),
             wide_narrow, wide_narrow],
            query_t, window_query, window_key, key_v, value_v, sel, sel_t, rows, hbm=3, copies=3,
        )
        return (rim_in, local), {(0, 1): (local[1],), (1, 1): (rim_in,)}

    parts, takes, (rim_in, local) = exchanged(states, add_about_body, gather_about_body, place, early)
    numer, denom, featq, featq_t, query_v, wquery, wkey = local
    window_out, weights, cot, gain_v = call(
        window_body,
        [wide, ((heads, length, 2 * WINDOW), F32), wide_narrow, (gain_row.shape, F32)],
        cotangent, gain_row, wquery, wkey, value_v, rim_in, place=place, hbm=2, copies=2,
    )
    half = ((length, per * HEAD_DIM), F32)
    square = ((length, 128), F32)
    merged, linear, inverse, prefix, norm, before = [], [], [], [], [], []
    for c in range(CHUNKS):
        tail = [((8, length), F32)] if c + 1 == CHUNKS else [square, square]
        out = call(
            lambda *refs, c=c: merge_body(takes[c], c, *refs),
            [half, half, square, ((per * ROWS, HEAD_DIM), F32), ((per * 8, ROWS), F32)] + tail,
            *parts[c], featq, numer, denom, window_out, gain_v, cot, *before, place=place,
        )
        for held, item in zip((merged, linear, inverse, prefix, norm), out):
            held.append(item)
        before = out[5:]
    (stats,) = before
    ring = lax.axis_size("head")
    stats = [stats] + [lax.ppermute(stats, "head", [(i, (i + s) % ring) for i in range(ring)]) for s in range(1, ring)]
    *terms, grad, cols, ratios = call(
        lambda *refs: grad_body(float(full_width), ring, *refs),
        [state_shape] * CHUNKS + [wide, square, ((8, length), F32)],
        *stats, *merged, *linear, *inverse, gain_v, cot, featq_t,
    )

    def middle():
        grad_wquery, wkey_part, value_part, back, normed = call(
            window_back_body,
            [wide_narrow, wide, wide, ((2 * WINDOW, width), BF16), wide_narrow],
            wquery, wkey, value_v, rim_in, weights, grad, cols, gain_v, *merged, results=(0, 4),
        )
        back = lax.ppermute(back, "seq", [((i + 1) % count, i) for i in range(count)])
        return (grad_wquery, wkey_part, value_part, back, normed), {(0, 0): (wkey_part,)}

    parts, takes, (grad_wquery, wkey_part, value_part, back, normed) = exchanged(terms, add_body, gather_body, place, middle)
    grad_query, key_part, value_part, featk = call(
        local_back_body,
        [(query_t.shape, BF16), (key_t.shape, F32), wide, ((heads, length, ROWS), BF16)],
        query_v, key_v, value_v, sel, sel_t, rows, grad, ratios, value_part, *inverse, *prefix, *norm,
    )
    common = (key_v, value_v, sel, sel_t, featk, key_part, value_part, back)
    grad_key, grad_value, grad_wkey = call(
        lambda *refs: final_body(takes[0], 0, *refs),
        [((per * FEAT, length), BF16), ((length, per * HEAD_DIM), BF16), wide_narrow],
        *parts[0], *common, wkey_part, place=place,
    )
    grad_wkey, grad_query, grad_key, grad_value = call(
        lambda *refs: final_body(takes[1], 1, *refs),
        [wide_narrow, (query_t.shape, BF16), (key_t.shape, BF16), wide_narrow],
        *parts[1], *common, grad_wkey, grad_query, grad_key, grad_value, place=place, results=(0, 1, 2, 3), copies=6,
        held=[((per * FEAT, length), BF16), ((length, per * HEAD_DIM), BF16)],
    )
    return (normed, grad_query.T, grad_key.T, grad_value, grad_wquery, grad_wkey)


def solution(mesh):
    placed = P("seq", "head")
    return jax.shard_map(
        shards,
        mesh=mesh,
        in_specs=(placed, placed, placed, placed, placed, P("head"), placed),
        out_specs=(placed,) * 6,
        check_vma=False,
    )
```

```python
import math

import jax
import jax.numpy as jnp
import numpy as np
from jax import lax
from jax.experimental import pallas as pl
from jax.experimental.pallas import tpu as pltpu
from jax.sharding import PartitionSpec as P

HEADS = 16
HEAD_DIM = 128
FEAT = 16
WINDOW = 64
CHUNKS = 2

QUAD = FEAT * (FEAT + 1) // 2
LINEAR = QUAD
CONST = QUAD + FEAT
ROWS = 160
ROOT_HALF = float(np.float32(math.sqrt(0.5)))
SCORE = 1.0 / math.sqrt(FEAT)

F32 = jnp.float32
BF16 = jnp.bfloat16
VMEM_LIMIT = 24 * 1024 * 1024


def feature_tables():
    first = np.zeros((ROWS, FEAT), np.float32)
    second = np.zeros((ROWS, FEAT), np.float32)
    rows = np.zeros((8, ROWS), np.float32)
    scale = FEAT ** (-0.25)
    place = 0
    for distance in range(FEAT // 2 + 1):
        for i in range(FEAT if distance < FEAT // 2 else FEAT // 2):
            first[place, i] = scale
            second[place, (i + distance) % FEAT] = scale
            rows[2, place] = ROOT_HALF * (1.0 if distance == 0 else 2.0)
            place += 1
    for i in range(FEAT):
        first[LINEAR + i, i] = scale
    rows[1, LINEAR:CONST] = 1.0
    rows[0:2, CONST] = 1.0
    rows[2, LINEAR : CONST + 1] = 1.0
    sel = np.concatenate([first, second], axis=0)
    sel_t = np.concatenate([first.T, second.T], axis=0)
    return jnp.asarray(sel, BF16), jnp.asarray(sel_t, BF16), jnp.asarray(rows)


def mm(a, b):
    return lax.dot_general(a, b, (((1,), (0,)), ((), ())), preferred_element_type=F32)


def mm_nt(a, b):
    return lax.dot_general(a, b, (((1,), (1,)), ((), ())), preferred_element_type=F32)


def mm_tn(a, b):
    return lax.dot_general(a, b, (((0,), (0,)), ((), ())), preferred_element_type=F32)


def halves(x):
    high = x.astype(BF16)
    return high, (x - high.astype(F32)).astype(BF16)


def lane_sum(x):
    return jnp.sum(x, axis=1, keepdims=True)


def row_sum(x):
    ones = jnp.ones((8, x.shape[1]), BF16)
    high, low = halves(x)
    return mm_nt(ones, high) + mm_nt(ones, low)


def span(h, size):
    return slice(h * size, (h + 1) * size)


def iota(shape, axis):
    return lax.broadcasted_iota(jnp.int32, shape, axis)


def stack8(lines):
    count = -(-len(lines) // 8) * 8
    place = iota((count, lines[0].shape[1]), 0)
    out = jnp.zeros(place.shape, F32)
    for i, line in enumerate(lines):
        out = jnp.where(place == i, line, out)
    return out.astype(BF16)


def split(x):
    high = x.astype(BF16).astype(F32)
    return high, (x - high).astype(BF16).astype(F32)


def feature_rows(inputs_t, sel):
    a = mm(sel[:ROWS], inputs_t)
    b = mm(sel[ROWS : ROWS + QUAD], inputs_t)
    tail = (iota((ROWS - CONST, inputs_t.shape[1]), 0) == 0).astype(F32)
    return jnp.concatenate([a[:QUAD] * b * ROOT_HALF, a[LINEAR:CONST], tail], axis=0).astype(BF16)


def weighted_features(inputs_t, sel_t, rows):
    a = mm_tn(inputs_t, sel_t[:FEAT]) + rows[0:1]
    b = mm_tn(inputs_t, sel_t[FEAT:]) + rows[1:2]
    return (a * b * rows[2:3]).astype(BF16)


def pull_back(upstreams, inputs_t, sel, sel_t):
    firsts = [mm(sel[:QUAD], x) for x in inputs_t]
    seconds = [mm(sel[ROWS : ROWS + QUAD], x) for x in inputs_t]
    first_t = sel_t[:FEAT, :CONST]
    second_t = sel_t[FEAT:, :QUAD]
    sides = []
    for upstream, a, b in zip(upstreams, firsts, seconds):
        squares = upstream[:FEAT] * ROOT_HALF
        others = upstream[FEAT:QUAD] * (2.0 * ROOT_HALF)
        on_first = jnp.concatenate([squares * b[:FEAT], others * b[FEAT:], upstream[LINEAR:CONST]], axis=0)
        on_second = jnp.concatenate([squares * a[:FEAT], others * a[FEAT:]], axis=0)
        sides.append(halves(on_first) + halves(on_second))
    return [
        (mm(first_t, p_high) + mm(second_t, q_high)) + (mm(first_t, p_low) + mm(second_t, q_low))
        for p_high, p_low, q_high, q_low in sides
    ]


def norm_tile(norm):
    high, low = split(norm)
    pad = jnp.zeros((1, 256 - ROWS), F32)
    row = iota((8, 128), 0)
    out = jnp.where(row == 1, high[:, :128], 0.0)
    out = jnp.where(row == 2, jnp.concatenate([high[:, 128:], pad], axis=1), out)
    out = jnp.where(row == 3, low[:, :128], out)
    return jnp.where(row == 4, jnp.concatenate([low[:, 128:], pad], axis=1), out)


def tile_norm(tile):
    return jnp.concatenate([tile[1:2] + tile[3:4], (tile[2:3] + tile[4:5])[:, : ROWS - 128]], axis=1)


def outer(pairs):
    left, right = [], []
    for a, b in pairs:
        a_high, a_low = split(a)
        b_high, b_low = split(b)
        left += [a_high, a_low, a_high]
        right += [b_high, b_high, b_low]
    return mm_tn(stack8(left), stack8(right))


def store_state(out_ref, head, state, tile):
    row = iota((8, 128), 0)
    last = jnp.where(row == 0, state[CONST:], tile)
    out_ref[span(head, ROWS), :] = jnp.concatenate([state[:CONST], last], axis=0).astype(BF16)


def causal_mask(length):
    return iota((length, length), 0) >= iota((length, length), 1)


def state_body(key_hbm, value_hbm, wkey_hbm, sel_hbm, sel_t_hbm, rows_hbm, *refs):
    states = refs[:CHUNKS]
    rim_ref, key_ref, value_ref, sel_ref, sel_t_ref, rows_ref, sems = refs[CHUNKS:]
    length, width = value_ref.shape
    heads = width // HEAD_DIM
    cut = length - WINDOW
    pairs = [
        (key_hbm, key_ref),
        (sel_hbm, sel_ref),
        (value_hbm, value_ref),
        (wkey_hbm.at[cut:length, :], rim_ref.at[0:WINDOW, :]),
        (value_hbm.at[cut:length, :], rim_ref.at[WINDOW : 2 * WINDOW, :]),
        (sel_t_hbm, sel_t_ref),
        (rows_hbm, rows_ref),
    ]
    copies = [pltpu.make_async_copy(a, b, sems.at[i]) for i, (a, b) in enumerate(pairs)]
    for copy in copies:
        copy.start()
    copies[0].wait()
    copies[1].wait()
    sel = sel_ref[...]
    ones = jnp.ones((8, length), BF16)
    place = iota((8, 128), 0)
    feats = [feature_rows(key_ref[span(h, FEAT), :], sel) for h in range(heads)]
    norms = [mm_nt(ones, feat)[0:1] for feat in feats]
    copies[2].wait()
    values = [value_ref[:, span(h, HEAD_DIM)] for h in range(heads)]
    middles = [(jnp.sum(value.astype(F32), axis=0, keepdims=True) * (1.0 / length)).astype(BF16) for value in values]
    sums = [mm(feat, value) for feat, value in zip(feats, values)]
    moved = [mm(feat, jnp.broadcast_to(middle, value.shape)) for feat, middle, value in zip(feats, middles, values)]
    tiles = [jnp.where(place == 5, middle.astype(F32), norm_tile(norm)) for norm, middle in zip(norms, middles)]
    per = heads // CHUNKS
    for h in range(heads):
        store_state(states[h // per], h % per, sums[h] - moved[h], tiles[h])
    for copy in copies[3:]:
        copy.wait()


def add_about_body(mine_ref, theirs_ref, out_ref):
    place = iota((8, 128), 0)
    totals, tiles, moves = [], [], []
    for h in range(mine_ref.shape[0] // ROWS):
        mine = mine_ref[span(h, ROWS), :].astype(F32)
        theirs = theirs_ref[span(h, ROWS), :].astype(F32)
        mine_tile, their_tile = mine[CONST:], theirs[CONST:]
        mine_norm, their_norm = tile_norm(mine_tile), tile_norm(their_tile)
        mine_middle, their_middle = mine_tile[5:6], their_tile[5:6]
        middle = (0.5 * (mine_middle + their_middle)).astype(BF16).astype(F32)
        moves.append(outer([(mine_norm, mine_middle - middle), (their_norm, their_middle - middle)]))
        tiles.append(jnp.where(place == 5, middle, norm_tile(mine_norm + their_norm)))
        totals.append(mine + theirs)
    for h, total in enumerate(totals):
        store_state(out_ref, h, total + moves[h], tiles[h])


def add_body(mine_ref, theirs_ref, out_ref):
    for h in range(mine_ref.shape[0] // ROWS):
        total = mine_ref[span(h, ROWS), :].astype(F32) + theirs_ref[span(h, ROWS), :].astype(F32)
        store_state(out_ref, h, total, norm_tile(tile_norm(total[CONST:])))


def gather_about_body(bits, ahead, place_ref, *refs):
    parts, mine_ref, out_ref = refs[: len(bits)], refs[-2], refs[-1]
    place = iota((8, 128), 0)
    weights = [taken(place_ref, bit, False) for bit in bits] + [taken(place_ref, ahead, True)]
    totals, tiles, moves = [], [], []
    for h in range(mine_ref.shape[0] // ROWS):
        blocks = [ref[span(h, ROWS), :].astype(F32) for ref in parts + (mine_ref,)]
        middles = [block[CONST + 5 : CONST + 6] for block in blocks]
        norms = [tile_norm(block[CONST:]) * weight for block, weight in zip(blocks, weights)]
        norm = sum(norms)
        sizes = [n[:, CONST : CONST + 1] for n in norms]
        middle = sum(size * m for size, m in zip(sizes, middles)) * (1.0 / jnp.maximum(sum(sizes), 1.0))
        middle = middle.astype(BF16).astype(F32)
        moves.append(outer([(n, m - middle) for n, m in zip(norms, middles)]))
        tiles.append(jnp.where(place == 5, middle, norm_tile(norm)))
        totals.append(sum(block * weight for block, weight in zip(blocks, weights)))
    for h, total in enumerate(totals):
        store_state(out_ref, h, total + moves[h], tiles[h])


def gather_body(bits, ahead, place_ref, *refs):
    parts, mine_ref, out_ref = refs[: len(bits)], refs[-2], refs[-1]
    weights = [taken(place_ref, bit, True) for bit in bits] + [taken(place_ref, ahead, False)]
    for h in range(mine_ref.shape[0] // ROWS):
        total = sum(ref[span(h, ROWS), :].astype(F32) * weight for ref, weight in zip(parts + (mine_ref,), weights))
        store_state(out_ref, h, total, norm_tile(tile_norm(total[CONST:])))


def local_body(query_hbm, wquery_hbm, wkey_hbm, key_ref, value_ref, sel_ref, sel_t_ref, rows_ref,
               numer_ref, denom_ref, featq_ref, featq_t_ref, query_ref, wquery_ref, wkey_ref, sems):
    pairs = [(query_hbm, query_ref), (wquery_hbm, wquery_ref), (wkey_hbm, wkey_ref)]
    copies = [pltpu.make_async_copy(a, b, sems.at[i]) for i, (a, b) in enumerate(pairs)]
    for copy in copies:
        copy.start()
    length = value_ref.shape[0]
    heads = value_ref.shape[1] // HEAD_DIM
    sel = sel_ref[...]
    sel_t = sel_t_ref[...]
    rows = rows_ref[...]
    keys = [key_ref[span(h, FEAT), :] for h in range(heads)]
    copies[0].wait()
    causal = causal_mask(length)
    lane = iota((length, 128), 1)
    queries = [query_ref[span(h, FEAT), :] for h in range(heads)]
    scores = [mm_tn(query, key) * SCORE for query, key in zip(queries, keys)]
    columns = [feature_rows(query, sel) for query in queries]
    features = [weighted_features(query, sel_t, rows) for query in queries]
    kernels = [jnp.where(causal, 1.0 + score + 0.5 * score * score, 0.0) for score in scores]
    numers = [mm(kernel.astype(BF16), value_ref[:, span(h, HEAD_DIM)]) for h, kernel in enumerate(kernels)]
    denoms = jnp.zeros((length, 128), F32)
    for h in range(heads):
        denoms = jnp.where(lane == h, lane_sum(kernels[h]), denoms)
    for h in range(heads):
        featq_t_ref[span(h, ROWS), :] = columns[h]
        featq_ref[h] = features[h]
        numer_ref[:, span(h, HEAD_DIM)] = numers[h]
    denom_ref[...] = denoms
    copies[1].wait()
    copies[2].wait()


def window_body(place_ref, cot_hbm, gain_hbm, wquery_ref, wkey_ref, value_ref, rim_ref,
                out_ref, weights_ref, cot_ref, gain_ref, sems):
    pairs = [(cot_hbm, cot_ref), (gain_hbm, gain_ref)]
    copies = [pltpu.make_async_copy(a, b, sems.at[i]) for i, (a, b) in enumerate(pairs)]
    for copy in copies:
        copy.start()
    length = wquery_ref.shape[0]
    heads = value_ref.shape[1] // HEAD_DIM
    live = place_ref[0] > 0
    row = iota((WINDOW, 2 * WINDOW), 0)
    col = iota((WINDOW, 2 * WINDOW), 1)
    inside = (col > row) & (col <= row + WINDOW)
    edge = inside & ((col >= WINDOW) | live)
    starts = range(0, length, WINDOW)
    allowed = jnp.concatenate([edge] + [inside] * (len(starts) - 1), axis=0)
    for h in range(heads):
        columns = span(h, HEAD_DIM)
        keys = jnp.concatenate([rim_ref[:WINDOW, columns], wkey_ref[:, columns]], axis=0)
        values = jnp.concatenate([rim_ref[WINDOW:, columns], value_ref[:, columns]], axis=0)
        query = wquery_ref[:, columns]
        logits = jnp.concatenate([mm_nt(query[s : s + WINDOW], keys[s : s + 2 * WINDOW]) for s in starts], axis=0)
        masked = jnp.where(allowed, logits * (1.0 / math.sqrt(HEAD_DIM)), -1e30)
        exponent = jnp.where(allowed, jnp.exp(masked - jnp.max(masked, axis=1, keepdims=True)), 0.0)
        weights = exponent * (1.0 / lane_sum(exponent))
        weights_ref[h] = weights
        narrow = weights.astype(BF16)
        out_ref[:, columns] = jnp.concatenate([mm(narrow[s : s + WINDOW], values[s : s + 2 * WINDOW]) for s in starts], axis=0)
    copies[0].wait()
    copies[1].wait()


def taken(place_ref, bit, later):
    if bit is None:
        return 1.0
    side = (place_ref[0] >> bit) & 1
    return (1 - side if later else side).astype(F32)


def merge_body(bits, chunk, place_ref, *refs):
    steps = len(bits)
    parts = refs[:steps]
    feat_ref, numer_ref, denom_ref, window_ref, gain_ref, cot_ref = refs[steps : steps + 6]
    before = refs[steps + 6 : steps + 6 + (2 if chunk else 0)]
    outs = refs[steps + 6 + len(before) :]
    merged_ref, linear_ref, inverse_ref, prefix_ref, norm_ref = outs[:5]
    length = numer_ref.shape[0]
    per = merged_ref.shape[1] // HEAD_DIM
    lane = iota((length, 128), 1)
    inverses = jnp.zeros((length, 128), F32)
    squares = before[0][...] if chunk else jnp.zeros((length, HEAD_DIM), F32)
    crosses = before[1][...] if chunk else jnp.zeros((length, HEAD_DIM), F32)
    states, norms, lefts, rights = [], [], [], []
    for h in range(per):
        state = norm = None
        left, right = [], []
        for bit, part in zip(bits, parts):
            block = part[span(h, ROWS), :].astype(F32)
            middle = block[CONST + 5 : CONST + 6]
            block = block * taken(place_ref, bit, False)
            block_norm = tile_norm(block[CONST:])
            left += list(split(block_norm))
            right += [middle, middle]
            state = block if state is None else state + block
            norm = block_norm if norm is None else norm + block_norm
        states.append(state)
        norms.append(norm)
        lefts.append(stack8(left))
        rights.append(stack8(right))
    moved = [mm_tn(left, right) for left, right in zip(lefts, rights)]
    states = [state + move for state, move in zip(states, moved)]
    parted = [halves(state) for state in states]
    wholes = [chunk * per + h for h in range(per)]
    feats = [feat_ref[whole] for whole in wholes]
    extras = [mm_nt(feat, stack8(list(split(norm)))) for feat, norm in zip(feats, norms)]
    reads = [mm(feat, high) + mm(feat, low) for feat, (high, low) in zip(feats, parted)]
    linears, mergeds = [], []
    for h, whole in enumerate(wholes):
        columns = span(whole, HEAD_DIM)
        inverse = 1.0 / (denom_ref[:, whole : whole + 1] + (extras[h][:, 0:1] + extras[h][:, 1:2]))
        inverses = jnp.where(lane == h, inverse, inverses)
        linear = (numer_ref[:, columns] + reads[h]) * inverse
        merged = linear + window_ref[:, columns]
        squares = squares + merged * merged
        scaled_cot = cot_ref[:, columns].astype(F32) * gain_ref[0:1, columns]
        crosses = crosses + scaled_cot * merged
        linears.append(linear)
        mergeds.append(merged)
    for h in range(per):
        linear_ref[:, span(h, HEAD_DIM)] = linears[h]
        merged_ref[:, span(h, HEAD_DIM)] = mergeds[h]
        prefix_ref[span(h, ROWS), :] = states[h]
        norm_ref[span(h, 8), :] = jnp.broadcast_to(norms[h], (8, ROWS))
    inverse_ref[...] = inverses
    if chunk + 1 < CHUNKS:
        outs[5][...] = squares
        outs[6][...] = crosses
    else:
        place = iota((8, length), 0)
        outs[5][...] = jnp.where(place == 0, row_sum(squares), jnp.where(place == 1, row_sum(crosses), 0.0))


def grad_body(width, sources, *refs):
    stats_refs, refs = refs[:sources], refs[sources:]
    merged_refs, linear_refs, inverse_refs = refs[:CHUNKS], refs[CHUNKS : 2 * CHUNKS], refs[2 * CHUNKS : 3 * CHUNKS]
    gain_ref, cot_ref, feat_t_ref = refs[3 * CHUNKS : 3 * CHUNKS + 3]
    terms = refs[3 * CHUNKS + 3 : 4 * CHUNKS + 3]
    grad_ref, cols_ref, ratios_ref = refs[4 * CHUNKS + 3 :]
    length = grad_ref.shape[0]
    heads = grad_ref.shape[1] // HEAD_DIM
    per = heads // CHUNKS
    stats = stats_refs[0][...]
    for ref in stats_refs[1:]:
        stats = stats + ref[...]
    sums = jnp.transpose(jnp.concatenate([stats, jnp.zeros((120, length), F32)], axis=0))
    mean = sums[:, 0:1] / width + 1e-6
    inv_rms = 1.0 / jnp.sqrt(mean)
    pull = sums[:, 1:2] / (width * mean)
    lane = iota((length, 128), 1)
    cols_ref[...] = jnp.where(lane == heads, inv_rms, 0.0)
    grads, narrows, ratios = [], [], []
    for h in range(heads):
        chunk, local = h // per, span(h % per, HEAD_DIM)
        inverse = inverse_refs[chunk][:, h % per : h % per + 1]
        scaled_cot = cot_ref[:, span(h, HEAD_DIM)].astype(F32) * gain_ref[0:1, span(h, HEAD_DIM)]
        grad = (scaled_cot - merged_refs[chunk][:, local] * pull) * inv_rms
        grads.append(grad)
        narrows.append((grad * inverse).astype(BF16))
        ratios.append(row_sum(grad * linear_refs[chunk][:, local] * inverse)[0:1])
    feats = [feat_t_ref[span(h, ROWS), :] for h in range(heads)]
    sums = [mm(feat, narrow) for feat, narrow in zip(feats, narrows)]
    norms = [mm_nt(stack8(list(split(ratio))), feat) for ratio, feat in zip(ratios, feats)]
    for h in range(heads):
        store_state(terms[h // per], h % per, sums[h], norm_tile(norms[h][0:1] + norms[h][1:2]))
        grad_ref[:, span(h, HEAD_DIM)] = grads[h]
    ratios_ref[...] = jnp.zeros(ratios_ref.shape, F32)
    for h in range(heads):
        ratios_ref[h : h + 1, :] = ratios[h]


def window_back_body(wquery_ref, wkey_ref, value_ref, rim_ref, weights_ref, grad_ref, cols_ref, gain_ref, *refs):
    merged_refs, (gwq_ref, gwk_ref, gv_ref, back_ref, normed_ref) = refs[:CHUNKS], refs[CHUNKS:]
    length = wquery_ref.shape[0]
    heads = value_ref.shape[1] // HEAD_DIM
    root = 1.0 / math.sqrt(HEAD_DIM)
    starts = range(0, length, WINDOW)
    pad = jnp.zeros((WINDOW, HEAD_DIM), F32)
    inv_rms = cols_ref[:, heads : heads + 1]
    per = heads // CHUNKS
    groups = [slice(s, s + WINDOW) for s in starts]
    bands = [slice(s, s + 2 * WINDOW) for s in starts]
    spans = [span(h, HEAD_DIM) for h in range(heads)]
    keys = [jnp.concatenate([rim_ref[:WINDOW, c], wkey_ref[:, c]], axis=0) for c in spans]
    values = [jnp.concatenate([rim_ref[WINDOW:, c], value_ref[:, c]], axis=0) for c in spans]
    grads = [grad_ref[:, c].astype(BF16) for c in spans]
    queries = [wquery_ref[:, c] for c in spans]
    dprobs = [
        jnp.concatenate([mm_nt(grad[g], value[band]) for g, band in zip(groups, bands)], axis=0)
        for grad, value in zip(grads, values)
    ]
    dlogits = []
    for h, dprob in enumerate(dprobs):
        weights = weights_ref[h]
        dlogits.append((weights * (dprob - lane_sum(weights * dprob))).astype(BF16))
    for h, c in enumerate(spans):
        dlogit, narrow = dlogits[h], weights_ref[h].astype(BF16)
        key_parts = [mm_tn(dlogit[g], queries[h][g]) for g in groups]
        value_parts = [mm_tn(narrow[g], grads[h][g]) for g in groups]
        parts = [mm(dlogit[g], keys[h][band]) for g, band in zip(groups, bands)]
        back_ref[:WINDOW, c] = (key_parts[0][:WINDOW] * root).astype(BF16)
        back_ref[WINDOW:, c] = value_parts[0][:WINDOW].astype(BF16)
        key_sum = [p[WINDOW:] + q[:WINDOW] for p, q in zip(key_parts, key_parts[1:] + [pad])]
        value_sum = [p[WINDOW:] + q[:WINDOW] for p, q in zip(value_parts, value_parts[1:] + [pad])]
        gwq_ref[:, c] = (jnp.concatenate(parts, axis=0) * root).astype(BF16)
        gwk_ref[:, c] = jnp.concatenate(key_sum, axis=0) * root
        gv_ref[:, c] = jnp.concatenate(value_sum, axis=0)
        merged = merged_refs[h // per][:, span(h % per, HEAD_DIM)]
        normed_ref[:, c] = (merged * inv_rms * gain_ref[0:1, c]).astype(BF16)


def local_back_body(query_ref, key_ref, value_ref, sel_ref, sel_t_ref, rows_ref, grad_ref, ratios_ref, gv_in_ref, *refs):
    inverse_refs, prefix_refs, norm_refs = refs[:CHUNKS], refs[CHUNKS : 2 * CHUNKS], refs[2 * CHUNKS : 3 * CHUNKS]
    gq_ref, gk_ref, gv_ref, feat_ref = refs[3 * CHUNKS :]
    length = value_ref.shape[0]
    heads = value_ref.shape[1] // HEAD_DIM
    per = heads // CHUNKS
    sel = sel_ref[...]
    sel_t = sel_t_ref[...]
    causal = causal_mask(length)
    queries = [query_ref[span(h, FEAT), :] for h in range(heads)]
    keys = [key_ref[span(h, FEAT), :] for h in range(heads)]
    scaled = [grad_ref[:, span(h, HEAD_DIM)] * inverse_refs[h // per][:, h % per : h % per + 1] for h in range(heads)]
    parted = [halves(x) for x in scaled]
    cols = jnp.transpose(jnp.concatenate([ratios_ref[...], jnp.zeros((120, length), F32)], axis=0))
    scores = [mm_tn(query, key) * SCORE for query, key in zip(queries, keys)]
    probs = [mm_nt(narrow, value_ref[:, span(h, HEAD_DIM)]) for h, (narrow, _) in enumerate(parted)]
    kernels = [jnp.where(causal, 1.0 + score + 0.5 * score * score, 0.0).astype(BF16) for score in scores]
    values = [mm_tn(kernel, narrow) for kernel, (narrow, _) in zip(kernels, parted)]
    dscores = [
        jnp.where(causal, (probs[h] - cols[:, h : h + 1]) * (1.0 + scores[h]), 0.0).astype(BF16) for h in range(heads)
    ]
    by_query = [mm_nt(key, dscore) * SCORE for key, dscore in zip(keys, dscores)]
    by_key = [mm(query, dscore) * SCORE for query, dscore in zip(queries, dscores)]
    states = [halves(prefix_refs[h // per][span(h % per, ROWS), :]) for h in range(heads)]
    upstreams = [
        mm_nt(high, narrow) + (mm_nt(low, narrow) + mm_nt(high, rest))
        for (high, low), (narrow, rest) in zip(states, parted)
    ]
    drops = [
        outer([(norm_refs[h // per][h % per * 8 : h % per * 8 + 1, :], ratios_ref[h : h + 1, :])]) for h in range(heads)
    ]
    through = pull_back([up - drop for up, drop in zip(upstreams, drops)], queries, sel, sel_t)
    rows = rows_ref[...]
    features = [weighted_features(key, sel_t, rows) for key in keys]
    for h in range(heads):
        columns = span(h, HEAD_DIM)
        feat_ref[h] = features[h]
        gk_ref[span(h, FEAT), :] = by_key[h]
        gv_ref[:, columns] = gv_in_ref[:, columns] + values[h]
        gq_ref[span(h, FEAT), :] = (by_query[h] + through[h]).astype(BF16)


def final_body(bits, chunk, place_ref, *refs):
    steps = len(bits)
    parts = refs[:steps]
    key_ref, value_ref, sel_ref, sel_t_ref, feat_ref, gk_in_ref, gv_in_ref, back_ref = refs[steps : steps + 8]
    rest = refs[steps + 8 :]
    length = value_ref.shape[0]
    per = parts[0].shape[0] // ROWS
    cut = length - WINDOW
    sel = sel_ref[...]
    sel_t = sel_t_ref[...]
    ones = jnp.where(iota((8, length), 0) < 2, 1.0, 0.0).astype(BF16)
    if chunk + 1 < CHUNKS:
        gwk_in_ref, gk_ref, gv_ref, gwk_ref = rest
        gwk_ref[:cut, :] = gwk_in_ref[:cut, :].astype(BF16)
        gwk_ref[cut:, :] = (gwk_in_ref[cut:, :] + back_ref[:WINDOW, :].astype(F32)).astype(BF16)
    else:
        gwk_in, gq_in, gk_before, gv_before, gwk_out, gq_out, gk_out, gv_out, gk_ref, gv_ref, sems = rest
        own, other = chunk * per, (1 - chunk) * per
        early = [
            (gwk_in, gwk_out),
            (gv_before, gv_out.at[:, other * HEAD_DIM : (other + per) * HEAD_DIM]),
            (gk_before, gk_out.at[other * FEAT : (other + per) * FEAT, :]),
            (gq_in, gq_out),
        ]
        late = [
            (gv_ref, gv_out.at[:, own * HEAD_DIM : (own + per) * HEAD_DIM]),
            (gk_ref, gk_out.at[own * FEAT : (own + per) * FEAT, :]),
        ]
        copies = [pltpu.make_async_copy(a, b, sems.at[i]) for i, (a, b) in enumerate(early + late)]
        for copy in copies[: len(early)]:
            copy.start()
    wholes = [chunk * per + h for h in range(per)]
    states = []
    for h in range(per):
        state = None
        for bit, part in zip(bits, parts):
            block = part[span(h, ROWS), :].astype(F32) * taken(place_ref, bit, True)
            state = block if state is None else state + block
        states.append(state)
    parted = [halves(state) for state in states]
    values = [value_ref[:, span(whole, HEAD_DIM)] for whole in wholes]
    upstreams = [mm_nt(high, value) + mm_nt(low, value) for (high, low), value in zip(parted, values)]
    norms = [mm_tn(stack8(list(split(tile_norm(state[CONST:])))), ones) for state in states]
    reads = [mm(feat_ref[whole], high) + mm(feat_ref[whole], low) for whole, (high, low) in zip(wholes, parted)]
    keys = [key_ref[span(whole, FEAT), :] for whole in wholes]
    through = pull_back([up - norm for up, norm in zip(upstreams, norms)], keys, sel, sel_t)
    for h, whole in enumerate(wholes):
        columns = span(whole, HEAD_DIM)
        grad_value = gv_in_ref[:, columns] + reads[h]
        gv_ref[:cut, span(h, HEAD_DIM)] = grad_value[:cut].astype(BF16)
        gv_ref[cut:, span(h, HEAD_DIM)] = (grad_value[cut:] + back_ref[WINDOW:, columns].astype(F32)).astype(BF16)
    if chunk + 1 == CHUNKS:
        copies[-2].start()
    for h, whole in enumerate(wholes):
        gk_ref[span(h, FEAT), :] = (gk_in_ref[span(whole, FEAT), :] + through[h]).astype(BF16)
    if chunk + 1 == CHUNKS:
        copies[-1].start()
        for copy in copies:
            copy.wait()


def call(body, outs, *args, place=None, hbm=0, copies=0, results=(), ties=(), held=None):
    vmem = pl.BlockSpec(memory_space=pltpu.VMEM)
    specs = [pl.BlockSpec(memory_space=pltpu.HBM)] * hbm + [vmem] * (len(args) - hbm)
    args = tuple(
        pltpu.with_memory_space_constraint(a, pltpu.HBM if i < hbm else pltpu.VMEM) for i, a in enumerate(args)
    )
    if place is not None:
        specs = [pl.BlockSpec(memory_space=pltpu.SMEM)] + specs
        args = (place,) + args
    given = len(args)
    if ties:
        specs = specs + [pl.BlockSpec(memory_space=pl.ANY)] * len(ties)
        args = args + tuple(ties)
    return pl.pallas_call(
        body if not ties else lambda *refs: body(*refs[:given], *refs[given + len(ties) :]),
        out_shape=[
            pltpu.HBM(shape, dtype) if i in results else pltpu.VMEM(shape, dtype)
            for i, (shape, dtype) in enumerate(outs)
        ],
        in_specs=specs,
        out_specs=[
            pl.BlockSpec(memory_space=pltpu.HBM) if held and i in results else vmem for i in range(len(outs))
        ],
        scratch_shapes=[pltpu.VMEM(shape, dtype) for shape, dtype in held or ()]
        + ([pltpu.SemaphoreType.DMA((copies,))] if copies else []),
        compiler_params=pltpu.CompilerParams(vmem_limit_bytes=VMEM_LIMIT),
    )(*args)


def exchanged(states, add, gather, place, after_first):
    count = lax.axis_size("seq")
    bits = list(range(count.bit_length() - 1))
    orders = [bits if c % 2 == 0 else bits[::-1] for c in range(len(states))]
    held = list(states)
    parts = [[] for _ in states]
    extra, ties = None, {}
    for step in range(len(bits)):
        for c, order in enumerate(orders):
            pairs = [(i, i ^ (1 << order[step])) for i in range(count)]
            parts[c].append(lax.ppermute(held[c], "seq", pairs))
        if extra is None:
            extra, ties = after_first()
        if step + 1 == len(bits):
            break
        for c, order in enumerate(orders):
            tie = ties.get((step, c), ())
            shape = [(held[c].shape, BF16)]
            if c % 2:
                counts = order[:1] + [None] * step
                (held[c],) = call(
                    lambda *refs: gather(counts, order[step + 1], *refs), shape, *parts[c], states[c], place=place, ties=tie
                )
            else:
                (held[c],) = call(add, shape, held[c], parts[c][-1], ties=tie)
    takes = [order[:1] + [None] * (len(bits) - 1) if c % 2 else order for c, order in enumerate(orders)]
    return parts, takes, extra


def shards(query, key, value, window_query, window_key, gain, cotangent):
    length, width = value.shape
    heads = width // HEAD_DIM
    per = heads // CHUNKS
    count = lax.axis_size("seq")
    full_width = HEADS * HEAD_DIM
    place = lax.axis_index("seq").astype(jnp.int32).reshape(1)
    gain_row = gain.reshape(1, width)
    query_t, key_t = query.T, key.T
    state_shape = ((per * ROWS, HEAD_DIM), BF16)
    wide = ((length, width), F32)
    wide_narrow = ((length, width), BF16)
    tables = feature_tables()

    *states, rim, key_v, value_v, sel, sel_t, rows = call(
        state_body,
        [state_shape] * CHUNKS
        + [((2 * WINDOW, width), BF16), (key_t.shape, BF16), wide_narrow]
        + [(t.shape, t.dtype) for t in tables],
        key_t, value, window_key, *tables, hbm=6, copies=7,
    )

    def early():
        rim_in = lax.ppermute(rim, "seq", [(i, (i + 1) % count) for i in range(count)])
        local = call(
            local_body,
            [wide, ((length, 128), F32), ((heads, length, ROWS), BF16), ((heads * ROWS, length), BF16), (query_t.shape, BF16),
             wide_narrow, wide_narrow],
            query_t, window_query, window_key, key_v, value_v, sel, sel_t, rows, hbm=3, copies=3,
        )
        return (rim_in, local), {(0, 1): (local[1],), (1, 1): (rim_in,)}

    parts, takes, (rim_in, local) = exchanged(states, add_about_body, gather_about_body, place, early)
    numer, denom, featq, featq_t, query_v, wquery, wkey = local
    window_out, weights, cot, gain_v = call(
        window_body,
        [wide, ((heads, length, 2 * WINDOW), F32), wide_narrow, (gain_row.shape, F32)],
        cotangent, gain_row, wquery, wkey, value_v, rim_in, place=place, hbm=2, copies=2,
    )
    half = ((length, per * HEAD_DIM), F32)
    square = ((length, 128), F32)
    merged, linear, inverse, prefix, norm, before = [], [], [], [], [], []
    for c in range(CHUNKS):
        tail = [((8, length), F32)] if c + 1 == CHUNKS else [square, square]
        out = call(
            lambda *refs, c=c: merge_body(takes[c], c, *refs),
            [half, half, square, ((per * ROWS, HEAD_DIM), F32), ((per * 8, ROWS), F32)] + tail,
            *parts[c], featq, numer, denom, window_out, gain_v, cot, *before, place=place,
        )
        for held, item in zip((merged, linear, inverse, prefix, norm), out):
            held.append(item)
        before = out[5:]
    (stats,) = before
    ring = lax.axis_size("head")
    stats = [stats] + [lax.ppermute(stats, "head", [(i, (i + s) % ring) for i in range(ring)]) for s in range(1, ring)]
    *terms, grad, cols, ratios = call(
        lambda *refs: grad_body(float(full_width), ring, *refs),
        [state_shape] * CHUNKS + [wide, square, ((8, length), F32)],
        *stats, *merged, *linear, *inverse, gain_v, cot, featq_t,
    )

    def middle():
        grad_wquery, wkey_part, value_part, back, normed = call(
            window_back_body,
            [wide_narrow, wide, wide, ((2 * WINDOW, width), BF16), wide_narrow],
            wquery, wkey, value_v, rim_in, weights, grad, cols, gain_v, *merged, results=(0, 4),
        )
        back = lax.ppermute(back, "seq", [((i + 1) % count, i) for i in range(count)])
        return (grad_wquery, wkey_part, value_part, back, normed), {(0, 0): (wkey_part,)}

    parts, takes, (grad_wquery, wkey_part, value_part, back, normed) = exchanged(terms, add_body, gather_body, place, middle)
    grad_query, key_part, value_part, featk = call(
        local_back_body,
        [(query_t.shape, BF16), (key_t.shape, F32), wide, ((heads, length, ROWS), BF16)],
        query_v, key_v, value_v, sel, sel_t, rows, grad, ratios, value_part, *inverse, *prefix, *norm,
    )
    common = (key_v, value_v, sel, sel_t, featk, key_part, value_part, back)
    grad_key, grad_value, grad_wkey = call(
        lambda *refs: final_body(takes[0], 0, *refs),
        [((per * FEAT, length), BF16), ((length, per * HEAD_DIM), BF16), wide_narrow],
        *parts[0], *common, wkey_part, place=place,
    )
    grad_wkey, grad_query, grad_key, grad_value = call(
        lambda *refs: final_body(takes[1], 1, *refs),
        [wide_narrow, (query_t.shape, BF16), (key_t.shape, BF16), wide_narrow],
        *parts[1], *common, grad_wkey, grad_query, grad_key, grad_value, place=place, results=(0, 1, 2, 3), copies=6,
        held=[((per * FEAT, length), BF16), ((length, per * HEAD_DIM), BF16)],
    )
    return (normed, grad_query.T, grad_key.T, grad_value, grad_wquery, grad_wkey)


def solution(mesh):
    placed = P("seq", "head")
    return jax.shard_map(
        shards,
        mesh=mesh,
        in_specs=(placed, placed, placed, placed, placed, P("head"), placed),
        out_specs=(placed,) * 6,
        check_vma=False,
    )
```
